32 devices in a mesh: segment: 4 (over y, core), slab: 8 (over z, x).
Axes of the slice: x: 2, y: 2, z: 4, core: 2. Of those that a mesh axis runs over, the one named last changes fastest.
Arguments:
- video_in: bfloat16 [8, 16, 64, 384], P(None, 'slab'), may hold values from -6 to 6
- cache_in: bfloat16 [4, 2, 16, 64, 384], P('segment', None, 'slab'), may hold values from -0.25 to 2
- conv_weight: bfloat16 [4, 3, 3, 3, 384, 384], P('segment'), may hold values from -0.0625 to 0.0625
- conv_bias: float32 [4, 384], P('segment'), may hold values from -1.5 to 1.5
- norm_gain: float32 [4, 384], P('segment'), may hold values from 0.5 to 2
Outputs:
- video_out: bfloat16 [8, 16, 64, 384], P('segment', 'slab')
- cache_out: bfloat16 [4, 2, 16, 64, 384], P('segment', None, 'slab')
The draws below stay inside these ranges and needn't reach their ends.
All inputs are finite; a program needn't handle non-finite values.
Results may differ from the reference program's by a relative error of at most 0.0067.
Values may be sent and summed in bfloat16 or wider, within the bound.
No kernel may reach another device: no remote copies, remote signals or barrier semaphores. Data moves between devices by JAX's collectives and lax.ppermute only.
A program may use at most 64 MiB of HBM per device.

```python
import math
import jax
import jax.numpy as jnp
from jax import lax

CHANNELS = 384
COLUMNS = 64
LAYERS = 4
FRAMES = 8
HEIGHT = 16


def block_levels(own_key, dims, cuts, least, top_value):
    factor_of, own = 1.0, jax.random.fold_in(own_key, 6)
    for axis_at, blocks in cuts:
        draws = jnp.exp(jax.random.uniform(jax.random.fold_in(own, axis_at), (blocks,), jnp.float32, least / len(cuts), top_value / len(cuts)))
        factor_of = factor_of * jnp.repeat(draws, dims[axis_at] // blocks).reshape([-1 if axis == axis_at else 1 for axis in range(len(dims))])
    return factor_of


def centred(rng, shape, width, limit, shards=(), held_as=jnp.bfloat16):
    factor_of = block_levels(rng, shape, shards, -0.22, 0.18) if shards else 1.0
    entries = jax.random.normal(rng, shape, jnp.float32) * width * factor_of
    return jnp.minimum(jnp.maximum(entries, -limit), limit).astype(held_as)


def setup_inputs(seed: int = 0) -> dict:
    key_of = jax.random.split(jax.random.key(seed), 6)
    video_in = centred(key_of[0], (FRAMES, HEIGHT, COLUMNS, CHANNELS), 1.0, 6.0, ((1, 8),))
    cache_in = jnp.clip(-0.25 + 2.25 * jax.random.uniform(key_of[1], (LAYERS, 2, HEIGHT, COLUMNS, CHANNELS), jnp.float32) ** block_levels(key_of[1], (LAYERS, 2, HEIGHT, COLUMNS, CHANNELS), ((0, 4), (2, 8)), -0.2, 0.2), -0.25, 2.0).astype(jnp.bfloat16)
    conv_weight = centred(key_of[2], (LAYERS, 3, 3, 3, CHANNELS, CHANNELS), (27 * CHANNELS) ** -0.5, 0.0625, ((0, 4),))
    conv_bias = centred(key_of[3], (LAYERS, CHANNELS), 0.3, 1.5, ((0, 4),), jnp.float32)
    norm_gain = jnp.clip(jnp.exp(math.log(2.0) - 1.3862944 * jax.random.uniform(key_of[4], (LAYERS, CHANNELS), jnp.float32) ** block_levels(key_of[4], (LAYERS, CHANNELS), ((0, 4),), -0.2, 0.2)), 0.5, 2.0)
    return {"video_in": video_in, "cache_in": cache_in, "conv_weight": conv_weight, "conv_bias": conv_bias, "norm_gain": norm_gain}


def activate(layer_in, gain):
    values = layer_in.astype(jnp.float32)
    scaled = values * lax.rsqrt(lax.optimization_barrier(jnp.mean(values * values, axis=-1, keepdims=True)) + 1e-06) * gain.astype(jnp.float32)
    return jax.nn.silu(scaled).astype(jnp.bfloat16)

def convolve(padded, weight, bias, frames_out):
    rows_out = padded.shape[1] - 2
    cols_out = padded.shape[2] - 2
    total = jnp.zeros((frames_out * rows_out * cols_out, CHANNELS), jnp.float32) + bias.astype(jnp.float32)
    for shift_t in range(3):
        for shift_h in range(3):
            for shift_w in range(3):
                piece = padded[shift_t:shift_t + frames_out, shift_h:shift_h + rows_out, shift_w:shift_w + cols_out]
                total = total + jnp.dot(piece.reshape(-1, CHANNELS), weight[shift_t, shift_h, shift_w], preferred_element_type=jnp.float32)
    return total.reshape(frames_out, rows_out, cols_out, CHANNELS)

def reference(video_in, cache_in, conv_weight, conv_bias, norm_gain):
    current = video_in
    caches = []
    for layer in range(LAYERS):
        acts = activate(current, norm_gain[layer])
        full = jnp.concatenate([cache_in[layer], acts], axis=0)
        padded = jnp.pad(full, ((0, 0), (1, 1), (1, 1), (0, 0)))
        conv = convolve(padded, conv_weight[layer], conv_bias[layer], FRAMES)
        current = (current.astype(jnp.float32) + conv).astype(jnp.bfloat16)
        caches.append(full[-2:])
    return (current, jnp.stack(caches))
```

```python
import functools
import jax
import jax.numpy as jnp
from jax import lax
from jax.experimental import pallas as pl
from jax.experimental.pallas import tpu as pltpu
from jax.sharding import PartitionSpec as P

LAG = 2
F32 = jnp.float32
BF16 = jnp.bfloat16


def shifted_pairs(segments, pairs_seg, slabs, step):
    return [
        (a * slabs + s, b * slabs + s + step)
        for a, b in pairs_seg
        for s in range(slabs)
        if 0 <= s + step < slabs
    ]


def stage_body(rows_in, rows_out, cols, frames, first_row, height,
               x_ref, hist_ref, w_ref, bias_ref, gain_ref, out_ref, hist_out_ref, cache_ref,
               xs, hs, buf, outs, ws, sems, own):
    lanes_in, lanes_out = rows_in * cols, rows_out * cols
    channels = xs.shape[1]
    copies = [
        pltpu.make_async_copy(x_ref.at[:, :, pl.ds(0, lanes_in)], xs.at[:, :, pl.ds(0, lanes_in)], sems.at[0]),
        pltpu.make_async_copy(hist_ref.at[:, :, pl.ds(0, lanes_in)], hs.at[:, :, pl.ds(0, lanes_in)], sems.at[1]),
    ]
    weights = [pltpu.make_async_copy(w_ref.at[a], ws.at[a], sems.at[2 + a]) for a in range(3)]
    for c in copies + weights:
        c.start()
    for c in copies:
        c.wait()
    gain = gain_ref[...]
    lane = lax.broadcasted_iota(jnp.int32, (1, lanes_in), 1)
    col = lax.rem(lane, cols)
    left = (col != 0).astype(F32)
    right = (col != cols - 1).astype(F32)
    for t in range(frames + 2):
        if t < 2:
            acts = hs[t, :, pl.ds(0, lanes_in)].astype(F32)
        else:
            values = xs[t - 2, :, pl.ds(0, lanes_in)].astype(F32)
            scale = lax.rsqrt(jnp.mean(values * values, axis=0, keepdims=True) + 1e-06)
            g = values * scale * gain
            acts = 0.5 * g * (1.0 + jnp.tanh(0.5 * g))
            if t >= frames:
                hs_new = acts.astype(BF16)
                hs[t - frames, :, pl.ds(0, lanes_in)] = hs_new
        sides = (pltpu.roll(acts, 1, 1) * left, acts, pltpu.roll(acts, lanes_in - 1, 1) * right)
        for c in range(3):
            piece = sides[c].astype(BF16)
            turned = pltpu.roll(sides[c], lanes_in - cols, 1).astype(BF16)
            for b in range(3):
                if (b * cols) % 128:
                    part = turned[:, (b - 1) * cols:(b - 1) * cols + lanes_out]
                else:
                    part = piece[:, b * cols:b * cols + lanes_out]
                buf[pl.ds((b * 3 + c) * channels, channels), pl.ds(t * lanes_out, lanes_out)] = part
    store = pltpu.make_async_copy(hs.at[:, :, pl.ds(0, lanes_in)], hist_out_ref.at[:, :, pl.ds(0, lanes_in)], sems.at[1])
    store.start()
    for t in range(2):
        kept = hs[t, :, pl.ds(0, lanes_in)].astype(F32)
        at = (rows_in - own) // 2 * cols
        if at % 128:
            kept = pltpu.roll(kept, lanes_in - at, 1)
            at = 0
        cache_ref[t] = kept[:, at:at + own * cols].astype(BF16)
    for c in weights:
        c.wait()
    step = 256
    skip = (rows_in - rows_out) // 2 * cols
    for t in range(frames):
        mid = xs[t, :, pl.ds(0, lanes_in)].astype(F32)
        outs[:, pl.ds(t * lanes_out, lanes_out)] = pltpu.roll(mid, lanes_in - skip, 1)[:, :lanes_out]

    def part(n, _):
        at = pl.multiple_of(n * step, step)
        total = bias_ref[...] + outs[:, pl.ds(at, step)]
        for a in range(3):
            total = total + jnp.dot(ws[a], buf[:, pl.ds(a * lanes_out + at, step)], preferred_element_type=F32)
        place = at + lax.broadcasted_iota(jnp.int32, (1, step), 1)
        row = first_row + lax.rem(place, lanes_out) // cols
        inside = jnp.logical_and(row >= 0, row < height)
        outs[:, pl.ds(at, step)] = jnp.where(inside, total, 0.0)
        return 0

    lax.fori_loop(0, frames * lanes_out // step, part, 0)
    for t in range(frames):
        xs[t, :, pl.ds(0, lanes_out)] = outs[:, pl.ds(t * lanes_out, lanes_out)].astype(BF16)
    done = pltpu.make_async_copy(xs.at[:, :, pl.ds(0, lanes_out)], out_ref.at[:, :, pl.ds(0, lanes_out)], sems.at[0])
    done.start()
    done.wait()
    store.wait()


def layer_kernel(stages, cols, frames, height, own, flags, *refs):
    n = len(stages)
    xs_in, hist_ref, w_ref, bias_ref, gain_ref = refs[:n], refs[n], refs[n + 1], refs[n + 2], refs[n + 3]
    out_ref, hist_out_ref, cache_ref = refs[n + 4:n + 7]
    scratch = refs[n + 7:]
    for k, (rows_in, rows_out) in enumerate(stages):
        @pl.when(flags[k] == 1)
        def _():
            first = flags[n] - (rows_out - own) // 2
            stage_body(rows_in, rows_out, cols, frames, first, height,
                       xs_in[k], hist_ref, w_ref, bias_ref, gain_ref, out_ref, hist_out_ref, cache_ref,
                       *scratch, own)


def layer_call(stages, cols, frames, height, own, flags, xs, hist, weight, bias, gain):
    channels = weight.shape[1]
    lanes_in = max(r for r, _ in stages) * cols
    lanes_out = max(r for _, r in stages) * cols
    any_space = pl.BlockSpec(memory_space=pl.ANY)
    vmem = pl.BlockSpec(memory_space=pltpu.VMEM)
    n = len(stages)
    return pl.pallas_call(
        functools.partial(layer_kernel, stages, cols, frames, height, own),
        out_shape=(
            jax.ShapeDtypeStruct((frames, channels, lanes_out), BF16),
            jax.ShapeDtypeStruct(hist.shape, BF16),
            jax.ShapeDtypeStruct((2, channels, own * cols), BF16),
        ),
        in_specs=[pl.BlockSpec(memory_space=pltpu.SMEM)] + [any_space] * (n + 2) + [vmem] * 2,
        out_specs=(any_space, any_space, vmem),
        scratch_shapes=[
            pltpu.VMEM((frames, channels, lanes_in), BF16),
            pltpu.VMEM((2, channels, lanes_in), BF16),
            pltpu.VMEM((9 * channels, (frames + 2) * lanes_out), BF16),
            pltpu.VMEM((channels, frames * lanes_out), F32),
            pltpu.VMEM(weight.shape, BF16),
            pltpu.SemaphoreType.DMA((5,)),
        ],
        input_output_aliases={n + 1: 1},
        compiler_params=pltpu.CompilerParams(vmem_limit_bytes=56 * 2**20),
        cost_estimate=pl.CostEstimate(
            flops=2 * frames * lanes_out * 27 * channels * channels,
            bytes_accessed=2 * 27 * channels * channels, transcendentals=0),
    )(flags, *xs, hist, weight, bias, gain)


def local(segments, slabs, video_in, cache_in, conv_weight, conv_bias, norm_gain):
    frames, own, cols, channels = video_in.shape
    height = own * slabs
    segment = lax.axis_index("segment")
    slab = lax.axis_index("slab")
    axes = ("segment", "slab")
    block = frames // segments
    blocks = frames // block
    reach = -(-segments // own)
    evens = [(g, g) for g in range(0, segments, 2)]
    odds = [(g, g) for g in range(1, segments, 2)]

    def around(value, pairs_seg):
        parts = []
        for step in range(-reach, reach + 1):
            if step == 0:
                parts.append(value)
            else:
                parts.append(lax.ppermute(value, axes, shifted_pairs(segments, pairs_seg, slabs, -step)))
        whole = jnp.concatenate(parts, axis=1)
        extra = reach * own - segments
        return whole[:, extra:whole.shape[1] - extra] if extra else whole

    def lanes(value):
        return value.transpose(0, 3, 1, 2).reshape(value.shape[0], channels, -1)

    first = jnp.concatenate([cache_in[0], video_in[:block]], axis=0)
    first = around(first, evens)
    odd_cache = around(cache_in[0], odds)
    later = around(video_in[block:], [(0, 0)])
    weight = conv_weight[0].transpose(0, 4, 1, 2, 3).reshape(3, channels, 9 * channels)
    bias = conv_bias[0].reshape(channels, 1)
    gain = norm_gain[0].reshape(channels, 1)

    rows_out = [own + 2 * (segments - 1 - g) for g in range(segments)]
    halves = []
    for parity in range(2):
        mine = list(range(parity, segments, 2))
        halves.append([(rows_out[g] + 2, rows_out[g]) for g in mine])
    wide = [max(r for r, _ in h) for h in halves]

    def history(rows, parity):
        result = None
        for g in range(parity, segments, 2):
            cut = (rows.shape[1] - rows_out[g] - 2) // 2
            piece = lanes(rows[:, cut:rows.shape[1] - cut] if cut else rows)
            piece = jnp.pad(piece, ((0, 0), (0, 0), (0, wide[parity] * cols - piece.shape[2])))
            result = piece if result is None else jnp.where(segment == g, piece, result)
        return result

    hist_even = history(first[:2], 0)
    hist_odd = history(odd_cache, 1)
    video = [lanes(first[2:])] + [lanes(later[b * block:(b + 1) * block]) for b in range(blocks - 1)]

    swap = [(g * slabs + s, (g ^ 1) * slabs + s) for g in range(segments) for s in range(slabs)]
    planes = segments // 2
    hop = [((2 * p + 1) * slabs + s, (2 * p + 2) * slabs + s) for p in range(planes - 1) for s in range(slabs)]
    arrived = [None] * (blocks + LAG * planes)
    done = []
    ticks = blocks + LAG * (planes - 1)
    cache_even = cache_odd = None
    for tick in range(ticks):
        def flags(parity):
            on = []
            for p in range(planes):
                b = tick - LAG * p
                on.append((segment == 2 * p + parity).astype(jnp.int32) if 0 <= b < blocks else jnp.int32(0))
            return jnp.stack(on + [slab * own])
        received = arrived[tick - LAG] if tick >= LAG else video[0]
        even_in = [video[min(tick, blocks - 1)]] + [received] * (planes - 1)
        out, hist_even, cache_even = layer_call(
            halves[0], cols, block, height, own, flags(0), even_in, hist_even, weight, bias, gain)
        crossed = lax.ppermute(out, axes, swap)
        out, hist_odd, cache_odd = layer_call(
            halves[1], cols, block, height, own, flags(1), [crossed] * planes, hist_odd, weight, bias, gain)
        if tick < blocks:
            arrived[tick] = lax.ppermute(out, axes, hop)
        b = tick - LAG * (planes - 1)
        if 0 <= b < blocks:
            final = out[:, :, :own * cols]
            if b < segments - 1:
                final = lax.ppermute(
                    final, axes, [((segments - 1) * slabs + s, b * slabs + s) for s in range(slabs)])
            done.append(final)
        if tick == blocks - 1:
            cache_first = cache_even, cache_odd

    def natural(value):
        return value.reshape(value.shape[0], channels, own, cols).transpose(0, 2, 3, 1)

    result = done[-1]
    for b in range(blocks - 1):
        result = jnp.where(segment == b, done[b], result)
    late = segment >= 2
    cache = jnp.where(
        segment % 2 == 0,
        jnp.where(late, cache_even, cache_first[0]),
        jnp.where(late, cache_odd, cache_first[1]))
    return natural(result), natural(cache)[None]


def solution(mesh):
    segments, slabs = mesh.shape["segment"], mesh.shape["slab"]
    return jax.shard_map(
        functools.partial(local, segments, slabs),
        mesh=mesh,
        in_specs=(
            P(None, "slab", None, None),
            P("segment", None, "slab", None, None),
            P("segment", None, None, None, None, None),
            P("segment", None),
            P("segment", None),
        ),
        out_specs=(P("segment", "slab", None, None), P("segment", None, "slab", None, None)),
        check_vma=False,
    )
```

```python
import functools
import jax
import jax.numpy as jnp
from jax import lax
from jax.experimental import pallas as pl
from jax.experimental.pallas import tpu as pltpu
from jax.sharding import PartitionSpec as P

LAG = 2
CHUNK = 32
F32 = jnp.float32
BF16 = jnp.bfloat16
ANY = pl.BlockSpec(memory_space=pl.ANY)
VMEM = pl.BlockSpec(memory_space=pltpu.VMEM)
SMEM = pl.BlockSpec(memory_space=pltpu.SMEM)


def turn_kernel(w_ref, out_ref):
    out_ref[0] = jnp.transpose(w_ref[0, 0, 0], (1, 0))


def turned_weight(weight):
    channels = weight.shape[-1]
    return pl.pallas_call(
        turn_kernel,
        grid=(3, 3, 3),
        out_shape=jax.ShapeDtypeStruct((3, channels, 9 * channels), BF16),
        in_specs=[pl.BlockSpec((1, 1, 1, channels, channels), lambda b, a, c: (a, b, c, 0, 0))],
        out_specs=pl.BlockSpec((1, channels, channels), lambda b, a, c: (b, 0, 3 * a + c)),
        cost_estimate=pl.CostEstimate(flops=0, bytes_accessed=4 * weight.size, transcendentals=0),
    )(weight)


def layer_kernel(cases, rows_in, own, cols, block, height, n_in, place_ref, w_ref, bias_ref, gain_ref, *refs):
    ins = refs[:n_in]
    out_ref, acts_ref = refs[n_in:n_in + 2]
    xs, buf, total, ws, sems, wsems = refs[n_in + 2:]
    channels = xs.shape[0]
    row = block * cols
    rows_out = rows_in - 2
    lanes_in, lanes_out = rows_in * row, rows_out * row
    segment, slab = place_ref[0], place_ref[1]

    def slot(a, c):
        return (3 * a + c) * channels

    def source(part):
        at, index = part[0], part[1]
        return ins[at] if index is None else ins[at].at[index]

    active = functools.reduce(jnp.logical_or, [segment == g for g, _, _ in cases])
    weights = [pltpu.make_async_copy(w_ref.at[b], ws.at[b], wsems.at[b]) for b in range(3)]

    @pl.when(active)
    def _():
        for w in weights:
            w.start()

    for g, x_parts, before in cases:
        @pl.when(segment == g)
        def _():
            copies = []
            for parts, target in ((x_parts, xs), (before, buf.at[pl.ds(slot(0, 1), channels)])):
                at = 0
                for part in parts:
                    src = source(part)
                    width = part[3] * row
                    copies.append(pltpu.make_async_copy(
                        src.at[:, pl.ds(part[2] * row, width)], target.at[:, pl.ds(at, width)],
                        sems.at[len(copies)]))
                    at += width
            for c in copies:
                c.start()
            for c in copies:
                c.wait()

    @pl.when(active)
    def _():
        def squares(i, acc):
            v = xs[pl.ds(pl.multiple_of(i * CHUNK, CHUNK), CHUNK), :].astype(F32)
            v = v * v
            for k in range(0, CHUNK, 8):
                acc = acc + v[k:k + 8]
            return acc

        acc = lax.fori_loop(0, channels // CHUNK, squares, jnp.zeros((8, lanes_in), F32))
        scale = lax.rsqrt(jnp.sum(acc, axis=0, keepdims=True) * (1.0 / channels) + 1e-06)
        lane = lax.broadcasted_iota(jnp.int32, (CHUNK, row), 1)
        col = lax.rem(lane, cols)
        first, last = col == 0, col == cols - 1
        head = lane < row - cols

        def spread(i, _):
            at = pl.multiple_of(i * CHUNK, CHUNK)
            gain = gain_ref[pl.ds(at, CHUNK), :]
            for r in range(rows_in):
                here = pl.ds(r * row, row)
                g = xs[pl.ds(at, CHUNK), here].astype(F32) * scale[:, r * row:(r + 1) * row] * gain
                new = (0.5 * g * (1.0 + jnp.tanh(0.5 * g))).astype(BF16).astype(F32)
                old = buf[pl.ds(slot(0, 1) + at, CHUNK), here].astype(F32)
                mixed = pltpu.roll(jnp.where(head, new, old), cols, 1)
                for a, v in enumerate((old, mixed, new)):
                    if a:
                        buf[pl.ds(slot(a, 1) + at, CHUNK), here] = v.astype(BF16)
                    left = jnp.where(first, 0.0, pltpu.roll(v, 1, 1))
                    right = jnp.where(last, 0.0, pltpu.roll(v, row - 1, 1))
                    buf[pl.ds(slot(a, 0) + at, CHUNK), here] = left.astype(BF16)
                    buf[pl.ds(slot(a, 2) + at, CHUNK), here] = right.astype(BF16)
            return 0

        lax.fori_loop(0, channels // CHUNK, spread, 0)
        acts_done = pltpu.make_async_copy(buf.at[pl.ds(slot(2, 1), channels)], acts_ref, sems.at[0])
        acts_done.start()
        step = 2 * row
        for n in range(0, lanes_out, step):
            def tap(b, _):
                @pl.when(n == 0)
                def _():
                    pltpu.make_async_copy(w_ref.at[b], ws.at[b], wsems.at[b]).wait()
                part = jnp.dot(ws[b], buf[:, pl.ds(pl.multiple_of(b * row + n, row), step)], preferred_element_type=F32)

                @pl.when(b == 0)
                def _():
                    total[:, pl.ds(n, step)] = part

                @pl.when(b > 0)
                def _():
                    total[:, pl.ds(n, step)] += part
                return 0
            lax.fori_loop(0, 3, tap, 0)

        top = slab * own - (rows_out - own) // 2

        def finish(i, _):
            at = pl.multiple_of(i * CHUNK, CHUNK)
            for r in range(rows_out):
                there = pl.ds(r * row, row)
                value = xs[pl.ds(at, CHUNK), pl.ds((r + 1) * row, row)].astype(F32)
                value = value + (total[pl.ds(at, CHUNK), there] + bias_ref[pl.ds(at, CHUNK), :])
                inside = jnp.logical_and(top + r >= 0, top + r < height)
                xs[pl.ds(at, CHUNK), there] = jnp.where(inside, value, 0.0).astype(BF16)
            return 0

        lax.fori_loop(0, channels // CHUNK, finish, 0)
        out_done = pltpu.make_async_copy(xs.at[:, pl.ds(0, lanes_out)], out_ref, sems.at[1])
        out_done.start()
        acts_done.wait()
        out_done.wait()


def layer_call(cases, rows_in, own, cols, block, height, place, weight, bias, gain, ins):
    channels = weight.shape[1]
    row = block * cols
    return pl.pallas_call(
        functools.partial(layer_kernel, cases, rows_in, own, cols, block, height, len(ins)),
        out_shape=(
            jax.ShapeDtypeStruct((channels, (rows_in - 2) * row), BF16),
            jax.ShapeDtypeStruct((channels, rows_in * row), BF16),
        ),
        in_specs=[SMEM, ANY, VMEM, VMEM] + [ANY] * len(ins),
        out_specs=(ANY, ANY),
        scratch_shapes=[
            pltpu.VMEM((channels, rows_in * row), BF16),
            pltpu.VMEM((9 * channels, rows_in * row), BF16),
            pltpu.VMEM((channels, (rows_in - 2) * row), F32),
            pltpu.VMEM(weight.shape, BF16),
            pltpu.SemaphoreType.DMA((8,)),
            pltpu.SemaphoreType.DMA((3,)),
        ],
        compiler_params=pltpu.CompilerParams(vmem_limit_bytes=40 * 2**20),
        cost_estimate=pl.CostEstimate(
            flops=2 * (rows_in - 2) * row * 27 * channels * channels,
            bytes_accessed=2 * 27 * channels * channels, transcendentals=0),
    )(place, weight, bias, gain, *ins)


def local(segments, slabs, video_in, cache_in, conv_weight, conv_bias, norm_gain):
    frames, own, cols, channels = video_in.shape
    height = own * slabs
    segment = lax.axis_index("segment")
    slab = lax.axis_index("slab")
    axes = ("segment", "slab")
    block = frames // segments
    row = block * cols
    blocks = frames // block
    place = jnp.stack([segment, slab]).astype(jnp.int32)
    evens = range(0, segments, 2)
    odds = range(1, segments, 2)

    def moved(value, pairs, step):
        return lax.ppermute(value, axes, [
            (a * slabs + s, b * slabs + s + step) for a, b in pairs for s in range(slabs) if 0 <= s + step < slabs])

    def around(value, pairs, rows):
        above = moved(value[..., (own - rows) * row:], pairs, 1)
        below = moved(value[..., :rows * row], pairs, -1)
        return above, below

    def lanes(value):
        value = value.reshape(-1, block, own, cols, channels)
        return value.transpose(0, 4, 2, 1, 3).reshape(-1, channels, own * row)

    first = lanes(jnp.concatenate([cache_in[0], video_in[:block]], axis=0))
    later = lanes(video_in[block:])
    first_above, first_below = around(first, [(g, g) for g in evens], 2)
    weight = turned_weight(conv_weight[0])
    odd_above, odd_below = around(first[0], [(g, g) for g in odds], 1)
    later_above, later_below = around(later, [(0, 0)], 2)
    bias = conv_bias[0].reshape(channels, 1)
    gain = norm_gain[0].reshape(channels, 1)

    call = functools.partial(layer_call, own=own, cols=cols, block=block, height=height,
                             place=place, weight=weight, bias=bias, gain=gain)
    swap = [(g * slabs + s, (g ^ 1) * slabs + s) for g in range(segments) for s in range(slabs)]
    hop = [(g, g + 1) for g in odds if g + 1 < segments]
    planes = segments // 2
    arrived, done = [], []
    even_acts = odd_acts = None
    even_cache, odd_cache = [None] * planes, [None] * planes
    for tick in range(blocks + LAG * (planes - 1)):
        busy = [p for p in range(planes) if 0 <= tick - LAG * p < blocks]
        ins = [first, first_above, first_below]
        old = [(1, 0, 0, 2), (0, 0, 0, own), (2, 0, 0, 2)]
        if tick:
            ins.append(even_acts)
            kept = [(3, None, 0, own + 4)]
        cases = []
        for p in busy:
            b = tick - LAG * p
            if p == 0 and b == 0:
                parts = [(1, 1, 0, 2), (0, 1, 0, own), (2, 1, 0, 2)]
            else:
                n = len(ins)
                if p == 0:
                    ins += [later, later_above, later_below]
                    parts = [(n + 1, b - 1, 0, 2), (n, b - 1, 0, own), (n + 2, b - 1, 0, 2)]
                else:
                    ins += list(arrived[b])
                    parts = [(n + 1, None, 0, 2), (n, None, 0, own), (n + 2, None, 0, 2)]
            cases.append((2 * p, parts, old if b == 0 else kept))
        out, even_acts = call(cases, own + 4, ins=ins)
        crossed = lax.ppermute(out, axes, swap)

        ins = [crossed, first, odd_above, odd_below]
        old = [(2, None, 0, 1), (1, 0, 0, own), (3, None, 0, 1)]
        if tick:
            ins.append(odd_acts)
        cases = [(2 * p + 1, [(0, None, 0, own + 2)], old if tick == LAG * p else [(4, None, 0, own + 2)]) for p in busy]
        out, odd_acts = call(cases, own + 2, ins=ins)
        if tick < blocks:
            arrived.append((moved(out, hop, 0), moved(out[:, (own - 2) * row:], hop, 1), moved(out[:, :2 * row], hop, -1)))
        b = tick - LAG * (planes - 1)
        if 0 <= b < blocks:
            done.append(out if b == segments - 1 else moved(out, [(segments - 1, b)], 0))
        for p in busy:
            if tick - LAG * p == blocks - 1:
                even_cache[p] = even_acts[:, 2 * row:(2 + own) * row]
                odd_cache[p] = odd_acts[:, row:(1 + own) * row]

    def natural(value):
        return value.reshape(channels, own, block, cols).transpose(2, 1, 3, 0)

    result = done[-1]
    for b in range(blocks - 1):
        result = jnp.where(segment == b, done[b], result)
    cache = odd_cache[-1]
    for p in range(planes):
        cache = jnp.where(segment == 2 * p, even_cache[p], cache)
        cache = jnp.where(segment == 2 * p + 1, odd_cache[p], cache)
    return natural(result), natural(cache)[None]


def solution(mesh):
    segments, slabs = mesh.shape["segment"], mesh.shape["slab"]
    return jax.shard_map(
        functools.partial(local, segments, slabs),
        mesh=mesh,
        in_specs=(
            P(None, "slab", None, None),
            P("segment", None, "slab", None, None),
            P("segment", None, None, None, None, None),
            P("segment", None),
            P("segment", None),
        ),
        out_specs=(P("segment", "slab", None, None), P("segment", None, "slab", None, None)),
        check_vma=False,
    )
```

```python
import functools
import jax
import jax.numpy as jnp
from jax import lax
from jax.experimental import pallas as pl
from jax.experimental.pallas import tpu as pltpu
from jax.sharding import PartitionSpec as P

LAG = 1
CHUNK = 128
VMEM_BYTES = 24 * 2**20
F32 = jnp.float32
BF16 = jnp.bfloat16
ANY = pl.BlockSpec(memory_space=pl.ANY)
VMEM = pl.BlockSpec(memory_space=pltpu.VMEM)
SMEM = pl.BlockSpec(memory_space=pltpu.SMEM)


def turn_kernel(w_ref, out_ref, ws, sems):
    channels = w_ref.shape[-1]
    copies = [pltpu.make_async_copy(w_ref.at[k // 3, k % 3], ws.at[k], sems.at[k]) for k in range(9)]
    for copy in copies:
        copy.start()
    for k, copy in enumerate(copies):
        copy.wait()
        for c in range(3):
            out_ref[k % 3, :, pl.ds((k // 3 * 3 + c) * channels, channels)] = jnp.transpose(ws[k, c], (1, 0))


def turned_weight(weight):
    channels = weight.shape[-1]
    turned = pl.pallas_call(
        turn_kernel,
        out_shape=jax.ShapeDtypeStruct((3, channels, 9 * channels), BF16),
        in_specs=[ANY],
        out_specs=VMEM,
        scratch_shapes=[pltpu.VMEM((9, 3, channels, channels), BF16), pltpu.SemaphoreType.DMA((9,))],
        compiler_params=pltpu.CompilerParams(vmem_limit_bytes=VMEM_BYTES),
        cost_estimate=pl.CostEstimate(flops=0, bytes_accessed=4 * weight.size, transcendentals=0),
    )(weight)
    return pltpu.with_memory_space_constraint(turned, pltpu.VMEM)


def layer_kernel(cases, rows_in, own, cols, block, height, n_in, place_ref, w_ref, bias_ref, gain_ref, *refs):
    ins = refs[:n_in]
    out_ref, acts_ref, next_ref = refs[n_in:n_in + 3]
    xs, buf, total, sems = refs[n_in + 3:]
    channels = xs.shape[0]
    row = block * cols
    rows_out = rows_in - 2
    lanes_in, lanes_out = rows_in * row, rows_out * row
    segment, slab = place_ref[0], place_ref[1]
    next_ref[0], next_ref[1] = segment, slab

    def slot(a, c):
        return (3 * a + c) * channels

    def source(part):
        at, index = part[0], part[1]
        return ins[at] if index is None else ins[at].at[index]

    active = functools.reduce(jnp.logical_or, [segment == g for g, _, _ in cases])
    for g, x_parts, before in cases:
        @pl.when(segment == g)
        def _():
            copies = []
            for parts, target in ((x_parts, xs), (before, buf.at[pl.ds(slot(0, 1), channels)])):
                at = 0
                for part in parts:
                    src = source(part)
                    width = part[3] * row
                    copies.append(pltpu.make_async_copy(
                        src.at[:, pl.ds(part[2] * row, width)], target.at[:, pl.ds(at, width)],
                        sems.at[len(copies)]))
                    at += width
            for c in copies:
                c.start()
            for c in copies:
                c.wait()

    @pl.when(active)
    def _():
        def squares(i, acc):
            v = xs[pl.ds(pl.multiple_of(i * CHUNK, CHUNK), CHUNK), :].astype(F32)
            v = v * v
            for k in range(0, CHUNK, 8):
                acc = acc + v[k:k + 8]
            return acc

        acc = lax.fori_loop(0, channels // CHUNK, squares, jnp.zeros((8, lanes_in), F32))
        scale = lax.rsqrt(jnp.sum(acc, axis=0, keepdims=True) * (1.0 / channels) + 1e-06)
        lane = lax.broadcasted_iota(jnp.int32, (CHUNK, row), 1)
        col = lax.rem(lane, cols)
        first, last = col == 0, col == cols - 1
        head = lane < row - cols
        zero = jnp.zeros((), BF16)

        def spread(i, _):
            at = pl.multiple_of(i * CHUNK, CHUNK)
            gain = gain_ref[pl.ds(at, CHUNK), :]
            here = [pl.ds(r * row, row) for r in range(rows_in)]
            values = [xs[pl.ds(at, CHUNK), h].astype(F32) for h in here]
            olds = [buf[pl.ds(slot(0, 1) + at, CHUNK), h] for h in here]
            results = []
            for r in range(rows_in):
                g = values[r] * scale[:, r * row:(r + 1) * row] * gain
                new = (0.5 * g * (1.0 + jnp.tanh(0.5 * g))).astype(BF16)
                mixed = pltpu.roll(jnp.where(head, new, olds[r]), cols, 1)
                for a, v in enumerate((olds[r], mixed, new)):
                    results.append((a, 0, r, jnp.where(first, zero, pltpu.roll(v, 1, 1))))
                    results.append((a, 2, r, jnp.where(last, zero, pltpu.roll(v, row - 1, 1))))
                    if a:
                        results.append((a, 1, r, v))
            for a, c, r, v in results:
                buf[pl.ds(slot(a, c) + at, CHUNK), here[r]] = v
            return 0

        lax.fori_loop(0, channels // CHUNK, spread, 0)
        acts_done = pltpu.make_async_copy(buf.at[pl.ds(slot(2, 1), channels)], acts_ref, sems.at[0])
        acts_done.start()
        step = 2 * row
        for n in range(0, lanes_out, step):
            total[:, pl.ds(n, step)] = sum(
                jnp.dot(w_ref[b], buf[:, pl.ds(b * row + n, step)], preferred_element_type=F32) for b in range(3))

        top = slab * own - (rows_out - own) // 2

        def finish(i, _):
            at = pl.multiple_of(i * CHUNK, CHUNK)
            bias = bias_ref[pl.ds(at, CHUNK), :]
            sums = []
            for r in range(rows_out):
                value = xs[pl.ds(at, CHUNK), pl.ds((r + 1) * row, row)].astype(F32)
                value = value + (total[pl.ds(at, CHUNK), pl.ds(r * row, row)] + bias)
                inside = jnp.logical_and(top + r >= 0, top + r < height)
                sums.append(jnp.where(inside, value, 0.0).astype(BF16))
            for r in range(rows_out):
                xs[pl.ds(at, CHUNK), pl.ds(r * row, row)] = sums[r]
            return 0

        lax.fori_loop(0, channels // CHUNK, finish, 0)
        out_done = pltpu.make_async_copy(xs.at[:, pl.ds(0, lanes_out)], out_ref, sems.at[1])
        out_done.start()
        acts_done.wait()
        out_done.wait()


def layer_call(cases, rows_in, own, cols, block, height, place, weight, bias, gain, ins):
    channels = weight.shape[1]
    row = block * cols
    return pl.pallas_call(
        functools.partial(layer_kernel, cases, rows_in, own, cols, block, height, len(ins)),
        out_shape=(
            jax.ShapeDtypeStruct((channels, (rows_in - 2) * row), BF16),
            jax.ShapeDtypeStruct((channels, rows_in * row), BF16),
            jax.ShapeDtypeStruct(place.shape, place.dtype),
        ),
        in_specs=[SMEM, VMEM, VMEM, VMEM] + [ANY] * len(ins),
        out_specs=(ANY, ANY, SMEM),
        scratch_shapes=[
            pltpu.VMEM((channels, rows_in * row), BF16),
            pltpu.VMEM((9 * channels, rows_in * row), BF16),
            pltpu.VMEM((channels, (rows_in - 2) * row), F32),
            pltpu.SemaphoreType.DMA((8,)),
        ],
        compiler_params=pltpu.CompilerParams(vmem_limit_bytes=VMEM_BYTES),
        cost_estimate=pl.CostEstimate(
            flops=2 * (rows_in - 2) * row * 27 * channels * channels, bytes_accessed=0, transcendentals=0),
    )(place, weight, bias, gain, *ins)


def local(segments, slabs, video_in, cache_in, conv_weight, conv_bias, norm_gain):
    frames, own, cols, channels = video_in.shape
    height = own * slabs
    segment = lax.axis_index("segment")
    slab = lax.axis_index("slab")
    axes = ("segment", "slab")
    block = frames // segments
    row = block * cols
    blocks = frames // block
    place = jnp.stack([segment, slab]).astype(jnp.int32)
    evens = range(0, segments, 2)
    odds = range(1, segments, 2)

    def moved(value, pairs, step):
        return lax.ppermute(value, axes, [
            (a * slabs + s, b * slabs + s + step) for a, b in pairs for s in range(slabs) if 0 <= s + step < slabs])

    def around(value, pairs, rows):
        above = moved(value[..., (own - rows) * row:], pairs, 1)
        below = moved(value[..., :rows * row], pairs, -1)
        return above, below

    def lanes(value):
        value = value.reshape(-1, block, own, cols, channels)
        return value.transpose(0, 4, 2, 1, 3).reshape(-1, channels, own * row)

    first = lanes(jnp.concatenate([cache_in[0], video_in[:block]], axis=0))
    first_above, first_below = around(first, [(g, g) for g in evens], 2)
    later, first_above, first_below = lax.optimization_barrier((lanes(video_in[block:]), first_above, first_below))
    weight = turned_weight(conv_weight[0])
    odd_above, odd_below = around(first[0], [(g, g) for g in odds], 1)
    later_above, later_below = around(later, [(0, 0)], 2)
    bias = conv_bias[0].reshape(channels, 1)
    gain = norm_gain[0].reshape(channels, 1)

    call = functools.partial(layer_call, own=own, cols=cols, block=block, height=height,
                             weight=weight, bias=bias, gain=gain)
    swap = [(g * slabs + s, (g ^ 1) * slabs + s) for g in range(segments) for s in range(slabs)]
    hop = [(g, g + 1) for g in odds if g + 1 < segments]
    planes = segments // 2
    arrived, done = [], []
    even_acts = odd_acts = None
    even_cache, odd_cache = [None] * planes, [None] * planes
    for tick in range(blocks + LAG * (planes - 1)):
        busy = [p for p in range(planes) if 0 <= tick - LAG * p < blocks]
        ins = [first, first_above, first_below]
        old = [(1, 0, 0, 2), (0, 0, 0, own), (2, 0, 0, 2)]
        if tick:
            ins.append(even_acts)
            kept = [(3, None, 0, own + 4)]
        cases = []
        for p in busy:
            b = tick - LAG * p
            if p == 0 and b == 0:
                parts = [(1, 1, 0, 2), (0, 1, 0, own), (2, 1, 0, 2)]
            else:
                n = len(ins)
                if p == 0:
                    ins += [later, later_above, later_below]
                    parts = [(n + 1, b - 1, 0, 2), (n, b - 1, 0, own), (n + 2, b - 1, 0, 2)]
                else:
                    ins += list(arrived[b])
                    parts = [(n + 1, None, 0, 2), (n, None, 0, own), (n + 2, None, 0, 2)]
            cases.append((2 * p, parts, old if b == 0 else kept))
        if tick == blocks + LAG * (planes - 1) - 1:
            ins += done[:-1]
        out, even_acts, place = call(cases, own + 4, place=place, ins=ins)
        crossed = lax.ppermute(out, axes, swap)

        ins = [crossed, first, odd_above, odd_below]
        old = [(2, None, 0, 1), (1, 0, 0, own), (3, None, 0, 1)]
        if tick:
            ins.append(odd_acts)
        if tick == blocks + LAG * (planes - 1) - 1:
            ins.append(done[-1])
        cases = [(2 * p + 1, [(0, None, 0, own + 2)], old if tick == LAG * p else [(4, None, 0, own + 2)]) for p in busy]
        out, odd_acts, place = call(cases, own + 2, place=place, ins=ins)
        if tick < blocks:
            arrived.append((moved(out, hop, 0), moved(out[:, (own - 2) * row:], hop, 1), moved(out[:, :2 * row], hop, -1)))
        b = tick - LAG * (planes - 1)
        if 0 <= b < blocks:
            done.append(out if b == segments - 1 else moved(out, [(segments - 1, b)], 0))
        for p in busy:
            if tick - LAG * p == blocks - 1:
                even_cache[p] = even_acts[:, 2 * row:(2 + own) * row]
                odd_cache[p] = odd_acts[:, row:(1 + own) * row]

    def natural(value):
        return value.reshape(channels, own, block, cols).transpose(2, 1, 3, 0)

    result = done[-1]
    for b in range(blocks - 1):
        result = jnp.where(segment == b, done[b], result)
    cache = odd_cache[-1]
    for p in range(planes):
        cache = jnp.where(segment == 2 * p, even_cache[p], cache)
        cache = jnp.where(segment == 2 * p + 1, odd_cache[p], cache)
    return natural(result), natural(cache)[None]


def solution(mesh):
    segments, slabs = mesh.shape["segment"], mesh.shape["slab"]
    return jax.shard_map(
        functools.partial(local, segments, slabs),
        mesh=mesh,
        in_specs=(
            P(None, "slab", None, None),
            P("segment", None, "slab", None, None),
            P("segment", None, None, None, None, None),
            P("segment", None),
            P("segment", None),
        ),
        out_specs=(P("segment", "slab", None, None), P("segment", None, "slab", None, None)),
        check_vma=False,
    )
```

```python
import functools
import jax
import jax.numpy as jnp
from jax import lax
from jax.experimental import pallas as pl
from jax.experimental.pallas import tpu as pltpu
from jax.sharding import PartitionSpec as P

LAG = 2
CHUNK = 128
VMEM_BYTES = 56 * 2**20
F32 = jnp.float32
BF16 = jnp.bfloat16
ANY = pl.BlockSpec(memory_space=pl.ANY)
VMEM = pl.BlockSpec(memory_space=pltpu.VMEM)
SMEM = pl.BlockSpec(memory_space=pltpu.SMEM)


def turn_kernel(w_ref, out_ref, ws, turned, sems, out_sems):
    channels = w_ref.shape[-1]
    copies = [pltpu.make_async_copy(w_ref.at[k % 3, k // 3], ws.at[k], sems.at[k]) for k in range(9)]
    outs = [pltpu.make_async_copy(turned.at[b], out_ref.at[b], out_sems.at[b]) for b in range(3)]
    for copy in copies:
        copy.start()
    for k, copy in enumerate(copies):
        copy.wait()
        for c in range(3):
            turned[k // 3, :, pl.ds((k % 3 * 3 + c) * channels, channels)] = jnp.transpose(ws[k, c], (1, 0))
        if k % 3 == 2:
            outs[k // 3].start()
    for out in outs:
        out.wait()


def turned_weight(weight):
    channels = weight.shape[-1]
    shape = (3, channels, 9 * channels)
    return pl.pallas_call(
        turn_kernel,
        out_shape=jax.ShapeDtypeStruct(shape, BF16),
        in_specs=[ANY],
        out_specs=ANY,
        scratch_shapes=[
            pltpu.VMEM((9, 3, channels, channels), BF16),
            pltpu.VMEM(shape, BF16),
            pltpu.SemaphoreType.DMA((9,)),
            pltpu.SemaphoreType.DMA((3,)),
        ],
        compiler_params=pltpu.CompilerParams(vmem_limit_bytes=VMEM_BYTES),
        cost_estimate=pl.CostEstimate(flops=0, bytes_accessed=4 * weight.size, transcendentals=0),
    )(weight)


def layer_kernel(cases, rows_in, own, cols, block, height, n_in, place_ref, w_ref, bias_ref, gain_ref, *refs):
    ins = refs[:n_in]
    out_ref, acts_ref, next_ref = refs[n_in:n_in + 3]
    xs, buf, total, ws, sems, wsems = refs[n_in + 3:]
    channels = xs.shape[0]
    row = block * cols
    rows_out = rows_in - 2
    lanes_in, lanes_out = rows_in * row, rows_out * row
    segment, slab = place_ref[0], place_ref[1]
    next_ref[0], next_ref[1] = segment, slab

    def slot(a, c):
        return (3 * a + c) * channels

    def source(part):
        at, index = part[0], part[1]
        return ins[at] if index is None else ins[at].at[index]

    active = functools.reduce(jnp.logical_or, [segment == g for g, _, _ in cases])
    weights = [pltpu.make_async_copy(w_ref.at[b], ws.at[b], wsems.at[b]) for b in range(3)]

    for g, x_parts, before in cases:
        @pl.when(segment == g)
        def _():
            copies = []
            for parts, target in ((x_parts, xs), (before, buf.at[pl.ds(slot(0, 1), channels)])):
                at = 0
                for part in parts:
                    src = source(part)
                    width = part[3] * row
                    copies.append(pltpu.make_async_copy(
                        src.at[:, pl.ds(part[2] * row, width)], target.at[:, pl.ds(at, width)],
                        sems.at[len(copies)]))
                    at += width
            for c in copies + weights:
                c.start()
            for c in copies:
                c.wait()

    @pl.when(active)
    def _():
        def squares(i, acc):
            v = xs[pl.ds(pl.multiple_of(i * CHUNK, CHUNK), CHUNK), :].astype(F32)
            v = v * v
            for k in range(0, CHUNK, 8):
                acc = acc + v[k:k + 8]
            return acc

        acc = lax.fori_loop(0, channels // CHUNK, squares, jnp.zeros((8, lanes_in), F32))
        scale = lax.rsqrt(jnp.sum(acc, axis=0, keepdims=True) * (1.0 / channels) + 1e-06)
        lane = lax.broadcasted_iota(jnp.int32, (CHUNK, row), 1)
        col = lax.rem(lane, cols)
        first, last = col == 0, col == cols - 1
        head = lane < row - cols
        zero = jnp.zeros((), BF16)

        def spread(i, _):
            at = pl.multiple_of(i * CHUNK, CHUNK)
            gain = gain_ref[pl.ds(at, CHUNK), :]
            here = [pl.ds(r * row, row) for r in range(rows_in)]
            values = [xs[pl.ds(at, CHUNK), h].astype(F32) for h in here]
            olds = [buf[pl.ds(slot(0, 1) + at, CHUNK), h] for h in here]
            results = []
            for r in range(rows_in):
                g = values[r] * scale[:, r * row:(r + 1) * row] * gain
                new = (0.5 * g * (1.0 + jnp.tanh(0.5 * g))).astype(BF16)
                mixed = pltpu.roll(jnp.where(head, new, olds[r]), cols, 1)
                for a, v in enumerate((olds[r], mixed, new)):
                    results.append((a, 0, r, jnp.where(first, zero, pltpu.roll(v, 1, 1))))
                    results.append((a, 2, r, jnp.where(last, zero, pltpu.roll(v, row - 1, 1))))
                    if a:
                        results.append((a, 1, r, v))
            for a, c, r, v in results:
                buf[pl.ds(slot(a, c) + at, CHUNK), here[r]] = v
            return 0

        lax.fori_loop(0, channels // CHUNK, spread, 0)
        acts_done = pltpu.make_async_copy(buf.at[pl.ds(slot(2, 1), channels)], acts_ref, sems.at[0])
        acts_done.start()
        step = 2 * row
        for n in range(0, lanes_out, step):
            part = None
            for b in range(3):
                if n == 0:
                    weights[b].wait()
                tap = jnp.dot(ws[b], buf[:, pl.ds(b * row + n, step)], preferred_element_type=F32)
                part = tap if part is None else part + tap
            total[:, pl.ds(n, step)] = part

        top = slab * own - (rows_out - own) // 2

        def finish(i, _):
            at = pl.multiple_of(i * CHUNK, CHUNK)
            bias = bias_ref[pl.ds(at, CHUNK), :]
            sums = []
            for r in range(rows_out):
                value = xs[pl.ds(at, CHUNK), pl.ds((r + 1) * row, row)].astype(F32)
                value = value + (total[pl.ds(at, CHUNK), pl.ds(r * row, row)] + bias)
                inside = jnp.logical_and(top + r >= 0, top + r < height)
                sums.append(jnp.where(inside, value, 0.0).astype(BF16))
            for r in range(rows_out):
                xs[pl.ds(at, CHUNK), pl.ds(r * row, row)] = sums[r]
            return 0

        lax.fori_loop(0, channels // CHUNK, finish, 0)
        out_done = pltpu.make_async_copy(xs.at[:, pl.ds(0, lanes_out)], out_ref, sems.at[1])
        out_done.start()
        acts_done.wait()
        out_done.wait()


def layer_call(cases, rows_in, own, cols, block, height, place, weight, bias, gain, ins):
    channels = weight.shape[1]
    row = block * cols
    return pl.pallas_call(
        functools.partial(layer_kernel, cases, rows_in, own, cols, block, height, len(ins)),
        out_shape=(
            jax.ShapeDtypeStruct((channels, (rows_in - 2) * row), BF16),
            jax.ShapeDtypeStruct((channels, rows_in * row), BF16),
            jax.ShapeDtypeStruct(place.shape, place.dtype),
        ),
        in_specs=[SMEM, ANY, VMEM, VMEM] + [ANY] * len(ins),
        out_specs=(ANY, ANY, SMEM),
        scratch_shapes=[
            pltpu.VMEM((channels, rows_in * row), BF16),
            pltpu.VMEM((9 * channels, rows_in * row), BF16),
            pltpu.VMEM((channels, (rows_in - 2) * row), F32),
            pltpu.VMEM(weight.shape, BF16),
            pltpu.SemaphoreType.DMA((8,)),
            pltpu.SemaphoreType.DMA((3,)),
        ],
        compiler_params=pltpu.CompilerParams(vmem_limit_bytes=VMEM_BYTES),
        cost_estimate=pl.CostEstimate(
            flops=2 * (rows_in - 2) * row * 27 * channels * channels, bytes_accessed=0, transcendentals=0),
    )(place, weight, bias, gain, *ins)


def local(segments, slabs, video_in, cache_in, conv_weight, conv_bias, norm_gain):
    frames, own, cols, channels = video_in.shape
    height = own * slabs
    segment = lax.axis_index("segment")
    slab = lax.axis_index("slab")
    axes = ("segment", "slab")
    block = frames // segments
    row = block * cols
    blocks = frames // block
    place = jnp.stack([segment, slab]).astype(jnp.int32)
    evens = range(0, segments, 2)
    odds = range(1, segments, 2)

    def moved(value, pairs, step):
        return lax.ppermute(value, axes, [
            (a * slabs + s, b * slabs + s + step) for a, b in pairs for s in range(slabs) if 0 <= s + step < slabs])

    def around(value, pairs, rows):
        above = moved(value[..., (own - rows) * row:], pairs, 1)
        below = moved(value[..., :rows * row], pairs, -1)
        return above, below

    def lanes(value):
        value = value.reshape(-1, block, own, cols, channels)
        return value.transpose(0, 4, 2, 1, 3).reshape(-1, channels, own * row)

    first = lanes(jnp.concatenate([cache_in[0], video_in[:block]], axis=0))
    first_above, first_below = around(first, [(g, g) for g in evens], 2)
    later, first_above, first_below = lax.optimization_barrier((lanes(video_in[block:]), first_above, first_below))
    weight = turned_weight(conv_weight[0])
    odd_above, odd_below = around(first[0], [(g, g) for g in odds], 1)
    later_above, later_below = around(later, [(0, 0)], 2)
    bias = conv_bias[0].reshape(channels, 1)
    gain = norm_gain[0].reshape(channels, 1)

    call = functools.partial(layer_call, own=own, cols=cols, block=block, height=height,
                             weight=weight, bias=bias, gain=gain)
    across = [(g, g + 1) for g in evens]
    hop = [(g, g + 1) for g in odds if g + 1 < segments]
    planes = segments // 2
    arrived, done = [], []
    even_acts = odd_acts = None
    even_cache, odd_cache = [None] * planes, [None] * planes
    for tick in range(blocks + LAG * (planes - 1)):
        busy = [p for p in range(planes) if 0 <= tick - LAG * p < blocks]
        ins = [first, first_above, first_below]
        old = [(1, 0, 0, 2), (0, 0, 0, own), (2, 0, 0, 2)]
        if tick:
            ins.append(even_acts)
            kept = [(3, None, 0, own + 4)]
        cases = []
        for p in busy:
            b = tick - LAG * p
            if p == 0 and b == 0:
                parts = [(1, 1, 0, 2), (0, 1, 0, own), (2, 1, 0, 2)]
            else:
                n = len(ins)
                if p == 0:
                    ins += [later, later_above, later_below]
                    parts = [(n + 1, b - 1, 0, 2), (n, b - 1, 0, own), (n + 2, b - 1, 0, 2)]
                else:
                    ins += list(arrived[b])
                    parts = [(n + 1, None, 0, 2), (n, None, 0, own), (n + 2, None, 0, 2)]
            cases.append((2 * p, parts, old if b == 0 else kept))
        if tick == 0:
            ins += [odd_above, odd_below]
        if tick == blocks + LAG * (planes - 1) - 1:
            ins += done[:-1]
        out, even_acts, place = call(cases, own + 4, place=place, ins=ins)
        crossed = moved(out, across, 0)

        ins = [crossed, first, odd_above, odd_below]
        old = [(2, None, 0, 1), (1, 0, 0, own), (3, None, 0, 1)]
        if tick:
            ins.append(odd_acts)
        if tick == 0:
            ins += [later_above, later_below]
        if tick == blocks + LAG * (planes - 1) - 1:
            ins.append(done[-1])
        cases = [(2 * p + 1, [(0, None, 0, own + 2)], old if tick == LAG * p else [(4, None, 0, own + 2)]) for p in busy]
        out, odd_acts, place = call(cases, own + 2, place=place, ins=ins)
        if tick < blocks:
            arrived.append((moved(out, hop, 0), moved(out[:, (own - 2) * row:], hop, 1), moved(out[:, :2 * row], hop, -1)))
        b = tick - LAG * (planes - 1)
        if 0 <= b < blocks:
            done.append(out if b == segments - 1 else moved(out, [(segments - 1, b)], 0))
        for p in busy:
            if tick - LAG * p == blocks - 1:
                even_cache[p] = even_acts[:, 2 * row:(2 + own) * row]
                odd_cache[p] = odd_acts[:, row:(1 + own) * row]

    def natural(value):
        return value.reshape(channels, own, block, cols).transpose(2, 1, 3, 0)

    result = done[-1]
    for b in range(blocks - 1):
        result = jnp.where(segment == b, done[b], result)
    cache = odd_cache[-1]
    for p in range(planes):
        cache = jnp.where(segment == 2 * p, even_cache[p], cache)
        cache = jnp.where(segment == 2 * p + 1, odd_cache[p], cache)
    return natural(result), natural(cache)[None]


def solution(mesh):
    segments, slabs = mesh.shape["segment"], mesh.shape["slab"]
    return jax.shard_map(
        functools.partial(local, segments, slabs),
        mesh=mesh,
        in_specs=(
            P(None, "slab", None, None),
            P("segment", None, "slab", None, None),
            P("segment", None, None, None, None, None),
            P("segment", None),
            P("segment", None),
        ),
        out_specs=(P("segment", "slab", None, None), P("segment", None, "slab", None, None)),
        check_vma=False,
    )
```

```python
import functools
import jax
import jax.numpy as jnp
from jax import lax
from jax.experimental import pallas as pl
from jax.experimental.pallas import tpu as pltpu
from jax.sharding import PartitionSpec as P

LAG = 2
CHUNK = 128
VMEM_BYTES = 24 * 2**20
F32 = jnp.float32
BF16 = jnp.bfloat16
ANY = pl.BlockSpec(memory_space=pl.ANY)
VMEM = pl.BlockSpec(memory_space=pltpu.VMEM)
SMEM = pl.BlockSpec(memory_space=pltpu.SMEM)


def turn_kernel(w_ref, bias_ref, gain_ref, out_ref, bias_out, gain_out, ws, sems):
    channels = w_ref.shape[-1]
    copies = [pltpu.make_async_copy(w_ref.at[k // 3, k % 3], ws.at[k], sems.at[k]) for k in range(9)]
    for copy in copies:
        copy.start()
    for row, out in ((bias_ref, bias_out), (gain_ref, gain_out)):
        out[...] = jnp.transpose(jnp.broadcast_to(row[...], (8, channels)), (1, 0))[:, :1]
    for k, copy in enumerate(copies):
        copy.wait()
        for c in range(3):
            out_ref[k % 3, :, pl.ds((k // 3 * 3 + c) * channels, channels)] = jnp.transpose(ws[k, c], (1, 0))


def turned_weights(weight, bias, gain):
    channels = weight.shape[-1]
    return pl.pallas_call(
        turn_kernel,
        out_shape=(
            jax.ShapeDtypeStruct((3, channels, 9 * channels), BF16),
            jax.ShapeDtypeStruct((channels, 1), F32),
            jax.ShapeDtypeStruct((channels, 1), F32),
        ),
        in_specs=[ANY, VMEM, VMEM],
        out_specs=(VMEM, VMEM, VMEM),
        scratch_shapes=[pltpu.VMEM((9, 3, channels, channels), BF16), pltpu.SemaphoreType.DMA((9,))],
        compiler_params=pltpu.CompilerParams(vmem_limit_bytes=VMEM_BYTES),
        cost_estimate=pl.CostEstimate(flops=0, bytes_accessed=4 * weight.size, transcendentals=0),
    )(weight, bias, gain)


def layer_kernel(cases, rows_in, own, cols, block, height, n_in, place_ref, w_ref, bias_ref, gain_ref, *refs):
    ins = refs[:n_in]
    out_ref, acts_ref, next_ref = refs[n_in:n_in + 3]
    xs, buf, total, sems = refs[n_in + 6:]
    channels = xs.shape[0]
    row = block * cols
    rows_out = rows_in - 2
    lanes_in, lanes_out = rows_in * row, rows_out * row
    segment, slab = place_ref[0], place_ref[1]
    next_ref[0], next_ref[1] = segment, slab

    def slot(a, c):
        return (3 * a + c) * channels

    def source(part):
        at, index = part[0], part[1]
        return ins[at] if index is None else ins[at].at[index]

    active = functools.reduce(jnp.logical_or, [segment == g for g, _, _ in cases])
    for g, x_parts, before in cases:
        @pl.when(segment == g)
        def _():
            copies = []
            for parts, target in ((x_parts, xs), (before, buf.at[pl.ds(slot(0, 1), channels)])):
                at = 0
                for part in parts:
                    src = source(part)
                    width = part[3] * row
                    copies.append(pltpu.make_async_copy(
                        src.at[:, pl.ds(part[2] * row, width)], target.at[:, pl.ds(at, width)],
                        sems.at[len(copies)]))
                    at += width
            for c in copies:
                c.start()
            for c in copies:
                c.wait()

    @pl.when(active)
    def _():
        def squares(i, acc):
            v = xs[pl.ds(pl.multiple_of(i * CHUNK, CHUNK), CHUNK), :].astype(F32)
            v = v * v
            for k in range(0, CHUNK, 8):
                acc = acc + v[k:k + 8]
            return acc

        acc = lax.fori_loop(0, channels // CHUNK, squares, jnp.zeros((8, lanes_in), F32))
        scale = lax.rsqrt(jnp.sum(acc, axis=0, keepdims=True) * (1.0 / channels) + 1e-06)
        lane = lax.broadcasted_iota(jnp.int32, (CHUNK, row), 1)
        col = lax.rem(lane, cols)
        first, last = col == 0, col == cols - 1
        head = lane < row - cols
        zero = jnp.zeros((), BF16)

        def spread(i, _):
            at = pl.multiple_of(i * CHUNK, CHUNK)
            gain = gain_ref[pl.ds(at, CHUNK), :]
            here = [pl.ds(r * row, row) for r in range(rows_in)]
            values = [xs[pl.ds(at, CHUNK), h].astype(F32) for h in here]
            olds = [buf[pl.ds(slot(0, 1) + at, CHUNK), h] for h in here]
            results = []
            for r in range(rows_in):
                g = values[r] * scale[:, r * row:(r + 1) * row] * gain
                new = (0.5 * g * (1.0 + jnp.tanh(0.5 * g))).astype(BF16)
                mixed = pltpu.roll(jnp.where(head, new, olds[r]), cols, 1)
                for a, v in enumerate((olds[r], mixed, new)):
                    results.append((a, 0, r, jnp.where(first, zero, pltpu.roll(v, 1, 1))))
                    results.append((a, 2, r, jnp.where(last, zero, pltpu.roll(v, row - 1, 1))))
                    if a:
                        results.append((a, 1, r, v))
            for a, c, r, v in results:
                buf[pl.ds(slot(a, c) + at, CHUNK), here[r]] = v
            return 0

        lax.fori_loop(0, channels // CHUNK, spread, 0)
        acts_done = pltpu.make_async_copy(buf.at[pl.ds(slot(2, 1), channels)], acts_ref, sems.at[0])
        acts_done.start()
        step = 2 * row

        def taps(n, _):
            at = pl.multiple_of(n * step, step)
            part = None
            for b in range(3):
                tap = jnp.dot(w_ref[b], buf[:, pl.ds(at + b * row, step)], preferred_element_type=F32)
                part = tap if part is None else part + tap
            total[:, pl.ds(at, step)] = part
            return 0

        lax.fori_loop(0, lanes_out // step, taps, 0)
        top = slab * own - (rows_out - own) // 2

        def finish(i, _):
            at = pl.multiple_of(i * CHUNK, CHUNK)
            bias = bias_ref[pl.ds(at, CHUNK), :]
            sums = []
            for r in range(rows_out):
                value = xs[pl.ds(at, CHUNK), pl.ds((r + 1) * row, row)].astype(F32)
                value = value + (total[pl.ds(at, CHUNK), pl.ds(r * row, row)] + bias)
                inside = jnp.logical_and(top + r >= 0, top + r < height)
                sums.append(jnp.where(inside, value, 0.0).astype(BF16))
            for r in range(rows_out):
                xs[pl.ds(at, CHUNK), pl.ds(r * row, row)] = sums[r]
            return 0

        lax.fori_loop(0, channels // CHUNK, finish, 0)
        out_done = pltpu.make_async_copy(xs.at[:, pl.ds(0, lanes_out)], out_ref, sems.at[1])
        out_done.start()
        acts_done.wait()
        out_done.wait()


def layer_call(cases, rows_in, own, cols, block, height, fixed, ins):
    place, weight, bias, gain = fixed
    channels = weight.shape[1]
    row = block * cols
    return pl.pallas_call(
        functools.partial(layer_kernel, cases, rows_in, own, cols, block, height, len(ins)),
        out_shape=(
            jax.ShapeDtypeStruct((channels, (rows_in - 2) * row), BF16),
            jax.ShapeDtypeStruct((channels, rows_in * row), BF16),
            jax.ShapeDtypeStruct(place.shape, place.dtype),
            jax.ShapeDtypeStruct(weight.shape, weight.dtype),
            jax.ShapeDtypeStruct(bias.shape, bias.dtype),
            jax.ShapeDtypeStruct(gain.shape, gain.dtype),
        ),
        in_specs=[SMEM, VMEM, VMEM, VMEM] + [ANY] * len(ins),
        out_specs=(ANY, ANY, SMEM, VMEM, VMEM, VMEM),
        input_output_aliases={1: 3, 2: 4, 3: 5},
        scratch_shapes=[
            pltpu.VMEM((channels, rows_in * row), BF16),
            pltpu.VMEM((9 * channels, rows_in * row), BF16),
            pltpu.VMEM((channels, (rows_in - 2) * row), F32),
            pltpu.SemaphoreType.DMA((8,)),
        ],
        compiler_params=pltpu.CompilerParams(vmem_limit_bytes=VMEM_BYTES),
        cost_estimate=pl.CostEstimate(
            flops=2 * (rows_in - 2) * row * 27 * channels * channels, bytes_accessed=0, transcendentals=0),
    )(place, weight, bias, gain, *ins)


def local(segments, slabs, video_in, cache_in, conv_weight, conv_bias, norm_gain):
    frames, own, cols, channels = video_in.shape
    height = own * slabs
    segment = lax.axis_index("segment")
    slab = lax.axis_index("slab")
    axes = ("segment", "slab")
    block = frames // segments
    row = block * cols
    blocks = frames // block
    place = jnp.stack([segment, slab]).astype(jnp.int32)
    evens = range(0, segments, 2)
    odds = range(1, segments, 2)

    def moved(value, pairs, step):
        return lax.ppermute(value, axes, [
            (a * slabs + s, b * slabs + s + step) for a, b in pairs for s in range(slabs) if 0 <= s + step < slabs])

    def around(value, pairs, rows):
        above = moved(value[..., (own - rows) * row:], pairs, 1)
        below = moved(value[..., :rows * row], pairs, -1)
        return above, below

    def lanes(value):
        value = value.reshape(-1, block, own, cols, channels)
        return value.transpose(0, 4, 2, 1, 3).reshape(-1, channels, own * row)

    first = lanes(jnp.concatenate([cache_in[0], video_in[:block]], axis=0))
    first_above, first_below = around(first, [(g, g) for g in evens], 2)
    later, first_above, first_below = lax.optimization_barrier((lanes(video_in[block:]), first_above, first_below))
    fixed = (place,) + tuple(turned_weights(conv_weight[0], conv_bias, norm_gain))
    odd_above, odd_below = around(first[0], [(g, g) for g in odds], 1)
    later_above, later_below = around(later, [(0, 0)], 2)

    call = functools.partial(layer_call, own=own, cols=cols, block=block, height=height)
    across = [(g, g + 1) for g in evens]
    hop = [(g, g + 1) for g in odds if g + 1 < segments]
    planes = segments // 2
    arrived, done = [], []
    even_acts = odd_acts = None
    even_cache, odd_cache = [None] * planes, [None] * planes
    ticks = blocks + LAG * (planes - 1)
    for tick in range(ticks):
        busy = [p for p in range(planes) if 0 <= tick - LAG * p < blocks]
        ins = [first, first_above, first_below]
        old = [(1, 0, 0, 2), (0, 0, 0, own), (2, 0, 0, 2)]
        if tick:
            ins.append(even_acts)
            kept = [(3, None, 0, own + 4)]
        cases = []
        for p in busy:
            b = tick - LAG * p
            if p == 0 and b == 0:
                parts = [(1, 1, 0, 2), (0, 1, 0, own), (2, 1, 0, 2)]
            else:
                n = len(ins)
                if p == 0:
                    ins += [later, later_above, later_below]
                    parts = [(n + 1, b - 1, 0, 2), (n, b - 1, 0, own), (n + 2, b - 1, 0, 2)]
                else:
                    ins += list(arrived[b])
                    parts = [(n + 1, None, 0, 2), (n, None, 0, own), (n + 2, None, 0, 2)]
            cases.append((2 * p, parts, old if b == 0 else kept))
        if tick == 0:
            ins += [odd_above, odd_below]
        if tick == ticks - 1:
            ins.append(done[-2])
        out, even_acts, *fixed = call(cases, own + 4, fixed=fixed, ins=ins)
        if 0 < tick <= blocks:
            out, *arrived[tick - 1] = lax.optimization_barrier((out, *arrived[tick - 1]))
        crossed = moved(out, across, 0)

        ins = [crossed, first, odd_above, odd_below]
        old = [(2, None, 0, 1), (1, 0, 0, own), (3, None, 0, 1)]
        if tick:
            ins.append(odd_acts)
        if tick == 0:
            ins += [later_above, later_below]
        if tick >= ticks - 2:
            ins.append(done[0] if tick < ticks - 1 else done[-1])
        cases = [(2 * p + 1, [(0, None, 0, own + 2)], old if tick == LAG * p else [(4, None, 0, own + 2)]) for p in busy]
        out, odd_acts, *fixed = call(cases, own + 2, fixed=fixed, ins=ins)
        if tick < blocks:
            arrived.append((moved(out, hop, 0), moved(out[:, (own - 2) * row:], hop, 1), moved(out[:, :2 * row], hop, -1)))
        b = tick - LAG * (planes - 1)
        if 0 <= b < blocks:
            done.append(out if b == segments - 1 else moved(out, [(segments - 1, b)], 0))
        for p in busy:
            if tick - LAG * p == blocks - 1:
                even_cache[p] = even_acts[:, 2 * row:(2 + own) * row]
                odd_cache[p] = odd_acts[:, row:(1 + own) * row]

    def natural(value):
        return value.reshape(channels, own, block, cols).transpose(2, 1, 3, 0)

    result = done[-1]
    for b in range(blocks - 1):
        result = jnp.where(segment == b, done[b], result)
    cache = odd_cache[-1]
    for p in range(planes):
        cache = jnp.where(segment == 2 * p, even_cache[p], cache)
        cache = jnp.where(segment == 2 * p + 1, odd_cache[p], cache)
    return natural(result), natural(cache)[None]


def solution(mesh):
    segments, slabs = mesh.shape["segment"], mesh.shape["slab"]
    return jax.shard_map(
        functools.partial(local, segments, slabs),
        mesh=mesh,
        in_specs=(
            P(None, "slab", None, None),
            P("segment", None, "slab", None, None),
            P("segment", None, None, None, None, None),
            P("segment", None),
            P("segment", None),
        ),
        out_specs=(P("segment", "slab", None, None), P("segment", None, "slab", None, None)),
        check_vma=False,
    )
```

```python
import functools
import jax
import jax.numpy as jnp
from jax import lax
from jax.experimental import pallas as pl
from jax.experimental.pallas import tpu as pltpu
from jax.sharding import PartitionSpec as P

LAG = 2
CHUNK = 128
VMEM_BYTES = 24 * 2**20
F32 = jnp.float32
BF16 = jnp.bfloat16
ANY = pl.BlockSpec(memory_space=pl.ANY)
VMEM = pl.BlockSpec(memory_space=pltpu.VMEM)
SMEM = pl.BlockSpec(memory_space=pltpu.SMEM)


def turn_kernel(w_ref, bias_ref, gain_ref, _, out_ref, bias_out, gain_out, ws, rows, sems):
    channels = w_ref.shape[-1]
    copies = [pltpu.make_async_copy(w_ref.at[k // 3, k % 3], ws.at[k], sems.at[k]) for k in range(9)]
    vectors = [pltpu.make_async_copy(ref, rows.at[pl.ds(k, 1)], sems.at[9 + k])
               for k, ref in enumerate((bias_ref, gain_ref))]
    for copy in vectors + copies:
        copy.start()
    for k, copy in enumerate(copies):
        copy.wait()
        for c in range(3):
            out_ref[k % 3, :, pl.ds((k // 3 * 3 + c) * channels, channels)] = jnp.transpose(ws[k, c], (1, 0))
    for copy in vectors:
        copy.wait()
    turned = jnp.transpose(rows[...], (1, 0))
    bias_out[...] = turned[:, 0:1]
    gain_out[...] = turned[:, 1:2]


def turned_weights(weight, bias, gain, ahead):
    channels = weight.shape[-1]
    return pl.pallas_call(
        turn_kernel,
        out_shape=(
            jax.ShapeDtypeStruct((3, channels, 9 * channels), BF16),
            jax.ShapeDtypeStruct((channels, 1), F32),
            jax.ShapeDtypeStruct((channels, 1), F32),
        ),
        in_specs=[pl.BlockSpec(memory_space=pltpu.HBM)] * 3 + [ANY],
        out_specs=(VMEM, VMEM, VMEM),
        scratch_shapes=[
            pltpu.VMEM((9, 3, channels, channels), BF16),
            pltpu.VMEM((8, channels), F32),
            pltpu.SemaphoreType.DMA((11,)),
        ],
        compiler_params=pltpu.CompilerParams(vmem_limit_bytes=VMEM_BYTES),
        cost_estimate=pl.CostEstimate(flops=0, bytes_accessed=4 * weight.size, transcendentals=0),
    )(*(pltpu.with_memory_space_constraint(v, pltpu.HBM) for v in (weight, bias, gain)), ahead)


def layer_kernel(cases, rows_in, own, cols, block, height, n_in, place_ref, w_ref, bias_ref, gain_ref, *refs):
    ins = refs[:n_in]
    out_ref, acts_ref, next_ref = refs[n_in:n_in + 3]
    xs, buf, total, sems = refs[n_in + 6:]
    channels = xs.shape[0]
    row = block * cols
    rows_out = rows_in - 2
    lanes_in, lanes_out = rows_in * row, rows_out * row
    segment, slab = place_ref[0], place_ref[1]
    next_ref[0], next_ref[1] = segment, slab

    def slot(a, c):
        return (3 * a + c) * channels

    def source(part):
        at, index = part[0], part[1]
        return ins[at] if index is None else ins[at].at[index]

    active = functools.reduce(jnp.logical_or, [segment == g for g, _, _ in cases])
    for g, x_parts, before in cases:
        @pl.when(segment == g)
        def _():
            copies = []
            for parts, target in ((x_parts, xs), (before, buf.at[pl.ds(slot(0, 1), channels)])):
                at = 0
                for part in parts:
                    src = source(part)
                    width = part[3] * row
                    copies.append(pltpu.make_async_copy(
                        src.at[:, pl.ds(part[2] * row, width)], target.at[:, pl.ds(at, width)],
                        sems.at[len(copies)]))
                    at += width
            for c in copies:
                c.start()
            for c in copies:
                c.wait()

    @pl.when(active)
    def _():
        def squares(i, acc):
            v = xs[pl.ds(pl.multiple_of(i * CHUNK, CHUNK), CHUNK), :].astype(F32)
            v = v * v
            for k in range(0, CHUNK, 8):
                acc = acc + v[k:k + 8]
            return acc

        acc = lax.fori_loop(0, channels // CHUNK, squares, jnp.zeros((8, lanes_in), F32))
        scale = lax.rsqrt(jnp.sum(acc, axis=0, keepdims=True) * (1.0 / channels) + 1e-06)
        lane = lax.broadcasted_iota(jnp.int32, (CHUNK, row), 1)
        col = lax.rem(lane, cols)
        first, last = col == 0, col == cols - 1
        head = lane < row - cols
        zero = jnp.zeros((), BF16)

        def spread(i, _):
            at = pl.multiple_of(i * CHUNK, CHUNK)
            gain = gain_ref[pl.ds(at, CHUNK), :]
            here = [pl.ds(r * row, row) for r in range(rows_in)]
            values = [xs[pl.ds(at, CHUNK), h].astype(F32) for h in here]
            olds = [buf[pl.ds(slot(0, 1) + at, CHUNK), h] for h in here]
            results = []
            for r in range(rows_in):
                g = values[r] * scale[:, r * row:(r + 1) * row] * gain
                new = (0.5 * g * (1.0 + jnp.tanh(0.5 * g))).astype(BF16)
                mixed = pltpu.roll(jnp.where(head, new, olds[r]), cols, 1)
                for a, v in enumerate((olds[r], mixed, new)):
                    results.append((a, 0, r, jnp.where(first, zero, pltpu.roll(v, 1, 1))))
                    results.append((a, 2, r, jnp.where(last, zero, pltpu.roll(v, row - 1, 1))))
                    if a:
                        results.append((a, 1, r, v))
            for a, c, r, v in results:
                buf[pl.ds(slot(a, c) + at, CHUNK), here[r]] = v
            return 0

        lax.fori_loop(0, channels // CHUNK, spread, 0)
        acts_done = pltpu.make_async_copy(buf.at[pl.ds(slot(2, 1), channels)], acts_ref, sems.at[0])
        acts_done.start()
        step = 2 * row
        top = slab * own - (rows_out - own) // 2

        def taps(n, _):
            at = pl.multiple_of(n * step, step)
            part = xs[:, pl.ds(at + row, step)].astype(F32) + bias_ref[...]
            for b in range(3):
                part = part + jnp.dot(w_ref[b], buf[:, pl.ds(at + b * row, step)], preferred_element_type=F32)
            line = top + 2 * n + lax.broadcasted_iota(jnp.int32, (1, step), 1) // row
            total[:, pl.ds(at, step)] = jnp.where(
                jnp.logical_and(line >= 0, line < height), part, 0.0).astype(BF16)
            return 0

        lax.fori_loop(0, lanes_out // step, taps, 0)
        out_done = pltpu.make_async_copy(total, out_ref, sems.at[1])
        out_done.start()
        acts_done.wait()
        out_done.wait()


def layer_call(cases, rows_in, own, cols, block, height, fixed, ins):
    place, weight, bias, gain = fixed
    channels = weight.shape[1]
    row = block * cols
    return pl.pallas_call(
        functools.partial(layer_kernel, cases, rows_in, own, cols, block, height, len(ins)),
        out_shape=(
            jax.ShapeDtypeStruct((channels, (rows_in - 2) * row), BF16),
            jax.ShapeDtypeStruct((channels, rows_in * row), BF16),
            jax.ShapeDtypeStruct(place.shape, place.dtype),
            jax.ShapeDtypeStruct(weight.shape, weight.dtype),
            jax.ShapeDtypeStruct(bias.shape, bias.dtype),
            jax.ShapeDtypeStruct(gain.shape, gain.dtype),
        ),
        in_specs=[SMEM, VMEM, VMEM, VMEM] + [ANY] * len(ins),
        out_specs=(ANY, ANY, SMEM, VMEM, VMEM, VMEM),
        input_output_aliases={1: 3, 2: 4, 3: 5},
        scratch_shapes=[
            pltpu.VMEM((channels, rows_in * row), BF16),
            pltpu.VMEM((9 * channels, rows_in * row), BF16),
            pltpu.VMEM((channels, (rows_in - 2) * row), BF16),
            pltpu.SemaphoreType.DMA((8,)),
        ],
        compiler_params=pltpu.CompilerParams(vmem_limit_bytes=VMEM_BYTES),
        cost_estimate=pl.CostEstimate(
            flops=2 * (rows_in - 2) * row * 27 * channels * channels, bytes_accessed=0, transcendentals=0),
    )(place, weight, bias, gain, *ins)


def local(segments, slabs, video_in, cache_in, conv_weight, conv_bias, norm_gain):
    frames, own, cols, channels = video_in.shape
    height = own * slabs
    segment = lax.axis_index("segment")
    slab = lax.axis_index("slab")
    axes = ("segment", "slab")
    block = frames // segments
    row = block * cols
    blocks = frames // block
    place = jnp.stack([segment, slab]).astype(jnp.int32)
    evens = range(0, segments, 2)
    odds = range(1, segments, 2)

    def moved(value, pairs, step):
        return lax.ppermute(value, axes, [
            (a * slabs + s, b * slabs + s + step) for a, b in pairs for s in range(slabs) if 0 <= s + step < slabs])

    def around(value, pairs, rows):
        above = moved(value[..., (own - rows) * row:], pairs, 1)
        below = moved(value[..., :rows * row], pairs, -1)
        return above, below

    def lanes(value):
        value = value.reshape(-1, block, own, cols, channels)
        return value.transpose(0, 4, 2, 1, 3).reshape(-1, channels, own * row)

    first = lanes(jnp.concatenate([cache_in[0], video_in[:block]], axis=0))
    first_above, first_below = around(first, [(g, g) for g in evens], 2)
    odd_above, odd_below = around(first[0], [(g, g) for g in odds], 1)
    later, place, weight = lax.optimization_barrier((lanes(video_in[block:]), place, conv_weight[0]))
    weight, bias, gain = turned_weights(weight, conv_bias, norm_gain, later)
    later, weight = lax.optimization_barrier((later, weight))
    later_above, later_below = around(later, [(0, 0)], 2)
    fixed = (place, weight, bias, gain)

    call = functools.partial(layer_call, own=own, cols=cols, block=block, height=height)
    across = [(g, g ^ 1) for g in range(segments)]
    hop = [(g, g + 1) for g in odds if g + 1 < segments]
    planes = segments // 2
    arrived, done = [], []
    even_acts = odd_acts = None
    even_cache, odd_cache = [None] * planes, [None] * planes
    ticks = blocks + LAG * (planes - 1)
    for tick in range(ticks):
        busy = [p for p in range(planes) if 0 <= tick - LAG * p < blocks]
        ins = [first, first_above, first_below]
        old = [(1, 0, 0, 2), (0, 0, 0, own), (2, 0, 0, 2)]
        if tick:
            ins.append(even_acts)
            kept = [(3, None, 0, own + 4)]
        cases = []
        for p in busy:
            b = tick - LAG * p
            if p == 0 and b == 0:
                parts = [(1, 1, 0, 2), (0, 1, 0, own), (2, 1, 0, 2)]
            else:
                n = len(ins)
                if p == 0:
                    ins += [later, later_above, later_below]
                    parts = [(n + 1, b - 1, 0, 2), (n, b - 1, 0, own), (n + 2, b - 1, 0, 2)]
                else:
                    ins += list(arrived[b])
                    parts = [(n + 1, None, 0, 2), (n, None, 0, own), (n + 2, None, 0, 2)]
            cases.append((2 * p, parts, old if b == 0 else kept))
        if tick == 0:
            ins += [odd_above, odd_below]
        if tick == ticks - 1:
            ins.append(done[-2])
        out, even_acts, *fixed = call(cases, own + 4, fixed=fixed, ins=ins)
        if 0 < tick <= blocks:
            out, *arrived[tick - 1] = lax.optimization_barrier((out, *arrived[tick - 1]))
        crossed = moved(out, across, 0)

        ins = [crossed, first, odd_above, odd_below]
        old = [(2, None, 0, 1), (1, 0, 0, own), (3, None, 0, 1)]
        if tick:
            ins.append(odd_acts)
        if tick == 0:
            ins += [later_above, later_below]
        if tick >= ticks - 2:
            ins.append(done[0] if tick < ticks - 1 else done[-1])
        cases = [(2 * p + 1, [(0, None, 0, own + 2)], old if tick == LAG * p else [(4, None, 0, own + 2)]) for p in busy]
        out, odd_acts, *fixed = call(cases, own + 2, fixed=fixed, ins=ins)
        if tick < blocks:
            arrived.append((moved(out, hop, 0), moved(out[:, (own - 2) * row:], hop, 1), moved(out[:, :2 * row], hop, -1)))
        b = tick - LAG * (planes - 1)
        if 0 <= b < blocks:
            done.append(out if b == segments - 1 else moved(out, [(segments - 1, b)], 0))
        for p in busy:
            if tick - LAG * p == blocks - 1:
                even_cache[p] = even_acts[:, 2 * row:(2 + own) * row]
                odd_cache[p] = odd_acts[:, row:(1 + own) * row]

    def natural(value):
        return value.reshape(channels, own, block, cols).transpose(2, 1, 3, 0)

    result, segment = lax.optimization_barrier((done[-1], segment))
    for b in range(blocks - 1):
        result = jnp.where(segment == b, done[b], result)
    cache = odd_cache[-1]
    for p in range(planes):
        cache = jnp.where(segment == 2 * p, even_cache[p], cache)
        cache = jnp.where(segment == 2 * p + 1, odd_cache[p], cache)
    return natural(result), natural(cache)[None]


def solution(mesh):
    segments, slabs = mesh.shape["segment"], mesh.shape["slab"]
    return jax.shard_map(
        functools.partial(local, segments, slabs),
        mesh=mesh,
        in_specs=(
            P(None, "slab", None, None),
            P("segment", None, "slab", None, None),
            P("segment", None, None, None, None, None),
            P("segment", None),
            P("segment", None),
        ),
        out_specs=(P("segment", "slab", None, None), P("segment", None, "slab", None, None)),
        check_vma=False,
    )
```

```python
import functools
import jax
import jax.numpy as jnp
from jax import lax
from jax.experimental import pallas as pl
from jax.experimental.pallas import tpu as pltpu
from jax.sharding import PartitionSpec as P

LAG = 2
CHUNK = 128
VMEM_BYTES = 24 * 2**20
F32 = jnp.float32
BF16 = jnp.bfloat16
ANY = pl.BlockSpec(memory_space=pl.ANY)
VMEM = pl.BlockSpec(memory_space=pltpu.VMEM)
SMEM = pl.BlockSpec(memory_space=pltpu.SMEM)


def turn_kernel(cuts, w_ref, bias_ref, gain_ref, later_ref, first_ref, out_ref, bias_out, gain_out, _, *refs):
    ws, rows, sems, cut_sems = refs[-4:]
    channels = w_ref.shape[-1]
    copies = [pltpu.make_async_copy(w_ref.at[k // 3, k % 3], ws.at[k], sems.at[k]) for k in range(9)]
    vectors = [pltpu.make_async_copy(ref, rows.at[pl.ds(k, 1)], sems.at[9 + k])
               for k, ref in enumerate((bias_ref, gain_ref))]
    parts = [pltpu.make_async_copy(first_ref.at[pl.ds(0, n), :, pl.ds(at, width)], refs[k], cut_sems.at[k])
             for k, (n, at, width) in enumerate(cuts)]
    for copy in vectors + copies + parts:
        copy.start()
    for k, copy in enumerate(copies):
        copy.wait()
        for c in range(3):
            out_ref[k % 3, :, pl.ds((k // 3 * 3 + c) * channels, channels)] = jnp.transpose(ws[k, c], (1, 0))
    for copy in vectors + parts:
        copy.wait()
    turned = jnp.transpose(rows[...], (1, 0))
    bias_out[...] = turned[:, 0:1]
    gain_out[...] = turned[:, 1:2]


def turned_weights(weight, bias, gain, later, first, cuts):
    channels = weight.shape[-1]
    return pl.pallas_call(
        functools.partial(turn_kernel, cuts),
        out_shape=(
            jax.ShapeDtypeStruct((3, channels, 9 * channels), BF16),
            jax.ShapeDtypeStruct((channels, 1), F32),
            jax.ShapeDtypeStruct((channels, 1), F32),
            jax.ShapeDtypeStruct(later.shape, later.dtype),
            *(jax.ShapeDtypeStruct((n, channels, width), BF16) for n, _, width in cuts),
        ),
        in_specs=[pl.BlockSpec(memory_space=pltpu.HBM)] * 3 + [ANY] * 2,
        out_specs=(VMEM, VMEM, VMEM, ANY) + (ANY,) * len(cuts),
        input_output_aliases={3: 3},
        scratch_shapes=[
            pltpu.VMEM((9, 3, channels, channels), BF16),
            pltpu.VMEM((8, channels), F32),
            pltpu.SemaphoreType.DMA((11,)),
            pltpu.SemaphoreType.DMA((len(cuts),)),
        ],
        compiler_params=pltpu.CompilerParams(vmem_limit_bytes=VMEM_BYTES),
        cost_estimate=pl.CostEstimate(flops=0, bytes_accessed=4 * weight.size, transcendentals=0),
    )(*(pltpu.with_memory_space_constraint(v, pltpu.HBM) for v in (weight, bias, gain)), later, first)


def layer_kernel(cases, rows_in, own, cols, block, height, n_in, place_ref, w_ref, bias_ref, gain_ref, *refs):
    ins = refs[:n_in]
    out_ref, acts_ref, next_ref = refs[n_in:n_in + 3]
    xs, buf, total, sems = refs[n_in + 6:]
    channels = xs.shape[0]
    row = block * cols
    rows_out = rows_in - 2
    lanes_in, lanes_out = rows_in * row, rows_out * row
    segment, slab = place_ref[0], place_ref[1]
    next_ref[0], next_ref[1] = segment, slab

    def slot(a, c):
        return (3 * a + c) * channels

    def source(part):
        at, index = part[0], part[1]
        return ins[at] if index is None else ins[at].at[index]

    active = functools.reduce(jnp.logical_or, [segment == g for g, _, _ in cases])
    for g, x_parts, before in cases:
        @pl.when(segment == g)
        def _():
            copies = []
            for parts, target in ((x_parts, xs), (before, buf.at[pl.ds(slot(0, 1), channels)])):
                at = 0
                for part in parts:
                    src = source(part)
                    width = part[3] * row
                    copies.append(pltpu.make_async_copy(
                        src.at[:, pl.ds(part[2] * row, width)], target.at[:, pl.ds(at, width)],
                        sems.at[len(copies)]))
                    at += width
            for c in copies:
                c.start()
            for c in copies:
                c.wait()

    @pl.when(active)
    def _():
        def squares(i, acc):
            v = xs[pl.ds(pl.multiple_of(i * CHUNK, CHUNK), CHUNK), :].astype(F32)
            v = v * v
            for k in range(0, CHUNK, 8):
                acc = acc + v[k:k + 8]
            return acc

        acc = lax.fori_loop(0, channels // CHUNK, squares, jnp.zeros((8, lanes_in), F32))
        scale = lax.rsqrt(jnp.sum(acc, axis=0, keepdims=True) * (1.0 / channels) + 1e-06)
        lane = lax.broadcasted_iota(jnp.int32, (CHUNK, row), 1)
        col = lax.rem(lane, cols)
        first, last = col == 0, col == cols - 1
        head = lane < row - cols
        zero = jnp.zeros((), BF16)

        def spread(i, _):
            at = pl.multiple_of(i * CHUNK, CHUNK)
            gain = gain_ref[pl.ds(at, CHUNK), :]
            here = [pl.ds(r * row, row) for r in range(rows_in)]
            values = [xs[pl.ds(at, CHUNK), h].astype(F32) for h in here]
            olds = [buf[pl.ds(slot(0, 1) + at, CHUNK), h] for h in here]
            results = []
            for r in range(rows_in):
                g = values[r] * scale[:, r * row:(r + 1) * row] * gain
                new = (0.5 * g * (1.0 + jnp.tanh(0.5 * g))).astype(BF16)
                mixed = pltpu.roll(jnp.where(head, new, olds[r]), cols, 1)
                for a, v in enumerate((olds[r], mixed, new)):
                    results.append((a, 0, r, jnp.where(first, zero, pltpu.roll(v, 1, 1))))
                    results.append((a, 2, r, jnp.where(last, zero, pltpu.roll(v, row - 1, 1))))
                    if a:
                        results.append((a, 1, r, v))
            for a, c, r, v in results:
                buf[pl.ds(slot(a, c) + at, CHUNK), here[r]] = v
            return 0

        lax.fori_loop(0, channels // CHUNK, spread, 0)
        acts_done = pltpu.make_async_copy(buf.at[pl.ds(slot(2, 1), channels)], acts_ref, sems.at[0])
        acts_done.start()
        step = 2 * row
        top = slab * own - (rows_out - own) // 2

        def taps(n, _):
            at = pl.multiple_of(n * step, step)
            part = xs[:, pl.ds(at + row, step)].astype(F32) + bias_ref[...]
            part = lax.fori_loop(0, 3, lambda b, part: part + jnp.dot(
                w_ref[b], buf[:, pl.ds(pl.multiple_of(at + b * row, row), step)], preferred_element_type=F32), part)
            line = top + 2 * n + lax.broadcasted_iota(jnp.int32, (1, step), 1) // row
            total[:, pl.ds(at, step)] = jnp.where(
                jnp.logical_and(line >= 0, line < height), part, 0.0).astype(BF16)
            return 0

        lax.fori_loop(0, lanes_out // step, taps, 0)
        out_done = pltpu.make_async_copy(total, out_ref, sems.at[1])
        out_done.start()
        acts_done.wait()
        out_done.wait()


def layer_call(cases, rows_in, own, cols, block, height, fixed, ins):
    place, weight, bias, gain = fixed
    channels = weight.shape[1]
    row = block * cols
    return pl.pallas_call(
        functools.partial(layer_kernel, cases, rows_in, own, cols, block, height, len(ins)),
        out_shape=(
            jax.ShapeDtypeStruct((channels, (rows_in - 2) * row), BF16),
            jax.ShapeDtypeStruct((channels, rows_in * row), BF16),
            jax.ShapeDtypeStruct(place.shape, place.dtype),
            jax.ShapeDtypeStruct(weight.shape, weight.dtype),
            jax.ShapeDtypeStruct(bias.shape, bias.dtype),
            jax.ShapeDtypeStruct(gain.shape, gain.dtype),
        ),
        in_specs=[SMEM, VMEM, VMEM, VMEM] + [ANY] * len(ins),
        out_specs=(ANY, ANY, SMEM, VMEM, VMEM, VMEM),
        input_output_aliases={1: 3, 2: 4, 3: 5},
        scratch_shapes=[
            pltpu.VMEM((channels, rows_in * row), BF16),
            pltpu.VMEM((9 * channels, rows_in * row), BF16),
            pltpu.VMEM((channels, (rows_in - 2) * row), BF16),
            pltpu.SemaphoreType.DMA((8,)),
        ],
        compiler_params=pltpu.CompilerParams(vmem_limit_bytes=VMEM_BYTES),
        cost_estimate=pl.CostEstimate(
            flops=2 * (rows_in - 2) * row * 27 * channels * channels, bytes_accessed=0, transcendentals=0),
    )(place, weight, bias, gain, *ins)


def local(segments, slabs, video_in, cache_in, conv_weight, conv_bias, norm_gain):
    frames, own, cols, channels = video_in.shape
    height = own * slabs
    segment = lax.axis_index("segment")
    slab = lax.axis_index("slab")
    axes = ("segment", "slab")
    block = frames // segments
    row = block * cols
    blocks = frames // block
    place = jnp.stack([segment, slab]).astype(jnp.int32)
    evens = range(0, segments, 2)
    odds = range(1, segments, 2)

    def moved(value, pairs, step):
        return lax.ppermute(value, axes, [
            (a * slabs + s, b * slabs + s + step) for a, b in pairs for s in range(slabs) if 0 <= s + step < slabs])

    def lanes(value):
        value = value.reshape(-1, block, own, cols, channels)
        return value.transpose(0, 4, 2, 1, 3).reshape(-1, channels, own * row)

    first = lanes(jnp.concatenate([cache_in[0], video_in[:block]], axis=0))
    first_below = moved(first[..., :2 * row], [(g, g) for g in evens], -1)
    place, weight = lax.optimization_barrier((place, conv_weight[0]))
    cuts = ((2, (own - 2) * row, 2 * row), (1, (own - 1) * row, row), (1, 0, row))
    weight, bias, gain, later, above, odd_last, odd_first = turned_weights(
        weight, conv_bias, norm_gain, lanes(video_in[block:]), first, cuts)
    first_above = moved(above, [(g, g) for g in evens], 1)
    odd_above = moved(odd_last, [(g, g) for g in odds], 1)
    odd_below = moved(odd_first, [(g, g) for g in odds], -1)
    later_below = moved(later[..., :2 * row], [(0, 0)], -1)
    fixed = (place, weight, bias, gain)

    call = functools.partial(layer_call, own=own, cols=cols, block=block, height=height)
    across = [(g, g ^ 1) for g in range(segments)]
    hop = [(g, g + 1) for g in odds if g + 1 < segments]
    planes = segments // 2
    arrived, done = [], []
    even_acts = odd_acts = None
    even_cache, odd_cache = [None] * planes, [None] * planes
    ticks = blocks + LAG * (planes - 1)
    for tick in range(ticks):
        busy = [p for p in range(planes) if 0 <= tick - LAG * p < blocks]
        ins = [first, first_above, first_below]
        old = [(1, 0, 0, 2), (0, 0, 0, own), (2, 0, 0, 2)]
        if tick:
            ins.append(even_acts)
            kept = [(3, None, 0, own + 4)]
        cases = []
        for p in busy:
            b = tick - LAG * p
            if p == 0 and b == 0:
                parts = [(1, 1, 0, 2), (0, 1, 0, own), (2, 1, 0, 2)]
            else:
                n = len(ins)
                if p == 0:
                    ins += [later, later_above, later_below]
                    parts = [(n + 1, b - 1, 0, 2), (n, b - 1, 0, own), (n + 2, b - 1, 0, 2)]
                else:
                    ins += list(arrived[b])
                    parts = [(n + 1, None, 0, 2), (n, None, 0, own), (n + 2, None, 0, 2)]
            cases.append((2 * p, parts, old if b == 0 else kept))
        if tick == 0:
            ins += [odd_above, odd_below]
        if tick == ticks - 1:
            ins.append(done[-2])
        out, even_acts, *fixed = call(cases, own + 4, fixed=fixed, ins=ins)
        if 0 < tick <= blocks:
            out, *arrived[tick - 1] = lax.optimization_barrier((out, *arrived[tick - 1]))
        crossed = moved(out, across, 0)
        if tick == 0:
            crossed, sent = lax.optimization_barrier((crossed, later[..., (own - 2) * row:]))
            later_above = moved(sent, [(0, 0)], 1)

        ins = [crossed, first, odd_above, odd_below]
        old = [(2, 0, 0, 1), (1, 0, 0, own), (3, 0, 0, 1)]
        if tick:
            ins.append(odd_acts)
        if tick == 0:
            ins.append(later_below)
        if tick >= ticks - 2:
            ins.append(done[0] if tick < ticks - 1 else done[-1])
        cases = [(2 * p + 1, [(0, None, 0, own + 2)], old if tick == LAG * p else [(4, None, 0, own + 2)]) for p in busy]
        out, odd_acts, *fixed = call(cases, own + 2, fixed=fixed, ins=ins)
        if tick < blocks:
            arrived.append((moved(out, hop, 0), moved(out[:, (own - 2) * row:], hop, 1), moved(out[:, :2 * row], hop, -1)))
        b = tick - LAG * (planes - 1)
        if 0 <= b < blocks:
            done.append(out if b == segments - 1 else moved(out, [(segments - 1, b)], 0))
        for p in busy:
            if tick - LAG * p == blocks - 1:
                even_cache[p] = even_acts[:, 2 * row:(2 + own) * row]
                odd_cache[p] = odd_acts[:, row:(1 + own) * row]

    def natural(value):
        return value.reshape(channels, own, block, cols).transpose(2, 1, 3, 0)

    result, segment = lax.optimization_barrier((done[-1], segment))
    for b in range(blocks - 1):
        result = jnp.where(segment == b, done[b], result)
    cache = odd_cache[-1]
    for p in range(planes):
        cache = jnp.where(segment == 2 * p, even_cache[p], cache)
        cache = jnp.where(segment == 2 * p + 1, odd_cache[p], cache)
    return natural(result), natural(cache)[None]


def solution(mesh):
    segments, slabs = mesh.shape["segment"], mesh.shape["slab"]
    return jax.shard_map(
        functools.partial(local, segments, slabs),
        mesh=mesh,
        in_specs=(
            P(None, "slab", None, None),
            P("segment", None, "slab", None, None),
            P("segment", None, None, None, None, None),
            P("segment", None),
            P("segment", None),
        ),
        out_specs=(P("segment", "slab", None, None), P("segment", None, "slab", None, None)),
        check_vma=False,
    )
```

```python
import functools
import jax
import jax.numpy as jnp
from jax import lax
from jax.experimental import pallas as pl
from jax.experimental.pallas import tpu as pltpu
from jax.sharding import PartitionSpec as P

LAG = 2
CHUNK = 128
VMEM_BYTES = 24 * 2**20
F32 = jnp.float32
BF16 = jnp.bfloat16
ANY = pl.BlockSpec(memory_space=pl.ANY)
VMEM = pl.BlockSpec(memory_space=pltpu.VMEM)
SMEM = pl.BlockSpec(memory_space=pltpu.SMEM)


def turn_kernel(cuts, w_ref, bias_ref, gain_ref, later_ref, first_ref, out_ref, bias_out, gain_out, _, *refs):
    ws, rows, sems, cut_sems = refs[-4:]
    channels = w_ref.shape[-1]
    copies = [pltpu.make_async_copy(w_ref.at[k // 3, k % 3], ws.at[k], sems.at[k]) for k in range(9)]
    vectors = [pltpu.make_async_copy(ref, rows.at[pl.ds(k, 1)], sems.at[9 + k])
               for k, ref in enumerate((bias_ref, gain_ref))]
    parts = [pltpu.make_async_copy(first_ref.at[pl.ds(0, n), :, pl.ds(at, width)], refs[k], cut_sems.at[k])
             for k, (n, at, width) in enumerate(cuts)]
    for copy in vectors + copies + parts:
        copy.start()
    for k, copy in enumerate(copies):
        copy.wait()
        for c in range(3):
            out_ref[k % 3, :, pl.ds((k // 3 * 3 + c) * channels, channels)] = jnp.transpose(ws[k, c], (1, 0))
    for copy in vectors + parts:
        copy.wait()
    turned = jnp.transpose(rows[...], (1, 0))
    bias_out[...] = turned[:, 0:1]
    gain_out[...] = turned[:, 1:2]


def turned_weights(weight, bias, gain, later, first, cuts):
    channels = weight.shape[-1]
    return pl.pallas_call(
        functools.partial(turn_kernel, cuts),
        out_shape=(
            jax.ShapeDtypeStruct((3, channels, 9 * channels), BF16),
            jax.ShapeDtypeStruct((channels, 1), F32),
            jax.ShapeDtypeStruct((channels, 1), F32),
            jax.ShapeDtypeStruct(later.shape, later.dtype),
            *(jax.ShapeDtypeStruct((n, channels, width), BF16) for n, _, width in cuts),
        ),
        in_specs=[pl.BlockSpec(memory_space=pltpu.HBM)] * 3 + [ANY] * 2,
        out_specs=(VMEM, VMEM, VMEM, ANY) + (ANY,) * len(cuts),
        input_output_aliases={3: 3},
        scratch_shapes=[
            pltpu.VMEM((9, 3, channels, channels), BF16),
            pltpu.VMEM((8, channels), F32),
            pltpu.SemaphoreType.DMA((11,)),
            pltpu.SemaphoreType.DMA((len(cuts),)),
        ],
        compiler_params=pltpu.CompilerParams(vmem_limit_bytes=VMEM_BYTES),
        cost_estimate=pl.CostEstimate(flops=0, bytes_accessed=4 * weight.size, transcendentals=0),
    )(*(pltpu.with_memory_space_constraint(v, pltpu.HBM) for v in (weight, bias, gain)), later, first)


def layer_kernel(cases, rows_in, own, cols, block, height, n_in, place_ref, w_ref, bias_ref, gain_ref, *refs):
    ins = refs[:n_in]
    out_ref, acts_ref = refs[n_in:n_in + 2]
    xs, buf, total, sems = refs[n_in + 5:]
    channels = xs.shape[0]
    row = block * cols
    rows_out = rows_in - 2
    lanes_in, lanes_out = rows_in * row, rows_out * row
    segment, slab = place_ref[0], place_ref[1]

    def slot(a, c):
        return (3 * a + c) * channels

    def source(part):
        at, index = part[0], part[1]
        return ins[at] if index is None else ins[at].at[index]

    active = functools.reduce(jnp.logical_or, [segment == g for g, _, _ in cases])
    for g, x_parts, before in cases:
        @pl.when(segment == g)
        def _():
            copies = []
            for parts, target in ((x_parts, xs), (before, buf.at[pl.ds(slot(0, 1), channels)])):
                at = 0
                for part in parts:
                    src = source(part)
                    width = part[3] * row
                    copies.append(pltpu.make_async_copy(
                        src.at[:, pl.ds(part[2] * row, width)], target.at[:, pl.ds(at, width)],
                        sems.at[len(copies)]))
                    at += width
            for c in copies:
                c.start()
            for c in copies:
                c.wait()

    @pl.when(active)
    def _():
        def squares(i, acc):
            v = xs[pl.ds(pl.multiple_of(i * CHUNK, CHUNK), CHUNK), :].astype(F32)
            v = v * v
            for k in range(0, CHUNK, 8):
                acc = acc + v[k:k + 8]
            return acc

        acc = lax.fori_loop(0, channels // CHUNK, squares, jnp.zeros((8, lanes_in), F32))
        scale = lax.rsqrt(jnp.sum(acc, axis=0, keepdims=True) * (1.0 / channels) + 1e-06)
        lane = lax.broadcasted_iota(jnp.int32, (CHUNK, row), 1)
        col = lax.rem(lane, cols)
        first, last = col == 0, col == cols - 1
        head = lane < row - cols
        zero = jnp.zeros((), BF16)

        def spread(i, _):
            at = pl.multiple_of(i * CHUNK, CHUNK)
            gain = gain_ref[pl.ds(at, CHUNK), :]
            here = [pl.ds(r * row, row) for r in range(rows_in)]
            values = [xs[pl.ds(at, CHUNK), h].astype(F32) for h in here]
            olds = [buf[pl.ds(slot(0, 1) + at, CHUNK), h] for h in here]
            results = []
            for r in range(rows_in):
                g = values[r] * scale[:, r * row:(r + 1) * row] * gain
                new = (0.5 * g * (1.0 + jnp.tanh(0.5 * g))).astype(BF16)
                mixed = pltpu.roll(jnp.where(head, new, olds[r]), cols, 1)
                for a, v in enumerate((olds[r], mixed, new)):
                    results.append((a, 0, r, jnp.where(first, zero, pltpu.roll(v, 1, 1))))
                    results.append((a, 2, r, jnp.where(last, zero, pltpu.roll(v, row - 1, 1))))
                    if a:
                        results.append((a, 1, r, v))
            for a, c, r, v in results:
                buf[pl.ds(slot(a, c) + at, CHUNK), here[r]] = v
            return 0

        lax.fori_loop(0, channels // CHUNK, spread, 0)
        acts_done = pltpu.make_async_copy(buf.at[pl.ds(slot(2, 1), channels)], acts_ref, sems.at[0])
        acts_done.start()
        step = 2 * row
        top = slab * own - (rows_out - own) // 2

        def taps(n, _):
            at = pl.multiple_of(n * step, step)
            part = xs[:, pl.ds(at + row, step)].astype(F32) + bias_ref[...]
            for b in range(3):
                part = part + jnp.dot(w_ref[b], buf[:, pl.ds(at + b * row, step)], preferred_element_type=F32)
            line = top + 2 * n + lax.broadcasted_iota(jnp.int32, (1, step), 1) // row
            total[:, pl.ds(at, step)] = jnp.where(
                jnp.logical_and(line >= 0, line < height), part, 0.0).astype(BF16)
            return 0

        lax.fori_loop(0, lanes_out // step, taps, 0)
        out_done = pltpu.make_async_copy(total, out_ref, sems.at[1])
        out_done.start()
        acts_done.wait()
        out_done.wait()


def layer_call(cases, rows_in, own, cols, block, height, place, fixed, ins):
    weight, bias, gain = fixed
    channels = weight.shape[1]
    row = block * cols
    return pl.pallas_call(
        functools.partial(layer_kernel, cases, rows_in, own, cols, block, height, len(ins)),
        out_shape=(
            jax.ShapeDtypeStruct((channels, (rows_in - 2) * row), BF16),
            jax.ShapeDtypeStruct((channels, rows_in * row), BF16),
            jax.ShapeDtypeStruct(weight.shape, weight.dtype),
            jax.ShapeDtypeStruct(bias.shape, bias.dtype),
            jax.ShapeDtypeStruct(gain.shape, gain.dtype),
        ),
        in_specs=[SMEM, VMEM, VMEM, VMEM] + [ANY] * len(ins),
        out_specs=(ANY, ANY, VMEM, VMEM, VMEM),
        input_output_aliases={1: 2, 2: 3, 3: 4},
        scratch_shapes=[
            pltpu.VMEM((channels, rows_in * row), BF16),
            pltpu.VMEM((9 * channels, rows_in * row), BF16),
            pltpu.VMEM((channels, (rows_in - 2) * row), BF16),
            pltpu.SemaphoreType.DMA((8,)),
        ],
        compiler_params=pltpu.CompilerParams(vmem_limit_bytes=VMEM_BYTES),
        cost_estimate=pl.CostEstimate(
            flops=2 * (rows_in - 2) * row * 27 * channels * channels, bytes_accessed=0, transcendentals=0),
    )(place, weight, bias, gain, *ins)


def local(segments, slabs, video_in, cache_in, conv_weight, conv_bias, norm_gain):
    frames, own, cols, channels = video_in.shape
    height = own * slabs
    segment = lax.axis_index("segment")
    slab = lax.axis_index("slab")
    axes = ("segment", "slab")
    block = frames // segments
    row = block * cols
    blocks = frames // block
    place = jnp.stack([segment, slab]).astype(jnp.int32)
    evens = range(0, segments, 2)
    odds = range(1, segments, 2)

    def moved(value, pairs, step):
        return lax.ppermute(value, axes, [
            (a * slabs + s, b * slabs + s + step) for a, b in pairs for s in range(slabs) if 0 <= s + step < slabs])

    def lanes(value):
        value = value.reshape(-1, block, own, cols, channels)
        return value.transpose(0, 4, 2, 1, 3).reshape(-1, channels, own * row)

    first = lanes(jnp.concatenate([cache_in[0], video_in[:block]], axis=0))
    first_below = moved(first[..., :2 * row], [(g, g) for g in evens], -1)
    first_above = moved(first[..., (own - 2) * row:], [(g, g) for g in evens], 1)
    place, weight = lax.optimization_barrier((place, conv_weight[0]))
    cuts = ((1, (own - 1) * row, row), (1, 0, row))
    weight, bias, gain, later, odd_last, odd_first = turned_weights(
        weight, conv_bias, norm_gain, lanes(video_in[block:]), first, cuts)
    odd_above = moved(odd_last, [(g, g) for g in odds], 1)
    odd_below = moved(odd_first, [(g, g) for g in odds], -1)
    later_below = moved(later[..., :2 * row], [(0, 0)], -1)
    later_above = moved(later[..., (own - 2) * row:], [(0, 0)], 1)
    fixed = (weight, bias, gain)

    call = functools.partial(layer_call, own=own, cols=cols, block=block, height=height, place=place)
    across = [(g, g ^ 1) for g in range(segments)]
    hop = [(g, g + 1) for g in odds if g + 1 < segments]
    planes = segments // 2
    arrived, done = [], []
    even_acts = odd_acts = None
    even_cache, odd_cache = [None] * planes, [None] * planes
    ticks = blocks + LAG * (planes - 1)
    for tick in range(ticks):
        busy = [p for p in range(planes) if 0 <= tick - LAG * p < blocks]
        ins = [first, first_above, first_below]
        old = [(1, 0, 0, 2), (0, 0, 0, own), (2, 0, 0, 2)]
        if tick:
            ins.append(even_acts)
            kept = [(3, None, 0, own + 4)]
        cases = []
        for p in busy:
            b = tick - LAG * p
            if p == 0 and b == 0:
                parts = [(1, 1, 0, 2), (0, 1, 0, own), (2, 1, 0, 2)]
            else:
                n = len(ins)
                if p == 0:
                    ins += [later, later_above, later_below]
                    parts = [(n + 1, b - 1, 0, 2), (n, b - 1, 0, own), (n + 2, b - 1, 0, 2)]
                else:
                    ins += list(arrived[b])
                    parts = [(n + 1, None, 0, 2), (n, None, 0, own), (n + 2, None, 0, 2)]
            cases.append((2 * p, parts, old if b == 0 else kept))
        if tick == 0:
            ins += [odd_above, odd_below]
        if tick == ticks - 1:
            ins.append(done[-2])
        out, even_acts, *fixed = call(cases, own + 4, fixed=fixed, ins=ins)
        if 0 < tick <= blocks:
            out, *arrived[tick - 1] = lax.optimization_barrier((out, *arrived[tick - 1]))
        crossed = moved(out, across, 0)

        ins = [crossed, first, odd_above, odd_below]
        old = [(2, 0, 0, 1), (1, 0, 0, own), (3, 0, 0, 1)]
        if tick:
            ins.append(odd_acts)
        if tick == 0:
            ins += [later_above, later_below]
        if tick >= ticks - 2:
            ins.append(done[0] if tick < ticks - 1 else done[-1])
        cases = [(2 * p + 1, [(0, None, 0, own + 2)], old if tick == LAG * p else [(4, None, 0, own + 2)]) for p in busy]
        out, odd_acts, *fixed = call(cases, own + 2, fixed=fixed, ins=ins)
        if tick < blocks:
            arrived.append((moved(out, hop, 0), moved(out[:, (own - 2) * row:], hop, 1), moved(out[:, :2 * row], hop, -1)))
        b = tick - LAG * (planes - 1)
        if 0 <= b < blocks:
            done.append(out if b == segments - 1 else moved(out, [(segments - 1, b)], 0))
        for p in busy:
            if tick - LAG * p == blocks - 1:
                even_cache[p] = even_acts[:, 2 * row:(2 + own) * row]
                odd_cache[p] = odd_acts[:, row:(1 + own) * row]

    def natural(value):
        return value.reshape(channels, own, block, cols).transpose(2, 1, 3, 0)

    result, segment = lax.optimization_barrier((done[-1], segment))
    for b in range(blocks - 1):
        result = jnp.where(segment == b, done[b], result)
    cache = odd_cache[-1]
    for p in range(planes):
        cache = jnp.where(segment == 2 * p, even_cache[p], cache)
        cache = jnp.where(segment == 2 * p + 1, odd_cache[p], cache)
    return natural(result), natural(cache)[None]


def solution(mesh):
    segments, slabs = mesh.shape["segment"], mesh.shape["slab"]
    return jax.shard_map(
        functools.partial(local, segments, slabs),
        mesh=mesh,
        in_specs=(
            P(None, "slab", None, None),
            P("segment", None, "slab", None, None),
            P("segment", None, None, None, None, None),
            P("segment", None),
            P("segment", None),
        ),
        out_specs=(P("segment", "slab", None, None), P("segment", None, "slab", None, None)),
        check_vma=False,
    )
```

```python
import functools
import jax
import jax.numpy as jnp
from jax import lax
from jax.experimental import pallas as pl
from jax.experimental.pallas import tpu as pltpu
from jax.sharding import PartitionSpec as P

LAG = 2
CHUNK = 128
VMEM_BYTES = 24 * 2**20
F32 = jnp.float32
BF16 = jnp.bfloat16
ANY = pl.BlockSpec(memory_space=pl.ANY)
VMEM = pl.BlockSpec(memory_space=pltpu.VMEM)
SMEM = pl.BlockSpec(memory_space=pltpu.SMEM)


def turn_kernel(cuts, w_ref, bias_ref, gain_ref, later_ref, first_ref, out_ref, bias_out, gain_out, _, *refs):
    ws, rows, sems, cut_sems = refs[-4:]
    channels = w_ref.shape[-1]
    copies = [pltpu.make_async_copy(w_ref.at[k // 3, k % 3], ws.at[k], sems.at[k]) for k in range(9)]
    vectors = [pltpu.make_async_copy(ref, rows.at[pl.ds(k, 1)], sems.at[9 + k])
               for k, ref in enumerate((bias_ref, gain_ref))]
    parts = [pltpu.make_async_copy(first_ref.at[pl.ds(0, n), :, pl.ds(at, width)], refs[k], cut_sems.at[k])
             for k, (n, at, width) in enumerate(cuts)]
    for copy in vectors + copies + parts:
        copy.start()
    for k, copy in enumerate(copies):
        copy.wait()
        for c in range(3):
            out_ref[k % 3, :, pl.ds((k // 3 * 3 + c) * channels, channels)] = jnp.transpose(ws[k, c], (1, 0))
    for copy in vectors + parts:
        copy.wait()
    turned = jnp.transpose(rows[...], (1, 0))
    bias_out[...] = turned[:, 0:1]
    gain_out[...] = turned[:, 1:2]


def turned_weights(weight, bias, gain, later, first, cuts):
    channels = weight.shape[-1]
    return pl.pallas_call(
        functools.partial(turn_kernel, cuts),
        out_shape=(
            jax.ShapeDtypeStruct((3, channels, 9 * channels), BF16),
            jax.ShapeDtypeStruct((channels, 1), F32),
            jax.ShapeDtypeStruct((channels, 1), F32),
            jax.ShapeDtypeStruct(later.shape, later.dtype),
            *(jax.ShapeDtypeStruct((n, channels, width), BF16) for n, _, width in cuts),
        ),
        in_specs=[pl.BlockSpec(memory_space=pltpu.HBM)] * 3 + [ANY] * 2,
        out_specs=(VMEM, VMEM, VMEM, ANY) + (ANY,) * len(cuts),
        input_output_aliases={3: 3},
        scratch_shapes=[
            pltpu.VMEM((9, 3, channels, channels), BF16),
            pltpu.VMEM((8, channels), F32),
            pltpu.SemaphoreType.DMA((11,)),
            pltpu.SemaphoreType.DMA((len(cuts),)),
        ],
        compiler_params=pltpu.CompilerParams(vmem_limit_bytes=VMEM_BYTES),
        cost_estimate=pl.CostEstimate(flops=0, bytes_accessed=4 * weight.size, transcendentals=0),
    )(*(pltpu.with_memory_space_constraint(v, pltpu.HBM) for v in (weight, bias, gain)), later, first)


def layer_kernel(cases, rows_in, own, cols, block, height, n_in, place_ref, w_ref, bias_ref, gain_ref, *refs):
    ins = refs[:n_in]
    out_ref, acts_ref = refs[n_in:n_in + 2]
    xs, buf, total, sems = refs[n_in + 5:]
    channels = xs.shape[0]
    row = block * cols
    rows_out = rows_in - 2
    lanes_in, lanes_out = rows_in * row, rows_out * row
    segment, slab = place_ref[0], place_ref[1]

    def slot(a, c):
        return (3 * a + c) * channels

    def source(part):
        at, index = part[0], part[1]
        return ins[at] if index is None else ins[at].at[index]

    active = functools.reduce(jnp.logical_or, [segment == g for g, _, _ in cases])
    for g, x_parts, before in cases:
        @pl.when(segment == g)
        def _():
            copies = []
            for parts, target in ((x_parts, xs), (before, buf.at[pl.ds(slot(0, 1), channels)])):
                at = 0
                for part in parts:
                    src = source(part)
                    width = part[3] * row
                    copies.append(pltpu.make_async_copy(
                        src.at[:, pl.ds(part[2] * row, width)], target.at[:, pl.ds(at, width)],
                        sems.at[len(copies)]))
                    at += width
            for c in copies:
                c.start()
            for c in copies:
                c.wait()

    @pl.when(active)
    def _():
        def squares(i, acc):
            v = xs[pl.ds(pl.multiple_of(i * CHUNK, CHUNK), CHUNK), :].astype(F32)
            v = v * v
            for k in range(0, CHUNK, 8):
                acc = acc + v[k:k + 8]
            return acc

        acc = lax.fori_loop(0, channels // CHUNK, squares, jnp.zeros((8, lanes_in), F32))
        scale = lax.rsqrt(jnp.sum(acc, axis=0, keepdims=True) * (1.0 / channels) + 1e-06)
        lane = lax.broadcasted_iota(jnp.int32, (CHUNK, row), 1)
        col = lax.rem(lane, cols)
        first, last = col == 0, col == cols - 1
        head = lane < row - cols
        zero = jnp.zeros((), BF16)

        def spread(i, _):
            at = pl.multiple_of(i * CHUNK, CHUNK)
            gain = gain_ref[pl.ds(at, CHUNK), :]
            here = [pl.ds(r * row, row) for r in range(rows_in)]
            values = [xs[pl.ds(at, CHUNK), h].astype(F32) for h in here]
            olds = [buf[pl.ds(slot(0, 1) + at, CHUNK), h] for h in here]
            results = []
            for r in range(rows_in):
                g = values[r] * scale[:, r * row:(r + 1) * row] * gain
                new = (0.5 * g * (1.0 + jnp.tanh(0.5 * g))).astype(BF16)
                mixed = pltpu.roll(jnp.where(head, new, olds[r]), cols, 1)
                for a, v in enumerate((olds[r], mixed, new)):
                    results.append((a, 0, r, jnp.where(first, zero, pltpu.roll(v, 1, 1))))
                    results.append((a, 2, r, jnp.where(last, zero, pltpu.roll(v, row - 1, 1))))
                    if a:
                        results.append((a, 1, r, v))
            for a, c, r, v in results:
                buf[pl.ds(slot(a, c) + at, CHUNK), here[r]] = v
            return 0

        lax.fori_loop(0, channels // CHUNK, spread, 0)
        acts_done = pltpu.make_async_copy(buf.at[pl.ds(slot(2, 1), channels)], acts_ref, sems.at[0])
        acts_done.start()
        step = 2 * row
        top = slab * own - (rows_out - own) // 2

        def taps(n, _):
            at = pl.multiple_of(n * step, step)
            part = xs[:, pl.ds(at + row, step)].astype(F32) + bias_ref[...]
            for b in range(3):
                part = part + jnp.dot(w_ref[b], buf[:, pl.ds(at + b * row, step)], preferred_element_type=F32)
            line = top + 2 * n + lax.broadcasted_iota(jnp.int32, (1, step), 1) // row
            total[:, pl.ds(at, step)] = jnp.where(
                jnp.logical_and(line >= 0, line < height), part, 0.0).astype(BF16)
            return 0

        lax.fori_loop(0, lanes_out // step, taps, 0)
        out_done = pltpu.make_async_copy(total, out_ref, sems.at[1])
        out_done.start()
        acts_done.wait()
        out_done.wait()


def layer_call(cases, rows_in, own, cols, block, height, place, fixed, ins):
    weight, bias, gain = fixed
    channels = weight.shape[1]
    row = block * cols
    return pl.pallas_call(
        functools.partial(layer_kernel, cases, rows_in, own, cols, block, height, len(ins)),
        out_shape=(
            jax.ShapeDtypeStruct((channels, (rows_in - 2) * row), BF16),
            jax.ShapeDtypeStruct((channels, rows_in * row), BF16),
            jax.ShapeDtypeStruct(weight.shape, weight.dtype),
            jax.ShapeDtypeStruct(bias.shape, bias.dtype),
            jax.ShapeDtypeStruct(gain.shape, gain.dtype),
        ),
        in_specs=[SMEM, VMEM, VMEM, VMEM] + [ANY] * len(ins),
        out_specs=(ANY, ANY, VMEM, VMEM, VMEM),
        input_output_aliases={1: 2, 2: 3, 3: 4},
        scratch_shapes=[
            pltpu.VMEM((channels, rows_in * row), BF16),
            pltpu.VMEM((9 * channels, rows_in * row), BF16),
            pltpu.VMEM((channels, (rows_in - 2) * row), BF16),
            pltpu.SemaphoreType.DMA((8,)),
        ],
        compiler_params=pltpu.CompilerParams(vmem_limit_bytes=VMEM_BYTES),
        cost_estimate=pl.CostEstimate(
            flops=2 * (rows_in - 2) * row * 27 * channels * channels, bytes_accessed=0, transcendentals=0),
    )(place, weight, bias, gain, *ins)


def local(segments, slabs, video_in, cache_in, conv_weight, conv_bias, norm_gain):
    frames, own, cols, channels = video_in.shape
    height = own * slabs
    segment = lax.axis_index("segment")
    slab = lax.axis_index("slab")
    axes = ("segment", "slab")
    block = frames // segments
    row = block * cols
    blocks = frames // block
    place = jnp.stack([segment, slab]).astype(jnp.int32)
    evens = range(0, segments, 2)
    odds = range(1, segments, 2)

    def moved(value, pairs, step):
        return lax.ppermute(value, axes, [
            (a * slabs + s, b * slabs + s + step) for a, b in pairs for s in range(slabs) if 0 <= s + step < slabs])

    def lanes(value):
        value = value.reshape(-1, block, own, cols, channels)
        return value.transpose(0, 4, 2, 1, 3).reshape(-1, channels, own * row)

    first = lanes(jnp.concatenate([cache_in[0], video_in[:block]], axis=0))
    first_below = moved(first[..., :2 * row], [(g, g) for g in evens], -1)
    first_above = moved(first[..., (own - 2) * row:], [(g, g) for g in evens], 1)
    place, weight = lax.optimization_barrier((place, conv_weight[0]))
    cuts = ((1, (own - 1) * row, row), (1, 0, row))
    weight, bias, gain, later, odd_last, odd_first = turned_weights(
        weight, conv_bias, norm_gain, lanes(video_in[block:]), first, cuts)
    odd_above = moved(odd_last, [(g, g) for g in odds], 1)
    odd_below = moved(odd_first, [(g, g) for g in odds], -1)
    later_below = moved(later[..., :2 * row], [(0, 0)], -1)
    later_above = moved(later[..., (own - 2) * row:], [(0, 0)], 1)
    fixed = (weight, bias, gain)

    call = functools.partial(layer_call, own=own, cols=cols, block=block, height=height, place=place)
    across = [(g, g ^ 1) for g in range(segments)]
    hop = [(g, g + 1) for g in odds if g + 1 < segments]
    planes = segments // 2
    arrived, done = [], []
    even_acts = odd_acts = None
    even_cache, odd_cache = [None] * planes, [None] * planes
    ticks = blocks + LAG * (planes - 1)
    for tick in range(ticks):
        busy = [p for p in range(planes) if 0 <= tick - LAG * p < blocks]
        ins = [first, first_above, first_below]
        old = [(1, 0, 0, 2), (0, 0, 0, own), (2, 0, 0, 2)]
        if tick:
            ins.append(even_acts)
            kept = [(3, None, 0, own + 4)]
        cases = []
        for p in busy:
            b = tick - LAG * p
            if p == 0 and b == 0:
                parts = [(1, 1, 0, 2), (0, 1, 0, own), (2, 1, 0, 2)]
            else:
                n = len(ins)
                if p == 0:
                    ins += [later, later_above, later_below]
                    parts = [(n + 1, b - 1, 0, 2), (n, b - 1, 0, own), (n + 2, b - 1, 0, 2)]
                else:
                    ins += list(arrived[b])
                    parts = [(n + 1, None, 0, 2), (n, None, 0, own), (n + 2, None, 0, 2)]
            cases.append((2 * p, parts, old if b == 0 else kept))
        if tick == 0:
            ins += [odd_above, odd_below]
        out, even_acts, *fixed = call(cases, own + 4, fixed=fixed, ins=ins)
        hops = arrived[tick - 1] if 0 < tick <= blocks else ()
        out, *hops = lax.optimization_barrier((out, *hops, *done[-1:]))
        if done:
            done[-1] = hops.pop()
        if hops:
            arrived[tick - 1] = hops
        crossed = moved(out, across, 0)

        ins = [crossed, first, odd_above, odd_below]
        old = [(2, 0, 0, 1), (1, 0, 0, own), (3, 0, 0, 1)]
        if tick:
            ins.append(odd_acts)
        if tick == 0:
            ins += [later_above, later_below]
        cases = [(2 * p + 1, [(0, None, 0, own + 2)], old if tick == LAG * p else [(4, None, 0, own + 2)]) for p in busy]
        out, odd_acts, *fixed = call(cases, own + 2, fixed=fixed, ins=ins)
        if tick < blocks:
            arrived.append((moved(out, hop, 0), moved(out[:, (own - 2) * row:], hop, 1), moved(out[:, :2 * row], hop, -1)))
        b = tick - LAG * (planes - 1)
        if 0 <= b < blocks:
            done.append(out if b == segments - 1 else moved(out, [(segments - 1, b)], 0))
        for p in busy:
            if tick - LAG * p == blocks - 1:
                even_cache[p] = even_acts[:, 2 * row:(2 + own) * row]
                odd_cache[p] = odd_acts[:, row:(1 + own) * row]

    def natural(value):
        return value.reshape(channels, own, block, cols).transpose(2, 1, 3, 0)

    result, segment = lax.optimization_barrier((done[-1], segment))
    for b in range(blocks - 1):
        result = jnp.where(segment == b, done[b], result)
    cache = odd_cache[-1]
    for p in range(planes):
        cache = jnp.where(segment == 2 * p, even_cache[p], cache)
        cache = jnp.where(segment == 2 * p + 1, odd_cache[p], cache)
    return natural(result), natural(cache)[None]


def solution(mesh):
    segments, slabs = mesh.shape["segment"], mesh.shape["slab"]
    return jax.shard_map(
        functools.partial(local, segments, slabs),
        mesh=mesh,
        in_specs=(
            P(None, "slab", None, None),
            P("segment", None, "slab", None, None),
            P("segment", None, None, None, None, None),
            P("segment", None),
            P("segment", None),
        ),
        out_specs=(P("segment", "slab", None, None), P("segment", None, "slab", None, None)),
        check_vma=False,
    )
```

```python
import functools
import jax
import jax.numpy as jnp
from jax import lax
from jax.experimental import pallas as pl
from jax.experimental.pallas import tpu as pltpu
from jax.sharding import PartitionSpec as P

LAG = 2
CHUNK = 128
VMEM_BYTES = 24 * 2**20
F32 = jnp.float32
BF16 = jnp.bfloat16
ANY = pl.BlockSpec(memory_space=pl.ANY)
VMEM = pl.BlockSpec(memory_space=pltpu.VMEM)
SMEM = pl.BlockSpec(memory_space=pltpu.SMEM)


def turn_kernel(cuts, w_ref, bias_ref, gain_ref, later_ref, first_ref, out_ref, bias_out, gain_out, _, *refs):
    ws, rows, sems, cut_sems = refs[-4:]
    channels = w_ref.shape[-1]
    copies = [pltpu.make_async_copy(w_ref.at[k // 3, k % 3], ws.at[k], sems.at[k]) for k in range(9)]
    vectors = [pltpu.make_async_copy(ref, rows.at[pl.ds(k, 1)], sems.at[9 + k])
               for k, ref in enumerate((bias_ref, gain_ref))]
    parts = [pltpu.make_async_copy(first_ref.at[pl.ds(0, n), :, pl.ds(at, width)], refs[k], cut_sems.at[k])
             for k, (n, at, width) in enumerate(cuts)]
    for copy in vectors + copies + parts:
        copy.start()
    for k, copy in enumerate(copies):
        copy.wait()
        for c in range(3):
            out_ref[k % 3, :, pl.ds((k // 3 * 3 + c) * channels, channels)] = jnp.transpose(ws[k, c], (1, 0))
    for copy in vectors + parts:
        copy.wait()
    turned = jnp.transpose(rows[...], (1, 0))
    bias_out[...] = turned[:, 0:1]
    gain_out[...] = turned[:, 1:2]


def turned_weights(weight, bias, gain, later, first, cuts):
    channels = weight.shape[-1]
    return pl.pallas_call(
        functools.partial(turn_kernel, cuts),
        out_shape=(
            jax.ShapeDtypeStruct((3, channels, 9 * channels), BF16),
            jax.ShapeDtypeStruct((channels, 1), F32),
            jax.ShapeDtypeStruct((channels, 1), F32),
            jax.ShapeDtypeStruct(later.shape, later.dtype),
            *(jax.ShapeDtypeStruct((n, channels, width), BF16) for n, _, width in cuts),
        ),
        in_specs=[pl.BlockSpec(memory_space=pltpu.HBM)] * 3 + [ANY] * 2,
        out_specs=(VMEM, VMEM, VMEM, ANY) + (ANY,) * len(cuts),
        input_output_aliases={3: 3},
        scratch_shapes=[
            pltpu.VMEM((9, 3, channels, channels), BF16),
            pltpu.VMEM((8, channels), F32),
            pltpu.SemaphoreType.DMA((11,)),
            pltpu.SemaphoreType.DMA((len(cuts),)),
        ],
        compiler_params=pltpu.CompilerParams(vmem_limit_bytes=VMEM_BYTES),
        cost_estimate=pl.CostEstimate(flops=0, bytes_accessed=4 * weight.size, transcendentals=0),
    )(*(pltpu.with_memory_space_constraint(v, pltpu.HBM) for v in (weight, bias, gain)), later, first)


def layer_kernel(cases, rows_in, own, cols, block, height, n_in, back, place_ref, w_ref, bias_ref, gain_ref, *refs):
    ins = refs[:n_in]
    out_ref, acts_ref = refs[n_in:n_in + 2]
    xs, buf, total, sems = refs[n_in + 5:]
    channels = xs.shape[0]
    row = block * cols
    rows_out = rows_in - 2
    lanes_in, lanes_out = rows_in * row, rows_out * row
    segment, slab = place_ref[0], place_ref[1]

    def slot(a, c):
        return (3 * a + c) * channels

    def source(part):
        at, index = part[0], part[1]
        return ins[at] if index is None else ins[at].at[index]

    active = functools.reduce(jnp.logical_or, [segment == g for g, _, _ in cases])
    if back is not None:
        @pl.when(segment == back[0])
        def _():
            copy = pltpu.make_async_copy(ins[back[1]], out_ref.at[:, pl.ds(0, ins[back[1]].shape[1])], sems.at[0])
            copy.start()
            copy.wait()

    for g, x_parts, before in cases:
        @pl.when(segment == g)
        def _():
            copies = []
            for parts, target in ((x_parts, xs), (before, buf.at[pl.ds(slot(0, 1), channels)])):
                at = 0
                for part in parts:
                    src = source(part)
                    width = part[3] * row
                    copies.append(pltpu.make_async_copy(
                        src.at[:, pl.ds(part[2] * row, width)], target.at[:, pl.ds(at, width)],
                        sems.at[len(copies)]))
                    at += width
            for c in copies:
                c.start()
            for c in copies:
                c.wait()

    @pl.when(active)
    def _():
        def squares(i, acc):
            v = xs[pl.ds(pl.multiple_of(i * CHUNK, CHUNK), CHUNK), :].astype(F32)
            v = v * v
            for k in range(0, CHUNK, 8):
                acc = acc + v[k:k + 8]
            return acc

        acc = lax.fori_loop(0, channels // CHUNK, squares, jnp.zeros((8, lanes_in), F32))
        scale = lax.rsqrt(jnp.sum(acc, axis=0, keepdims=True) * (1.0 / channels) + 1e-06)
        lane = lax.broadcasted_iota(jnp.int32, (CHUNK, row), 1)
        col = lax.rem(lane, cols)
        first, last = col == 0, col == cols - 1
        head = lane < row - cols
        zero = jnp.zeros((), BF16)

        def spread(i, _):
            at = pl.multiple_of(i * CHUNK, CHUNK)
            gain = gain_ref[pl.ds(at, CHUNK), :]
            here = [pl.ds(r * row, row) for r in range(rows_in)]
            values = [xs[pl.ds(at, CHUNK), h].astype(F32) for h in here]
            olds = [buf[pl.ds(slot(0, 1) + at, CHUNK), h] for h in here]
            results = []
            for r in range(rows_in):
                g = values[r] * scale[:, r * row:(r + 1) * row] * gain
                new = (0.5 * g * (1.0 + jnp.tanh(0.5 * g))).astype(BF16)
                mixed = pltpu.roll(jnp.where(head, new, olds[r]), cols, 1)
                for a, v in enumerate((olds[r], mixed, new)):
                    results.append((a, 0, r, jnp.where(first, zero, pltpu.roll(v, 1, 1))))
                    results.append((a, 2, r, jnp.where(last, zero, pltpu.roll(v, row - 1, 1))))
                    if a:
                        results.append((a, 1, r, v))
            for a, c, r, v in results:
                buf[pl.ds(slot(a, c) + at, CHUNK), here[r]] = v
            return 0

        lax.fori_loop(0, channels // CHUNK, spread, 0)
        acts_done = pltpu.make_async_copy(buf.at[pl.ds(slot(2, 1), channels)], acts_ref, sems.at[0])
        acts_done.start()
        step = 2 * row
        top = slab * own - (rows_out - own) // 2

        def taps(n, _):
            at = pl.multiple_of(n * step, step)
            part = xs[:, pl.ds(at + row, step)].astype(F32) + bias_ref[...]
            for b in range(3):
                part = part + jnp.dot(w_ref[b], buf[:, pl.ds(at + b * row, step)], preferred_element_type=F32)
            line = top + 2 * n + lax.broadcasted_iota(jnp.int32, (1, step), 1) // row
            total[:, pl.ds(at, step)] = jnp.where(
                jnp.logical_and(line >= 0, line < height), part, 0.0).astype(BF16)
            return 0

        lax.fori_loop(0, lanes_out // step, taps, 0)
        out_done = pltpu.make_async_copy(total, out_ref, sems.at[1])
        out_done.start()
        acts_done.wait()
        out_done.wait()


def layer_call(cases, rows_in, own, cols, block, height, place, fixed, ins, back=None):
    weight, bias, gain = fixed
    channels = weight.shape[1]
    row = block * cols
    return pl.pallas_call(
        functools.partial(layer_kernel, cases, rows_in, own, cols, block, height, len(ins), back),
        out_shape=(
            jax.ShapeDtypeStruct((channels, (rows_in - 2) * row), BF16),
            jax.ShapeDtypeStruct((channels, rows_in * row), BF16),
            jax.ShapeDtypeStruct(weight.shape, weight.dtype),
            jax.ShapeDtypeStruct(bias.shape, bias.dtype),
            jax.ShapeDtypeStruct(gain.shape, gain.dtype),
        ),
        in_specs=[SMEM, VMEM, VMEM, VMEM] + [ANY] * len(ins),
        out_specs=(ANY, ANY, VMEM, VMEM, VMEM),
        input_output_aliases={1: 2, 2: 3, 3: 4},
        scratch_shapes=[
            pltpu.VMEM((channels, rows_in * row), BF16),
            pltpu.VMEM((9 * channels, rows_in * row), BF16),
            pltpu.VMEM((channels, (rows_in - 2) * row), BF16),
            pltpu.SemaphoreType.DMA((8,)),
        ],
        compiler_params=pltpu.CompilerParams(vmem_limit_bytes=VMEM_BYTES),
        cost_estimate=pl.CostEstimate(
            flops=2 * (rows_in - 2) * row * 27 * channels * channels, bytes_accessed=0, transcendentals=0),
    )(place, weight, bias, gain, *ins)


def local(segments, slabs, video_in, cache_in, conv_weight, conv_bias, norm_gain):
    frames, own, cols, channels = video_in.shape
    height = own * slabs
    segment = lax.axis_index("segment")
    slab = lax.axis_index("slab")
    axes = ("segment", "slab")
    block = frames // segments
    row = block * cols
    blocks = frames // block
    place = jnp.stack([segment, slab]).astype(jnp.int32)
    evens = range(0, segments, 2)
    odds = range(1, segments, 2)

    def moved(value, pairs, step):
        return lax.ppermute(value, axes, [
            (a * slabs + s, b * slabs + s + step) for a, b in pairs for s in range(slabs) if 0 <= s + step < slabs])

    def lanes(value):
        value = value.reshape(-1, block, own, cols, channels)
        return value.transpose(0, 4, 2, 1, 3).reshape(-1, channels, own * row)

    first = lanes(jnp.concatenate([cache_in[0], video_in[:2 * block]], axis=0))
    first_below = moved(first[..., :2 * row], [(g, g) for g in evens], -1)
    first_above = moved(first[..., (own - 2) * row:], [(g, g) for g in evens], 1)
    place, weight = lax.optimization_barrier((place, conv_weight[0]))
    cuts = ((1, (own - 1) * row, row), (1, 0, row))
    weight, bias, gain, later, odd_last, odd_first = turned_weights(
        weight, conv_bias, norm_gain, lanes(video_in[2 * block:]), first, cuts)
    odd_above = moved(odd_last, [(g, g) for g in odds], 1)
    odd_below = moved(odd_first, [(g, g) for g in odds], -1)
    later_below = moved(later[..., :2 * row], [(0, 0)], -1)
    fixed = (weight, bias, gain)

    call = functools.partial(layer_call, own=own, cols=cols, block=block, height=height, place=place)
    across = [(g, g ^ 1) for g in range(segments)]
    hop = [(g, g + 1) for g in odds if g + 1 < segments]
    planes = segments // 2
    arrived, done = [], []
    even_acts = odd_acts = None
    even_cache, odd_cache = [None] * planes, [None] * planes
    ticks = blocks + LAG * (planes - 1)
    for tick in range(ticks):
        busy = [p for p in range(planes) if 0 <= tick - LAG * p < blocks]
        ins = [first, first_above, first_below]
        old = [(1, 0, 0, 2), (0, 0, 0, own), (2, 0, 0, 2)]
        if tick:
            ins.append(even_acts)
            kept = [(3, None, 0, own + 4)]
        cases = []
        for p in busy:
            b = tick - LAG * p
            if p == 0 and b < 2:
                parts = [(1, b + 1, 0, 2), (0, b + 1, 0, own), (2, b + 1, 0, 2)]
            else:
                n = len(ins)
                if p == 0:
                    ins += [later, later_above, later_below]
                    parts = [(n + 1, b - 2, 0, 2), (n, b - 2, 0, own), (n + 2, b - 2, 0, 2)]
                else:
                    ins += list(arrived[b])
                    parts = [(n + 1, None, 0, 2), (n, None, 0, own), (n + 2, None, 0, 2)]
            cases.append((2 * p, parts, old if b == 0 else kept))
        if tick == 0:
            ins += [odd_above, odd_below]
        back = None
        if tick == ticks - 1:
            back = (segments - 1, len(ins))
            ins.append(out)
        out, even_acts, *fixed = call(cases, own + 4, fixed=fixed, ins=ins, back=back)
        sent = list(arrived[tick - 1]) if 0 < tick <= blocks else []
        if tick == 1:
            sent.append(later_below)
        if tick == ticks - 2:
            sent += done
        out, *sent = lax.optimization_barrier((out, *sent))
        if tick == ticks - 2:
            done = sent[len(sent) - len(done):]
        if 0 < tick <= blocks:
            arrived[tick - 1] = sent[:3]
        if tick == 1:
            later_below = sent[3]
        crossed = moved(out, across, 0)
        if tick == 1:
            crossed, above = lax.optimization_barrier((crossed, later[..., (own - 2) * row:]))
            later_above = moved(above, [(0, 0)], 1)
        if tick == ticks - 1:
            done[-1] = crossed[:, :own * row]

        ins = [crossed, first, odd_above, odd_below]
        old = [(2, 0, 0, 1), (1, 0, 0, own), (3, 0, 0, 1)]
        if tick:
            ins.append(odd_acts)
        cases = [(2 * p + 1, [(0, None, 0, own + 2)], old if tick == LAG * p else [(4, None, 0, own + 2)]) for p in busy]
        out, odd_acts, *fixed = call(cases, own + 2, fixed=fixed, ins=ins)
        if tick < blocks:
            arrived.append((moved(out, hop, 0), moved(out[:, (own - 2) * row:], hop, 1), moved(out[:, :2 * row], hop, -1)))
        b = tick - LAG * (planes - 1)
        if 0 <= b < blocks:
            done.append(out if b >= segments - 2 else moved(out, [(segments - 1, b)], 0))
        for p in busy:
            if tick - LAG * p == blocks - 1:
                even_cache[p] = even_acts[:, 2 * row:(2 + own) * row]
                odd_cache[p] = odd_acts[:, row:(1 + own) * row]

    def natural(value):
        return value.reshape(channels, own, block, cols).transpose(2, 1, 3, 0)

    result, segment = lax.optimization_barrier((done[-1], segment))
    for b in range(blocks - 1):
        result = jnp.where(segment == b, done[b], result)
    cache = odd_cache[-1]
    for p in range(planes):
        cache = jnp.where(segment == 2 * p, even_cache[p], cache)
        cache = jnp.where(segment == 2 * p + 1, odd_cache[p], cache)
    return natural(result), natural(cache)[None]


def solution(mesh):
    segments, slabs = mesh.shape["segment"], mesh.shape["slab"]
    return jax.shard_map(
        functools.partial(local, segments, slabs),
        mesh=mesh,
        in_specs=(
            P(None, "slab", None, None),
            P("segment", None, "slab", None, None),
            P("segment", None, None, None, None, None),
            P("segment", None),
            P("segment", None),
        ),
        out_specs=(P("segment", "slab", None, None), P("segment", None, "slab", None, None)),
        check_vma=False,
    )
```

```python
import functools
import jax
import jax.numpy as jnp
from jax import lax
from jax.experimental import pallas as pl
from jax.experimental.pallas import tpu as pltpu
from jax.sharding import PartitionSpec as P

LAG = 2
CHUNK = 128
VMEM_BYTES = 24 * 2**20
F32 = jnp.float32
BF16 = jnp.bfloat16
ANY = pl.BlockSpec(memory_space=pl.ANY)
VMEM = pl.BlockSpec(memory_space=pltpu.VMEM)
SMEM = pl.BlockSpec(memory_space=pltpu.SMEM)


def turn_kernel(cuts, w_ref, bias_ref, gain_ref, later_ref, first_ref, out_ref, bias_out, gain_out, _, *refs):
    ws, rows, sems, cut_sems = refs[-4:]
    channels = w_ref.shape[-1]
    copies = [pltpu.make_async_copy(w_ref.at[k // 3, k % 3], ws.at[k], sems.at[k]) for k in range(9)]
    vectors = [pltpu.make_async_copy(ref, rows.at[pl.ds(k, 1)], sems.at[9 + k])
               for k, ref in enumerate((bias_ref, gain_ref))]
    parts = [pltpu.make_async_copy(first_ref.at[pl.ds(0, n), :, pl.ds(at, width)], refs[k], cut_sems.at[k])
             for k, (n, at, width) in enumerate(cuts)]
    for copy in vectors + copies + parts:
        copy.start()
    for k, copy in enumerate(copies):
        copy.wait()
        for c in range(3):
            out_ref[k % 3, :, pl.ds((k // 3 * 3 + c) * channels, channels)] = jnp.transpose(ws[k, c], (1, 0))
    for copy in vectors + parts:
        copy.wait()
    turned = jnp.transpose(rows[...], (1, 0))
    bias_out[...] = turned[:, 0:1]
    gain_out[...] = turned[:, 1:2]


def turned_weights(weight, bias, gain, later, first, cuts):
    channels = weight.shape[-1]
    return pl.pallas_call(
        functools.partial(turn_kernel, cuts),
        out_shape=(
            jax.ShapeDtypeStruct((3, channels, 9 * channels), BF16),
            jax.ShapeDtypeStruct((channels, 1), F32),
            jax.ShapeDtypeStruct((channels, 1), F32),
            jax.ShapeDtypeStruct(later.shape, later.dtype),
            *(jax.ShapeDtypeStruct((n, channels, width), BF16) for n, _, width in cuts),
        ),
        in_specs=[pl.BlockSpec(memory_space=pltpu.HBM)] * 3 + [ANY] * 2,
        out_specs=(VMEM, VMEM, VMEM, ANY) + (ANY,) * len(cuts),
        input_output_aliases={3: 3},
        scratch_shapes=[
            pltpu.VMEM((9, 3, channels, channels), BF16),
            pltpu.VMEM((8, channels), F32),
            pltpu.SemaphoreType.DMA((11,)),
            pltpu.SemaphoreType.DMA((len(cuts),)),
        ],
        compiler_params=pltpu.CompilerParams(vmem_limit_bytes=VMEM_BYTES),
        cost_estimate=pl.CostEstimate(flops=0, bytes_accessed=4 * weight.size, transcendentals=0),
    )(*(pltpu.with_memory_space_constraint(v, pltpu.HBM) for v in (weight, bias, gain)), later, first)


def layer_kernel(cases, rows_in, own, cols, block, height, n_in, back, place_ref, w_ref, bias_ref, gain_ref, *refs):
    ins = refs[:n_in]
    out_ref, acts_ref = refs[n_in:n_in + 2]
    xs, buf, total, sems = refs[n_in + 5:]
    channels = xs.shape[0]
    row = block * cols
    rows_out = rows_in - 2
    lanes_in, lanes_out = rows_in * row, rows_out * row
    segment, slab = place_ref[0], place_ref[1]

    def slot(a, c):
        return (3 * a + c) * channels

    def source(part):
        at, index = part[0], part[1]
        return ins[at] if index is None else ins[at].at[index]

    active = functools.reduce(jnp.logical_or, [segment == g for g, _, _ in cases])
    if back is not None:
        @pl.when(segment == back[0])
        def _():
            copy = pltpu.make_async_copy(ins[back[1]], out_ref.at[:, pl.ds(0, ins[back[1]].shape[1])], sems.at[0])
            copy.start()
            copy.wait()

    for g, x_parts, before in cases:
        @pl.when(segment == g)
        def _():
            copies = []
            for parts, target in ((x_parts, xs), (before, buf.at[pl.ds(slot(0, 1), channels)])):
                at = 0
                for part in parts:
                    src = source(part)
                    width = part[3] * row
                    copies.append(pltpu.make_async_copy(
                        src.at[:, pl.ds(part[2] * row, width)], target.at[:, pl.ds(at, width)],
                        sems.at[len(copies)]))
                    at += width
            for c in copies:
                c.start()
            for c in copies:
                c.wait()

    @pl.when(active)
    def _():
        def squares(i, acc):
            v = xs[pl.ds(pl.multiple_of(i * CHUNK, CHUNK), CHUNK), :].astype(F32)
            v = v * v
            for k in range(0, CHUNK, 8):
                acc = acc + v[k:k + 8]
            return acc

        acc = lax.fori_loop(0, channels // CHUNK, squares, jnp.zeros((8, lanes_in), F32))
        scale = lax.rsqrt(jnp.sum(acc, axis=0, keepdims=True) * (1.0 / channels) + 1e-06)
        lane = lax.broadcasted_iota(jnp.int32, (CHUNK, row), 1)
        col = lax.rem(lane, cols)
        first, last = col == 0, col == cols - 1
        head = lane < row - cols
        zero = jnp.zeros((), BF16)

        def spread(i, _):
            at = pl.multiple_of(i * CHUNK, CHUNK)
            gain = gain_ref[pl.ds(at, CHUNK), :]
            here = [pl.ds(r * row, row) for r in range(rows_in)]
            values = [xs[pl.ds(at, CHUNK), h].astype(F32) for h in here]
            olds = [buf[pl.ds(slot(0, 1) + at, CHUNK), h] for h in here]
            results = []
            for r in range(rows_in):
                g = values[r] * scale[:, r * row:(r + 1) * row] * gain
                new = (0.5 * g * (1.0 + jnp.tanh(0.5 * g))).astype(BF16)
                mixed = pltpu.roll(jnp.where(head, new, olds[r]), cols, 1)
                for a, v in enumerate((olds[r], mixed, new)):
                    results.append((a, 0, r, jnp.where(first, zero, pltpu.roll(v, 1, 1))))
                    results.append((a, 2, r, jnp.where(last, zero, pltpu.roll(v, row - 1, 1))))
                    if a:
                        results.append((a, 1, r, v))
            for a, c, r, v in results:
                buf[pl.ds(slot(a, c) + at, CHUNK), here[r]] = v
            return 0

        lax.fori_loop(0, channels // CHUNK, spread, 0)
        acts_done = pltpu.make_async_copy(buf.at[pl.ds(slot(2, 1), channels)], acts_ref, sems.at[0])
        acts_done.start()
        step = 2 * row
        top = slab * own - (rows_out - own) // 2

        def taps(n, _):
            at = pl.multiple_of(n * step, step)
            part = xs[:, pl.ds(at + row, step)].astype(F32) + bias_ref[...]
            for b in range(3):
                part = part + jnp.dot(w_ref[b], buf[:, pl.ds(at + b * row, step)], preferred_element_type=F32)
            line = top + 2 * n + lax.broadcasted_iota(jnp.int32, (1, step), 1) // row
            total[:, pl.ds(at, step)] = jnp.where(
                jnp.logical_and(line >= 0, line < height), part, 0.0).astype(BF16)
            return 0

        lax.fori_loop(0, lanes_out // step, taps, 0)
        out_done = pltpu.make_async_copy(total, out_ref, sems.at[1])
        out_done.start()
        acts_done.wait()
        out_done.wait()


def layer_call(cases, rows_in, own, cols, block, height, place, fixed, ins, back=None):
    weight, bias, gain = fixed
    channels = weight.shape[1]
    row = block * cols
    return pl.pallas_call(
        functools.partial(layer_kernel, cases, rows_in, own, cols, block, height, len(ins), back),
        out_shape=(
            jax.ShapeDtypeStruct((channels, (rows_in - 2) * row), BF16),
            jax.ShapeDtypeStruct((channels, rows_in * row), BF16),
            jax.ShapeDtypeStruct(weight.shape, weight.dtype),
            jax.ShapeDtypeStruct(bias.shape, bias.dtype),
            jax.ShapeDtypeStruct(gain.shape, gain.dtype),
        ),
        in_specs=[SMEM, VMEM, VMEM, VMEM] + [ANY] * len(ins),
        out_specs=(ANY, ANY, VMEM, VMEM, VMEM),
        input_output_aliases={1: 2, 2: 3, 3: 4},
        scratch_shapes=[
            pltpu.VMEM((channels, rows_in * row), BF16),
            pltpu.VMEM((9 * channels, rows_in * row), BF16),
            pltpu.VMEM((channels, (rows_in - 2) * row), BF16),
            pltpu.SemaphoreType.DMA((8,)),
        ],
        compiler_params=pltpu.CompilerParams(vmem_limit_bytes=VMEM_BYTES),
        cost_estimate=pl.CostEstimate(
            flops=2 * (rows_in - 2) * row * 27 * channels * channels, bytes_accessed=0, transcendentals=0),
    )(place, weight, bias, gain, *ins)


def local(segments, slabs, video_in, cache_in, conv_weight, conv_bias, norm_gain):
    frames, own, cols, channels = video_in.shape
    height = own * slabs
    segment = lax.axis_index("segment")
    slab = lax.axis_index("slab")
    axes = ("segment", "slab")
    block = frames // segments
    row = block * cols
    blocks = frames // block
    place = jnp.stack([segment, slab]).astype(jnp.int32)
    evens = range(0, segments, 2)
    odds = range(1, segments, 2)

    def moved(value, pairs, step):
        return lax.ppermute(value, axes, [
            (a * slabs + s, b * slabs + s + step) for a, b in pairs for s in range(slabs) if 0 <= s + step < slabs])

    def lanes(value):
        value = value.reshape(-1, block, own, cols, channels)
        return value.transpose(0, 4, 2, 1, 3).reshape(-1, channels, own * row)

    first = lanes(jnp.concatenate([cache_in[0], video_in[:block]], axis=0))
    first_below = moved(first[..., :2 * row], [(g, g) for g in evens], -1)
    first_above = moved(first[..., (own - 2) * row:], [(g, g) for g in evens], 1)
    place, weight = lax.optimization_barrier((place, conv_weight[0]))
    cuts = ((1, (own - 1) * row, row), (1, 0, row))
    weight, bias, gain, later, odd_last, odd_first = turned_weights(
        weight, conv_bias, norm_gain, lanes(video_in[block:]), first, cuts)
    odd_above = moved(odd_last, [(g, g) for g in odds], 1)
    odd_below = moved(odd_first, [(g, g) for g in odds], -1)
    later_below = moved(later[..., :2 * row], [(0, 0)], -1)
    fixed = (weight, bias, gain)

    call = functools.partial(layer_call, own=own, cols=cols, block=block, height=height, place=place)
    across = [(g, g ^ 1) for g in range(segments)]
    hop = [(g, g + 1) for g in odds if g + 1 < segments]
    planes = segments // 2
    arrived, done = [], []
    even_acts = odd_acts = None
    even_cache, odd_cache = [None] * planes, [None] * planes
    ticks = blocks + LAG * (planes - 1)
    for tick in range(ticks):
        busy = [p for p in range(planes) if 0 <= tick - LAG * p < blocks]
        ins = [first, first_above, first_below]
        old = [(1, 0, 0, 2), (0, 0, 0, own), (2, 0, 0, 2)]
        if tick:
            ins.append(even_acts)
            kept = [(3, None, 0, own + 4)]
        cases = []
        for p in busy:
            b = tick - LAG * p
            if p == 0 and b == 0:
                parts = [(1, 1, 0, 2), (0, 1, 0, own), (2, 1, 0, 2)]
            else:
                n = len(ins)
                if p == 0:
                    ins += [later, later_above, later_below]
                    parts = [(n + 1, b - 1, 0, 2), (n, b - 1, 0, own), (n + 2, b - 1, 0, 2)]
                else:
                    ins += list(arrived[b])
                    parts = [(n + 1, None, 0, 2), (n, None, 0, own), (n + 2, None, 0, 2)]
            cases.append((2 * p, parts, old if b == 0 else kept))
        if tick == 0:
            ins += [odd_above, odd_below]
        back = None
        if tick == ticks - 1:
            back = (segments - 1, len(ins))
            ins.append(done[-1])
        out, even_acts, *fixed = call(cases, own + 4, fixed=fixed, ins=ins, back=back)
        sent = list(arrived[tick - 1]) if 0 < tick <= blocks else []
        if tick == 0:
            sent = [later_below]
        elif tick == ticks - 1:
            sent = done[:-1]
        out, *sent = lax.optimization_barrier((out, *sent))
        if tick == 0:
            later_below, = sent
        elif tick == ticks - 1:
            done[:-1] = sent
        elif tick <= blocks:
            arrived[tick - 1] = sent
        crossed = moved(out, across, 0)
        if tick == 0:
            crossed, above = lax.optimization_barrier((crossed, later[..., (own - 2) * row:]))
            later_above = moved(above, [(0, 0)], 1)
        if tick == ticks - 1:
            done[-1] = crossed[:, :own * row]

        ins = [crossed, first, odd_above, odd_below]
        old = [(2, 0, 0, 1), (1, 0, 0, own), (3, 0, 0, 1)]
        if tick:
            ins.append(odd_acts)
        cases = [(2 * p + 1, [(0, None, 0, own + 2)], old if tick == LAG * p else [(4, None, 0, own + 2)]) for p in busy]
        out, odd_acts, *fixed = call(cases, own + 2, fixed=fixed, ins=ins)
        if tick < blocks:
            arrived.append((moved(out, hop, 0), moved(out[:, (own - 2) * row:], hop, 1), moved(out[:, :2 * row], hop, -1)))
        b = tick - LAG * (planes - 1)
        if 0 <= b < blocks:
            done.append(out)
            if b == segments - 2:
                done = list(lax.optimization_barrier(tuple(done)))
                done[:-1] = [moved(d, [(segments - 1, k)], 0) for k, d in enumerate(done[:-1])]
        for p in busy:
            if tick - LAG * p == blocks - 1:
                even_cache[p] = even_acts[:, 2 * row:(2 + own) * row]
                odd_cache[p] = odd_acts[:, row:(1 + own) * row]

    def natural(value):
        return value.reshape(channels, own, block, cols).transpose(2, 1, 3, 0)

    result, segment = lax.optimization_barrier((done[-1], segment))
    for b in range(blocks - 1):
        result = jnp.where(segment == b, done[b], result)
    cache = odd_cache[-1]
    for p in range(planes):
        cache = jnp.where(segment == 2 * p, even_cache[p], cache)
        cache = jnp.where(segment == 2 * p + 1, odd_cache[p], cache)
    return natural(result), natural(cache)[None]


def solution(mesh):
    segments, slabs = mesh.shape["segment"], mesh.shape["slab"]
    return jax.shard_map(
        functools.partial(local, segments, slabs),
        mesh=mesh,
        in_specs=(
            P(None, "slab", None, None),
            P("segment", None, "slab", None, None),
            P("segment", None, None, None, None, None),
            P("segment", None),
            P("segment", None),
        ),
        out_specs=(P("segment", "slab", None, None), P("segment", None, "slab", None, None)),
        check_vma=False,
    )
```

```python
import functools
import jax
import jax.numpy as jnp
from jax import lax
from jax.experimental import pallas as pl
from jax.experimental.pallas import tpu as pltpu
from jax.sharding import PartitionSpec as P

LAG = 2
CHUNK = 128
VMEM_BYTES = 24 * 2**20
F32 = jnp.float32
BF16 = jnp.bfloat16
ANY = pl.BlockSpec(memory_space=pl.ANY)
VMEM = pl.BlockSpec(memory_space=pltpu.VMEM)
SMEM = pl.BlockSpec(memory_space=pltpu.SMEM)


def turn_kernel(cuts, w_ref, bias_ref, gain_ref, first_ref, *refs):
    out_ref, bias_out, gain_out = refs[2:5]
    refs = refs[7:]
    ws, rows, sems, cut_sems = refs[-4:]
    channels = w_ref.shape[-1]
    copies = [pltpu.make_async_copy(w_ref.at[k // 3, k % 3], ws.at[k], sems.at[k]) for k in range(9)]
    vectors = [pltpu.make_async_copy(ref, rows.at[pl.ds(k, 1)], sems.at[9 + k])
               for k, ref in enumerate((bias_ref, gain_ref))]
    parts = [pltpu.make_async_copy(first_ref.at[pl.ds(0, n), :, pl.ds(at, width)], refs[k], cut_sems.at[k])
             for k, (n, at, width) in enumerate(cuts)]
    for copy in vectors + copies + parts:
        copy.start()
    for k, copy in enumerate(copies):
        copy.wait()
        for c in range(3):
            out_ref[k % 3, :, pl.ds((k // 3 * 3 + c) * channels, channels)] = jnp.transpose(ws[k, c], (1, 0))
    for copy in vectors + parts:
        copy.wait()
    turned = jnp.transpose(rows[...], (1, 0))
    bias_out[...] = turned[:, 0:1]
    gain_out[...] = turned[:, 1:2]


def turned_weights(weight, bias, gain, first, later, cuts):
    channels = weight.shape[-1]
    return pl.pallas_call(
        functools.partial(turn_kernel, cuts),
        out_shape=(
            jax.ShapeDtypeStruct((3, channels, 9 * channels), BF16),
            jax.ShapeDtypeStruct((channels, 1), F32),
            jax.ShapeDtypeStruct((channels, 1), F32),
            *(jax.ShapeDtypeStruct(v.shape, v.dtype) for v in later),
            *(jax.ShapeDtypeStruct((n, channels, width), BF16) for n, _, width in cuts),
        ),
        in_specs=[pl.BlockSpec(memory_space=pltpu.HBM)] * 3 + [ANY] * 3,
        out_specs=(VMEM, VMEM, VMEM, ANY, ANY) + (ANY,) * len(cuts),
        input_output_aliases={4: 3, 5: 4},
        scratch_shapes=[
            pltpu.VMEM((9, 3, channels, channels), BF16),
            pltpu.VMEM((8, channels), F32),
            pltpu.SemaphoreType.DMA((11,)),
            pltpu.SemaphoreType.DMA((len(cuts),)),
        ],
        compiler_params=pltpu.CompilerParams(vmem_limit_bytes=VMEM_BYTES),
        cost_estimate=pl.CostEstimate(flops=0, bytes_accessed=4 * weight.size, transcendentals=0),
    )(*(pltpu.with_memory_space_constraint(v, pltpu.HBM) for v in (weight, bias, gain)), first, *later)


def layer_kernel(cases, rows_in, own, cols, block, height, n_in, back, place_ref, w_ref, bias_ref, gain_ref, *refs):
    ins = refs[:n_in]
    out_ref, acts_ref = refs[n_in:n_in + 2]
    xs, buf, total, sems = refs[n_in + 5:]
    channels = xs.shape[0]
    row = block * cols
    rows_out = rows_in - 2
    lanes_in, lanes_out = rows_in * row, rows_out * row
    segment, slab = place_ref[0], place_ref[1]

    def slot(a, c):
        return (3 * a + c) * channels

    def source(part):
        at, index = part[0], part[1]
        return ins[at] if index is None else ins[at].at[index]

    active = functools.reduce(jnp.logical_or, [segment == g for g, _, _ in cases])
    if back is not None:
        @pl.when(segment == back[0])
        def _():
            copy = pltpu.make_async_copy(ins[back[1]], out_ref.at[:, pl.ds(0, ins[back[1]].shape[1])], sems.at[0])
            copy.start()
            copy.wait()

    for g, x_parts, before in cases:
        @pl.when(segment == g)
        def _():
            copies = []
            for parts, target in ((x_parts, xs), (before, buf.at[pl.ds(slot(0, 1), channels)])):
                at = 0
                for part in parts:
                    src = source(part)
                    width = part[3] * row
                    copies.append(pltpu.make_async_copy(
                        src.at[:, pl.ds(part[2] * row, width)], target.at[:, pl.ds(at, width)],
                        sems.at[len(copies)]))
                    at += width
            for c in copies:
                c.start()
            for c in copies:
                c.wait()

    @pl.when(active)
    def _():
        def squares(i, acc):
            v = xs[pl.ds(pl.multiple_of(i * CHUNK, CHUNK), CHUNK), :].astype(F32)
            v = v * v
            for k in range(0, CHUNK, 8):
                acc = acc + v[k:k + 8]
            return acc

        acc = lax.fori_loop(0, channels // CHUNK, squares, jnp.zeros((8, lanes_in), F32))
        scale = lax.rsqrt(jnp.sum(acc, axis=0, keepdims=True) * (1.0 / channels) + 1e-06)
        lane = lax.broadcasted_iota(jnp.int32, (CHUNK, row), 1)
        col = lax.rem(lane, cols)
        first, last = col == 0, col == cols - 1
        head = lane < row - cols
        zero = jnp.zeros((), BF16)

        def spread(i, _):
            at = pl.multiple_of(i * CHUNK, CHUNK)
            gain = gain_ref[pl.ds(at, CHUNK), :]
            here = [pl.ds(r * row, row) for r in range(rows_in)]
            values = [xs[pl.ds(at, CHUNK), h].astype(F32) for h in here]
            olds = [buf[pl.ds(slot(0, 1) + at, CHUNK), h] for h in here]
            results = []
            for r in range(rows_in):
                g = values[r] * scale[:, r * row:(r + 1) * row] * gain
                new = (0.5 * g * (1.0 + jnp.tanh(0.5 * g))).astype(BF16)
                mixed = pltpu.roll(jnp.where(head, new, olds[r]), cols, 1)
                for a, v in enumerate((olds[r], mixed, new)):
                    results.append((a, 0, r, jnp.where(first, zero, pltpu.roll(v, 1, 1))))
                    results.append((a, 2, r, jnp.where(last, zero, pltpu.roll(v, row - 1, 1))))
                    if a:
                        results.append((a, 1, r, v))
            for a, c, r, v in results:
                buf[pl.ds(slot(a, c) + at, CHUNK), here[r]] = v
            return 0

        lax.fori_loop(0, channels // CHUNK, spread, 0)
        acts_done = pltpu.make_async_copy(buf.at[pl.ds(slot(2, 1), channels)], acts_ref, sems.at[0])
        acts_done.start()
        step = 2 * row
        top = slab * own - (rows_out - own) // 2

        def taps(n, _):
            at = pl.multiple_of(n * step, step)
            part = xs[:, pl.ds(at + row, step)].astype(F32) + bias_ref[...]
            for b in range(3):
                part = part + jnp.dot(w_ref[b], buf[:, pl.ds(at + b * row, step)], preferred_element_type=F32)
            line = top + 2 * n + lax.broadcasted_iota(jnp.int32, (1, step), 1) // row
            total[:, pl.ds(at, step)] = jnp.where(
                jnp.logical_and(line >= 0, line < height), part, 0.0).astype(BF16)
            return 0

        lax.fori_loop(0, lanes_out // step, taps, 0)
        out_done = pltpu.make_async_copy(total, out_ref, sems.at[1])
        out_done.start()
        acts_done.wait()
        out_done.wait()


def layer_call(cases, rows_in, own, cols, block, height, place, fixed, ins, back=None):
    weight, bias, gain = fixed
    channels = weight.shape[1]
    row = block * cols
    return pl.pallas_call(
        functools.partial(layer_kernel, cases, rows_in, own, cols, block, height, len(ins), back),
        out_shape=(
            jax.ShapeDtypeStruct((channels, (rows_in - 2) * row), BF16),
            jax.ShapeDtypeStruct((channels, rows_in * row), BF16),
            jax.ShapeDtypeStruct(weight.shape, weight.dtype),
            jax.ShapeDtypeStruct(bias.shape, bias.dtype),
            jax.ShapeDtypeStruct(gain.shape, gain.dtype),
        ),
        in_specs=[SMEM, VMEM, VMEM, VMEM] + [ANY] * len(ins),
        out_specs=(ANY, ANY, VMEM, VMEM, VMEM),
        input_output_aliases={1: 2, 2: 3, 3: 4},
        scratch_shapes=[
            pltpu.VMEM((channels, rows_in * row), BF16),
            pltpu.VMEM((9 * channels, rows_in * row), BF16),
            pltpu.VMEM((channels, (rows_in - 2) * row), BF16),
            pltpu.SemaphoreType.DMA((8,)),
        ],
        compiler_params=pltpu.CompilerParams(vmem_limit_bytes=VMEM_BYTES),
        cost_estimate=pl.CostEstimate(
            flops=2 * (rows_in - 2) * row * 27 * channels * channels, bytes_accessed=0, transcendentals=0),
    )(place, weight, bias, gain, *ins)


def local(segments, slabs, video_in, cache_in, conv_weight, conv_bias, norm_gain):
    frames, own, cols, channels = video_in.shape
    height = own * slabs
    segment = lax.axis_index("segment")
    slab = lax.axis_index("slab")
    axes = ("segment", "slab")
    block = frames // segments
    row = block * cols
    blocks = frames // block
    place = jnp.stack([segment, slab]).astype(jnp.int32)
    evens = range(0, segments, 2)
    odds = range(1, segments, 2)

    def moved(value, pairs, step):
        return lax.ppermute(value, axes, [
            (a * slabs + s, b * slabs + s + step) for a, b in pairs for s in range(slabs) if 0 <= s + step < slabs])

    def lanes(value):
        value = value.reshape(-1, block, own, cols, channels)
        return value.transpose(0, 4, 2, 1, 3).reshape(-1, channels, own * row)

    first = lanes(jnp.concatenate([cache_in[0], video_in[:block]], axis=0))
    first_below = moved(first[..., :2 * row], [(g, g) for g in evens], -1)
    first_above = moved(first[..., (own - 2) * row:], [(g, g) for g in evens], 1)
    place, weight = lax.optimization_barrier((place, conv_weight[0]))
    cuts = ((1, (own - 1) * row, row), (1, 0, row))
    weight, bias, gain, second, later, odd_last, odd_first = turned_weights(
        weight, conv_bias, norm_gain, first, (lanes(video_in[block:2 * block]), lanes(video_in[2 * block:])), cuts)
    odd_above = moved(odd_last, [(g, g) for g in odds], 1)
    odd_below = moved(odd_first, [(g, g) for g in odds], -1)
    second_below, later_below = (moved(v[..., :2 * row], [(0, 0)], -1) for v in (second, later))
    second_above, later_above = (moved(v[..., (own - 2) * row:], [(0, 0)], 1) for v in (second, later))
    fixed = (weight, bias, gain)

    call = functools.partial(layer_call, own=own, cols=cols, block=block, height=height, place=place)
    across = [(g, g ^ 1) for g in range(segments)]
    hop = [(g, g + 1) for g in odds if g + 1 < segments]
    planes = segments // 2
    arrived, done = [], []
    even_acts = odd_acts = None
    even_cache, odd_cache = [None] * planes, [None] * planes
    ticks = blocks + LAG * (planes - 1)
    for tick in range(ticks):
        busy = [p for p in range(planes) if 0 <= tick - LAG * p < blocks]
        ins = [first, first_above, first_below]
        old = [(1, 0, 0, 2), (0, 0, 0, own), (2, 0, 0, 2)]
        if tick:
            ins.append(even_acts)
            kept = [(3, None, 0, own + 4)]
        cases = []
        for p in busy:
            b = tick - LAG * p
            if p == 0 and b == 0:
                parts = [(1, 1, 0, 2), (0, 1, 0, own), (2, 1, 0, 2)]
            else:
                n = len(ins)
                if p == 0:
                    ins += [second, second_above, second_below] if b == 1 else [later, later_above, later_below]
                    k = max(b - 2, 0)
                    parts = [(n + 1, k, 0, 2), (n, k, 0, own), (n + 2, k, 0, 2)]
                else:
                    ins += list(arrived[b])
                    parts = [(n + 1, None, 0, 2), (n, None, 0, own), (n + 2, None, 0, 2)]
            cases.append((2 * p, parts, old if b == 0 else kept))
        if tick == 0:
            ins += [odd_above, odd_below]
        back = None
        if tick == ticks - 1:
            back = (segments - 1, len(ins))
            ins.append(done[-1])
        out, even_acts, *fixed = call(cases, own + 4, fixed=fixed, ins=ins, back=back)
        sent = list(arrived[tick - 1]) if 0 < tick <= blocks else []
        sent += [(second_below, second_above), (later_below, later_above)][tick] if tick < 2 else []
        final = done[-1:] if tick < ticks - 1 else []
        out, *sent = lax.optimization_barrier((out, *sent, *final))
        if final:
            done[-1] = sent.pop()
        if tick == 0:
            second_below, second_above = sent
        elif tick <= blocks:
            arrived[tick - 1] = sent[:3]
        if tick == 1:
            later_below, later_above = sent[3:]
        crossed = moved(out, across, 0)
        if tick == ticks - 1:
            done[-1] = crossed[:, :own * row]

        ins = [crossed, first, odd_above, odd_below]
        old = [(2, 0, 0, 1), (1, 0, 0, own), (3, 0, 0, 1)]
        if tick:
            ins.append(odd_acts)
        cases = [(2 * p + 1, [(0, None, 0, own + 2)], old if tick == LAG * p else [(4, None, 0, own + 2)]) for p in busy]
        out, odd_acts, *fixed = call(cases, own + 2, fixed=fixed, ins=ins)
        if tick < blocks:
            arrived.append((moved(out, hop, 0), moved(out[:, (own - 2) * row:], hop, 1), moved(out[:, :2 * row], hop, -1)))
        b = tick - LAG * (planes - 1)
        if 0 <= b < blocks:
            done.append(out if b >= segments - 2 else moved(out, [(segments - 1, b)], 0))
        for p in busy:
            if tick - LAG * p == blocks - 1:
                even_cache[p] = even_acts[:, 2 * row:(2 + own) * row]
                odd_cache[p] = odd_acts[:, row:(1 + own) * row]

    def natural(value):
        return value.reshape(channels, own, block, cols).transpose(2, 1, 3, 0)

    result, segment = lax.optimization_barrier((done[-1], segment))
    for b in range(blocks - 1):
        result = jnp.where(segment == b, done[b], result)
    cache = odd_cache[-1]
    for p in range(planes):
        cache = jnp.where(segment == 2 * p, even_cache[p], cache)
        cache = jnp.where(segment == 2 * p + 1, odd_cache[p], cache)
    return natural(result), natural(cache)[None]


def solution(mesh):
    segments, slabs = mesh.shape["segment"], mesh.shape["slab"]
    return jax.shard_map(
        functools.partial(local, segments, slabs),
        mesh=mesh,
        in_specs=(
            P(None, "slab", None, None),
            P("segment", None, "slab", None, None),
            P("segment", None, None, None, None, None),
            P("segment", None),
            P("segment", None),
        ),
        out_specs=(P("segment", "slab", None, None), P("segment", None, "slab", None, None)),
        check_vma=False,
    )
```

```python
import functools
import jax
import jax.numpy as jnp
from jax import lax
from jax.experimental import pallas as pl
from jax.experimental.pallas import tpu as pltpu
from jax.sharding import PartitionSpec as P

LAG = 2
CHUNK = 128
VMEM_BYTES = 24 * 2**20
F32 = jnp.float32
BF16 = jnp.bfloat16
ANY = pl.BlockSpec(memory_space=pl.ANY)
VMEM = pl.BlockSpec(memory_space=pltpu.VMEM)
SMEM = pl.BlockSpec(memory_space=pltpu.SMEM)


def turn_kernel(cuts, w_ref, bias_ref, gain_ref, later_ref, first_ref, out_ref, bias_out, gain_out, _, *refs):
    ws, rows, sems, cut_sems = refs[-4:]
    channels = w_ref.shape[-1]
    copies = [pltpu.make_async_copy(w_ref.at[k // 3, k % 3], ws.at[k], sems.at[k]) for k in range(9)]
    vectors = [pltpu.make_async_copy(ref, rows.at[pl.ds(k, 1)], sems.at[9 + k])
               for k, ref in enumerate((bias_ref, gain_ref))]
    parts = [pltpu.make_async_copy(first_ref.at[pl.ds(0, n), :, pl.ds(at, width)], refs[k], cut_sems.at[k])
             for k, (n, at, width) in enumerate(cuts)]
    for copy in vectors + copies + parts:
        copy.start()
    for k, copy in enumerate(copies):
        copy.wait()
        for c in range(3):
            out_ref[k % 3, :, pl.ds((k // 3 * 3 + c) * channels, channels)] = jnp.transpose(ws[k, c], (1, 0))
    for copy in vectors + parts:
        copy.wait()
    turned = jnp.transpose(rows[...], (1, 0))
    bias_out[...] = turned[:, 0:1]
    gain_out[...] = turned[:, 1:2]


def turned_weights(weight, bias, gain, later, first, cuts):
    channels = weight.shape[-1]
    return pl.pallas_call(
        functools.partial(turn_kernel, cuts),
        out_shape=(
            jax.ShapeDtypeStruct((3, channels, 9 * channels), BF16),
            jax.ShapeDtypeStruct((channels, 1), F32),
            jax.ShapeDtypeStruct((channels, 1), F32),
            jax.ShapeDtypeStruct(later.shape, later.dtype),
            *(jax.ShapeDtypeStruct((n, channels, width), BF16) for n, _, width in cuts),
        ),
        in_specs=[pl.BlockSpec(memory_space=pltpu.HBM)] * 3 + [ANY] * 2,
        out_specs=(VMEM, VMEM, VMEM, ANY) + (ANY,) * len(cuts),
        input_output_aliases={3: 3},
        scratch_shapes=[
            pltpu.VMEM((9, 3, channels, channels), BF16),
            pltpu.VMEM((8, channels), F32),
            pltpu.SemaphoreType.DMA((11,)),
            pltpu.SemaphoreType.DMA((len(cuts),)),
        ],
        compiler_params=pltpu.CompilerParams(vmem_limit_bytes=VMEM_BYTES),
        cost_estimate=pl.CostEstimate(flops=0, bytes_accessed=4 * weight.size, transcendentals=0),
    )(*(pltpu.with_memory_space_constraint(v, pltpu.HBM) for v in (weight, bias, gain)), later, first)


def layer_kernel(cases, rows_in, own, cols, block, height, n_in, back, place_ref, w_ref, bias_ref, gain_ref, *refs):
    ins = refs[:n_in]
    out_ref, acts_ref = refs[n_in:n_in + 2]
    xs, buf, total, sems = refs[n_in + 5:]
    channels = xs.shape[0]
    row = block * cols
    rows_out = rows_in - 2
    lanes_in, lanes_out = rows_in * row, rows_out * row
    segment, slab = place_ref[0], place_ref[1]

    def slot(a, c):
        return (3 * a + c) * channels

    def source(part):
        at, index = part[0], part[1]
        return ins[at] if index is None else ins[at].at[index]

    active = functools.reduce(jnp.logical_or, [segment == g for g, _, _ in cases])
    if back is not None:
        @pl.when(segment == back[0])
        def _():
            copy = pltpu.make_async_copy(ins[back[1]], out_ref.at[:, pl.ds(0, ins[back[1]].shape[1])], sems.at[0])
            copy.start()
            copy.wait()

    for g, x_parts, before in cases:
        @pl.when(segment == g)
        def _():
            copies = []
            for parts, target in ((x_parts, xs), (before, buf.at[pl.ds(slot(0, 1), channels)])):
                at = 0
                for part in parts:
                    src = source(part)
                    width = part[3] * row
                    copies.append(pltpu.make_async_copy(
                        src.at[:, pl.ds(part[2] * row, width)], target.at[:, pl.ds(at, width)],
                        sems.at[len(copies)]))
                    at += width
            for c in copies:
                c.start()
            for c in copies:
                c.wait()

    @pl.when(active)
    def _():
        def squares(i, acc):
            v = xs[pl.ds(pl.multiple_of(i * CHUNK, CHUNK), CHUNK), :].astype(F32)
            v = v * v
            for k in range(0, CHUNK, 8):
                acc = acc + v[k:k + 8]
            return acc

        acc = lax.fori_loop(0, channels // CHUNK, squares, jnp.zeros((8, lanes_in), F32))
        scale = lax.rsqrt(jnp.sum(acc, axis=0, keepdims=True) * (1.0 / channels) + 1e-06)
        lane = lax.broadcasted_iota(jnp.int32, (CHUNK, row), 1)
        col = lax.rem(lane, cols)
        first, last = col == 0, col == cols - 1
        head = lane < row - cols
        zero = jnp.zeros((), BF16)

        def spread(i, _):
            at = pl.multiple_of(i * CHUNK, CHUNK)
            gain = gain_ref[pl.ds(at, CHUNK), :]
            here = [pl.ds(r * row, row) for r in range(rows_in)]
            values = [xs[pl.ds(at, CHUNK), h].astype(F32) for h in here]
            olds = [buf[pl.ds(slot(0, 1) + at, CHUNK), h] for h in here]
            results = []
            for r in range(rows_in):
                g = values[r] * scale[:, r * row:(r + 1) * row] * gain
                new = (0.5 * g * (1.0 + jnp.tanh(0.5 * g))).astype(BF16)
                mixed = pltpu.roll(jnp.where(head, new, olds[r]), cols, 1)
                for a, v in enumerate((olds[r], mixed, new)):
                    results.append((a, 0, r, jnp.where(first, zero, pltpu.roll(v, 1, 1))))
                    results.append((a, 2, r, jnp.where(last, zero, pltpu.roll(v, row - 1, 1))))
                    if a:
                        results.append((a, 1, r, v))
            for a, c, r, v in results:
                buf[pl.ds(slot(a, c) + at, CHUNK), here[r]] = v
            return 0

        lax.fori_loop(0, channels // CHUNK, spread, 0)
        acts_done = pltpu.make_async_copy(buf.at[pl.ds(slot(2, 1), channels)], acts_ref, sems.at[0])
        acts_done.start()
        step = 2 * row
        top = slab * own - (rows_out - own) // 2

        def taps(n, _):
            at = pl.multiple_of(n * step, step)
            part = xs[:, pl.ds(at + row, step)].astype(F32) + bias_ref[...]
            for b in range(3):
                part = part + jnp.dot(w_ref[b], buf[:, pl.ds(at + b * row, step)], preferred_element_type=F32)
            line = top + 2 * n + lax.broadcasted_iota(jnp.int32, (1, step), 1) // row
            total[:, pl.ds(at, step)] = jnp.where(
                jnp.logical_and(line >= 0, line < height), part, 0.0).astype(BF16)
            return 0

        lax.fori_loop(0, lanes_out // step, taps, 0)
        out_done = pltpu.make_async_copy(total, out_ref, sems.at[1])
        out_done.start()
        acts_done.wait()
        out_done.wait()


def layer_call(cases, rows_in, own, cols, block, height, place, fixed, ins, back=None):
    weight, bias, gain = fixed
    channels = weight.shape[1]
    row = block * cols
    return pl.pallas_call(
        functools.partial(layer_kernel, cases, rows_in, own, cols, block, height, len(ins), back),
        out_shape=(
            jax.ShapeDtypeStruct((channels, (rows_in - 2) * row), BF16),
            jax.ShapeDtypeStruct((channels, rows_in * row), BF16),
            jax.ShapeDtypeStruct(weight.shape, weight.dtype),
            jax.ShapeDtypeStruct(bias.shape, bias.dtype),
            jax.ShapeDtypeStruct(gain.shape, gain.dtype),
        ),
        in_specs=[SMEM, VMEM, VMEM, VMEM] + [ANY] * len(ins),
        out_specs=(ANY, ANY, VMEM, VMEM, VMEM),
        input_output_aliases={1: 2, 2: 3, 3: 4},
        scratch_shapes=[
            pltpu.VMEM((channels, rows_in * row), BF16),
            pltpu.VMEM((9 * channels, rows_in * row), BF16),
            pltpu.VMEM((channels, (rows_in - 2) * row), BF16),
            pltpu.SemaphoreType.DMA((8,)),
        ],
        compiler_params=pltpu.CompilerParams(vmem_limit_bytes=VMEM_BYTES),
        cost_estimate=pl.CostEstimate(
            flops=2 * (rows_in - 2) * row * 27 * channels * channels, bytes_accessed=0, transcendentals=0),
    )(place, weight, bias, gain, *ins)


def local(segments, slabs, video_in, cache_in, conv_weight, conv_bias, norm_gain):
    frames, own, cols, channels = video_in.shape
    height = own * slabs
    segment = lax.axis_index("segment")
    slab = lax.axis_index("slab")
    axes = ("segment", "slab")
    block = frames // segments
    row = block * cols
    blocks = frames // block
    place = jnp.stack([segment, slab]).astype(jnp.int32)
    evens = range(0, segments, 2)
    odds = range(1, segments, 2)

    def moved(value, pairs, step):
        return lax.ppermute(value, axes, [
            (a * slabs + s, b * slabs + s + step) for a, b in pairs for s in range(slabs) if 0 <= s + step < slabs])

    def lanes(value):
        value = value.reshape(-1, block, own, cols, channels)
        return value.transpose(0, 4, 2, 1, 3).reshape(-1, channels, own * row)

    first = lanes(jnp.concatenate([cache_in[0], video_in[:block]], axis=0))
    first_below = moved(first[..., :2 * row], [(g, g) for g in evens], -1)
    first_above = moved(first[..., (own - 2) * row:], [(g, g) for g in evens], 1)
    place, weight = lax.optimization_barrier((place, conv_weight[0]))
    cuts = ((1, (own - 1) * row, row), (1, 0, row))
    weight, bias, gain, later, odd_last, odd_first = turned_weights(
        weight, conv_bias, norm_gain, lanes(video_in[block:]), first, cuts)
    odd_above = moved(odd_last, [(g, g) for g in odds], 1)
    odd_below = moved(odd_first, [(g, g) for g in odds], -1)
    later_below = moved(later[..., :2 * row], [(0, 0)], -1)
    later_above = moved(later[..., (own - 2) * row:], [(0, 0)], 1)
    fixed = (weight, bias, gain)

    call = functools.partial(layer_call, own=own, cols=cols, block=block, height=height, place=place)
    across = [(g, g ^ 1) for g in range(segments)]
    hop = [(g, g + 1) for g in odds if g + 1 < segments]
    planes = segments // 2
    arrived, done = [], []
    even_acts = odd_acts = None
    even_cache, odd_cache = [None] * planes, [None] * planes
    ticks = blocks + LAG * (planes - 1)
    for tick in range(ticks):
        busy = [p for p in range(planes) if 0 <= tick - LAG * p < blocks]
        ins = [first, first_above, first_below]
        old = [(1, 0, 0, 2), (0, 0, 0, own), (2, 0, 0, 2)]
        if tick:
            ins.append(even_acts)
            kept = [(3, None, 0, own + 4)]
        cases = []
        for p in busy:
            b = tick - LAG * p
            if p == 0 and b == 0:
                parts = [(1, 1, 0, 2), (0, 1, 0, own), (2, 1, 0, 2)]
            else:
                n = len(ins)
                if p == 0:
                    ins += [later, later_above, later_below]
                    parts = [(n + 1, b - 1, 0, 2), (n, b - 1, 0, own), (n + 2, b - 1, 0, 2)]
                else:
                    ins += list(arrived[b])
                    parts = [(n + 1, None, 0, 2), (n, None, 0, own), (n + 2, None, 0, 2)]
            cases.append((2 * p, parts, old if b == 0 else kept))
        if tick == 0:
            ins += [odd_above, odd_below]
        back = None
        if tick == ticks - 1:
            back = (segments - 1, len(ins))
            ins.append(done[-1])
        out, even_acts, *fixed = call(cases, own + 4, fixed=fixed, ins=ins, back=back)
        sent = list(arrived[tick - 1]) if 0 < tick <= blocks else []
        if tick == ticks - 2:
            sent += [moved(d, [(segments - 1, k)], 0) for k, d in enumerate(done)]
        if sent:
            out, *sent = lax.optimization_barrier((out, *sent))
            arrived[tick - 1] = sent[:3]
        if tick == ticks - 2:
            done = sent[3:]
        crossed = moved(out, across, 0)
        if tick == ticks - 1:
            done[-1] = crossed[:, :own * row]

        ins = [crossed, first, odd_above, odd_below]
        old = [(2, 0, 0, 1), (1, 0, 0, own), (3, 0, 0, 1)]
        if tick:
            ins.append(odd_acts)
        if tick == 0:
            ins += [later_above, later_below]
        cases = [(2 * p + 1, [(0, None, 0, own + 2)], old if tick == LAG * p else [(4, None, 0, own + 2)]) for p in busy]
        out, odd_acts, *fixed = call(cases, own + 2, fixed=fixed, ins=ins)
        if tick < blocks:
            arrived.append((moved(out, hop, 0), moved(out[:, (own - 2) * row:], hop, 1), moved(out[:, :2 * row], hop, -1)))
        b = tick - LAG * (planes - 1)
        if 0 <= b < blocks:
            done.append(out)
        for p in busy:
            if tick - LAG * p == blocks - 1:
                even_cache[p] = even_acts[:, 2 * row:(2 + own) * row]
                odd_cache[p] = odd_acts[:, row:(1 + own) * row]

    def natural(value):
        return value.reshape(channels, own, block, cols).transpose(2, 1, 3, 0)

    result, segment = lax.optimization_barrier((done[-1], segment))
    for b in range(blocks - 1):
        result = jnp.where(segment == b, done[b], result)
    cache = odd_cache[-1]
    for p in range(planes):
        cache = jnp.where(segment == 2 * p, even_cache[p], cache)
        cache = jnp.where(segment == 2 * p + 1, odd_cache[p], cache)
    return natural(result), natural(cache)[None]


def solution(mesh):
    segments, slabs = mesh.shape["segment"], mesh.shape["slab"]
    return jax.shard_map(
        functools.partial(local, segments, slabs),
        mesh=mesh,
        in_specs=(
            P(None, "slab", None, None),
            P("segment", None, "slab", None, None),
            P("segment", None, None, None, None, None),
            P("segment", None),
            P("segment", None),
        ),
        out_specs=(P("segment", "slab", None, None), P("segment", None, "slab", None, None)),
        check_vma=False,
    )
```

```python
import functools
import jax
import jax.numpy as jnp
from jax import lax
from jax.experimental import pallas as pl
from jax.experimental.pallas import tpu as pltpu
from jax.sharding import PartitionSpec as P

LAG = 2
CHUNK = 192
VMEM_BYTES = 24 * 2**20
F32 = jnp.float32
BF16 = jnp.bfloat16
ANY = pl.BlockSpec(memory_space=pl.ANY)
VMEM = pl.BlockSpec(memory_space=pltpu.VMEM)
SMEM = pl.BlockSpec(memory_space=pltpu.SMEM)


def turn_kernel(cuts, w_ref, bias_ref, gain_ref, later_ref, first_ref, out_ref, bias_out, gain_out, _, *refs):
    ws, rows, sems, cut_sems = refs[-4:]
    channels = w_ref.shape[-1]
    copies = [pltpu.make_async_copy(w_ref.at[k // 3, k % 3], ws.at[k], sems.at[k]) for k in range(9)]
    vectors = [pltpu.make_async_copy(ref, rows.at[pl.ds(k, 1)], sems.at[9 + k])
               for k, ref in enumerate((bias_ref, gain_ref))]
    parts = [pltpu.make_async_copy(first_ref.at[pl.ds(0, n), :, pl.ds(at, width)], refs[k], cut_sems.at[k])
             for k, (n, at, width) in enumerate(cuts)]
    for copy in vectors + copies + parts:
        copy.start()
    for k, copy in enumerate(copies):
        copy.wait()
        for c in range(3):
            out_ref[k % 3, :, pl.ds((k // 3 * 3 + c) * channels, channels)] = jnp.transpose(ws[k, c], (1, 0))
    for copy in vectors + parts:
        copy.wait()
    turned = jnp.transpose(rows[...], (1, 0))
    bias_out[...] = turned[:, 0:1]
    gain_out[...] = turned[:, 1:2]


def turned_weights(weight, bias, gain, later, first, cuts):
    channels = weight.shape[-1]
    return pl.pallas_call(
        functools.partial(turn_kernel, cuts),
        out_shape=(
            jax.ShapeDtypeStruct((3, channels, 9 * channels), BF16),
            jax.ShapeDtypeStruct((channels, 1), F32),
            jax.ShapeDtypeStruct((channels, 1), F32),
            jax.ShapeDtypeStruct(later.shape, later.dtype),
            *(jax.ShapeDtypeStruct((n, channels, width), BF16) for n, _, width in cuts),
        ),
        in_specs=[pl.BlockSpec(memory_space=pltpu.HBM)] * 3 + [ANY] * 2,
        out_specs=(VMEM, VMEM, VMEM, ANY) + (ANY,) * len(cuts),
        input_output_aliases={3: 3},
        scratch_shapes=[
            pltpu.VMEM((9, 3, channels, channels), BF16),
            pltpu.VMEM((8, channels), F32),
            pltpu.SemaphoreType.DMA((11,)),
            pltpu.SemaphoreType.DMA((len(cuts),)),
        ],
        compiler_params=pltpu.CompilerParams(vmem_limit_bytes=VMEM_BYTES),
        cost_estimate=pl.CostEstimate(flops=0, bytes_accessed=4 * weight.size, transcendentals=0),
    )(*(pltpu.with_memory_space_constraint(v, pltpu.HBM) for v in (weight, bias, gain)), later, first)


def layer_kernel(cases, rows_in, own, cols, block, height, n_in, back, place_ref, w_ref, bias_ref, gain_ref, *refs):
    ins = refs[:n_in]
    out_ref, acts_ref = refs[n_in:n_in + 2]
    xs, buf, total, sems = refs[n_in + 5:]
    channels = xs.shape[0]
    row = block * cols
    rows_out = rows_in - 2
    lanes_in, lanes_out = rows_in * row, rows_out * row
    segment, slab = place_ref[0], place_ref[1]

    def slot(a, c):
        return (3 * a + c) * channels

    def source(part):
        at, index = part[0], part[1]
        return ins[at] if index is None else ins[at].at[index]

    active = functools.reduce(jnp.logical_or, [segment == g for g, _, _ in cases])
    if back is not None:
        @pl.when(segment == back[0])
        def _():
            copy = pltpu.make_async_copy(ins[back[1]], out_ref.at[:, pl.ds(0, ins[back[1]].shape[1])], sems.at[0])
            copy.start()
            copy.wait()

    for g, x_parts, before in cases:
        @pl.when(segment == g)
        def _():
            copies = []
            for parts, target in ((x_parts, xs), (before, buf.at[pl.ds(slot(0, 1), channels)])):
                at = 0
                for part in parts:
                    src = source(part)
                    width = part[3] * row
                    copies.append(pltpu.make_async_copy(
                        src.at[:, pl.ds(part[2] * row, width)], target.at[:, pl.ds(at, width)],
                        sems.at[len(copies)]))
                    at += width
            for c in copies:
                c.start()
            for c in copies:
                c.wait()

    @pl.when(active)
    def _():
        def squares(i, acc):
            v = xs[pl.ds(pl.multiple_of(i * CHUNK, CHUNK), CHUNK), :].astype(F32)
            v = v * v
            for k in range(0, CHUNK, 8):
                acc = acc + v[k:k + 8]
            return acc

        acc = lax.fori_loop(0, channels // CHUNK, squares, jnp.zeros((8, lanes_in), F32))
        scale = lax.rsqrt(jnp.sum(acc, axis=0, keepdims=True) * (1.0 / channels) + 1e-06)
        lane = lax.broadcasted_iota(jnp.int32, (CHUNK, row), 1)
        col = lax.rem(lane, cols)
        first, last = col == 0, col == cols - 1
        head = lane < row - cols
        zero = jnp.zeros((), BF16)

        def spread(i, _):
            at = pl.multiple_of(i * CHUNK, CHUNK)
            gain = gain_ref[pl.ds(at, CHUNK), :]
            here = [pl.ds(r * row, row) for r in range(rows_in)]
            values = [xs[pl.ds(at, CHUNK), h].astype(F32) for h in here]
            olds = [buf[pl.ds(slot(0, 1) + at, CHUNK), h] for h in here]
            results = []
            for r in range(rows_in):
                g = values[r] * scale[:, r * row:(r + 1) * row] * gain
                new = (0.5 * g * (1.0 + jnp.tanh(0.5 * g))).astype(BF16)
                mixed = pltpu.roll(jnp.where(head, new, olds[r]), cols, 1)
                for a, v in enumerate((olds[r], mixed, new)):
                    results.append((a, 0, r, jnp.where(first, zero, pltpu.roll(v, 1, 1))))
                    results.append((a, 2, r, jnp.where(last, zero, pltpu.roll(v, row - 1, 1))))
                    if a:
                        results.append((a, 1, r, v))
            for a, c, r, v in results:
                buf[pl.ds(slot(a, c) + at, CHUNK), here[r]] = v
            return 0

        lax.fori_loop(0, channels // CHUNK, spread, 0)
        acts_done = pltpu.make_async_copy(buf.at[pl.ds(slot(2, 1), channels)], acts_ref, sems.at[0])
        acts_done.start()
        step = 2 * row
        top = slab * own - (rows_out - own) // 2

        def taps(n, _):
            at = pl.multiple_of(n * step, step)
            part = xs[:, pl.ds(at + row, step)].astype(F32) + bias_ref[...]
            for b in range(3):
                part = part + jnp.dot(w_ref[b], buf[:, pl.ds(at + b * row, step)], preferred_element_type=F32)
            line = top + 2 * n + lax.broadcasted_iota(jnp.int32, (1, step), 1) // row
            total[:, pl.ds(at, step)] = jnp.where(
                jnp.logical_and(line >= 0, line < height), part, 0.0).astype(BF16)
            pltpu.make_async_copy(total.at[:, pl.ds(at, step)], out_ref.at[:, pl.ds(at, step)], sems.at[1]).start()
            return 0

        lax.fori_loop(0, lanes_out // step, taps, 0)
        out_done = pltpu.make_async_copy(total, out_ref, sems.at[1])
        acts_done.wait()
        out_done.wait()


def layer_call(cases, rows_in, own, cols, block, height, place, fixed, ins, back=None):
    weight, bias, gain = fixed
    channels = weight.shape[1]
    row = block * cols
    return pl.pallas_call(
        functools.partial(layer_kernel, cases, rows_in, own, cols, block, height, len(ins), back),
        out_shape=(
            jax.ShapeDtypeStruct((channels, (rows_in - 2) * row), BF16),
            jax.ShapeDtypeStruct((channels, rows_in * row), BF16),
            jax.ShapeDtypeStruct(weight.shape, weight.dtype),
            jax.ShapeDtypeStruct(bias.shape, bias.dtype),
            jax.ShapeDtypeStruct(gain.shape, gain.dtype),
        ),
        in_specs=[SMEM, VMEM, VMEM, VMEM] + [ANY] * len(ins),
        out_specs=(ANY, ANY, VMEM, VMEM, VMEM),
        input_output_aliases={1: 2, 2: 3, 3: 4},
        scratch_shapes=[
            pltpu.VMEM((channels, rows_in * row), BF16),
            pltpu.VMEM((9 * channels, rows_in * row), BF16),
            pltpu.VMEM((channels, (rows_in - 2) * row), BF16),
            pltpu.SemaphoreType.DMA((8,)),
        ],
        compiler_params=pltpu.CompilerParams(vmem_limit_bytes=VMEM_BYTES),
        cost_estimate=pl.CostEstimate(
            flops=2 * (rows_in - 2) * row * 27 * channels * channels, bytes_accessed=0, transcendentals=0),
    )(place, weight, bias, gain, *ins)


def local(segments, slabs, video_in, cache_in, conv_weight, conv_bias, norm_gain):
    frames, own, cols, channels = video_in.shape
    height = own * slabs
    segment = lax.axis_index("segment")
    slab = lax.axis_index("slab")
    axes = ("segment", "slab")
    block = frames // segments
    row = block * cols
    blocks = frames // block
    place = jnp.stack([segment, slab]).astype(jnp.int32)
    evens = range(0, segments, 2)
    odds = range(1, segments, 2)

    def moved(value, pairs, step):
        return lax.ppermute(value, axes, [
            (a * slabs + s, b * slabs + s + step) for a, b in pairs for s in range(slabs) if 0 <= s + step < slabs])

    def lanes(value):
        value = value.reshape(-1, block, own, cols, channels)
        return value.transpose(0, 4, 2, 1, 3).reshape(-1, channels, own * row)

    first = lanes(jnp.concatenate([cache_in[0], video_in[:block]], axis=0))
    first_below = moved(first[..., :2 * row], [(g, g) for g in evens], -1)
    first_above = moved(first[..., (own - 2) * row:], [(g, g) for g in evens], 1)
    place, weight = lax.optimization_barrier((place, conv_weight[0]))
    cuts = ((1, (own - 1) * row, row), (1, 0, row))
    weight, bias, gain, later, odd_last, odd_first = turned_weights(
        weight, conv_bias, norm_gain, lanes(video_in[block:]), first, cuts)
    odd_above = moved(odd_last, [(g, g) for g in odds], 1)
    odd_below = moved(odd_first, [(g, g) for g in odds], -1)
    later_below = moved(later[..., :2 * row], [(0, 0)], -1)
    later_above = moved(later[..., (own - 2) * row:], [(0, 0)], 1)
    fixed = (weight, bias, gain)

    call = functools.partial(layer_call, own=own, cols=cols, block=block, height=height, place=place)
    across = [(g, g ^ 1) for g in range(segments)]
    hop = [(g, g + 1) for g in odds if g + 1 < segments]
    planes = segments // 2
    arrived, done = [], []
    even_acts = odd_acts = None
    even_cache, odd_cache = [None] * planes, [None] * planes
    ticks = blocks + LAG * (planes - 1)
    for tick in range(ticks):
        busy = [p for p in range(planes) if 0 <= tick - LAG * p < blocks]
        ins = [first, first_above, first_below]
        old = [(1, 0, 0, 2), (0, 0, 0, own), (2, 0, 0, 2)]
        if tick:
            ins.append(even_acts)
            kept = [(3, None, 0, own + 4)]
        cases = []
        for p in busy:
            b = tick - LAG * p
            if p == 0 and b == 0:
                parts = [(1, 1, 0, 2), (0, 1, 0, own), (2, 1, 0, 2)]
            else:
                n = len(ins)
                if p == 0:
                    ins += [later, later_above, later_below]
                    parts = [(n + 1, b - 1, 0, 2), (n, b - 1, 0, own), (n + 2, b - 1, 0, 2)]
                else:
                    ins += list(arrived[b])
                    parts = [(n + 1, None, 0, 2), (n, None, 0, own), (n + 2, None, 0, 2)]
            cases.append((2 * p, parts, old if b == 0 else kept))
        if tick == 0:
            ins += [odd_above, odd_below]
        back = None
        if tick == ticks - 1:
            back = (segments - 1, len(ins))
            ins.append(done[-1])
        out, even_acts, *fixed = call(cases, own + 4, fixed=fixed, ins=ins, back=back)
        sent = list(arrived[tick - 1]) if 0 < tick <= blocks else []
        if tick == ticks - 2:
            sent += [moved(d, [(segments - 1, k)], 0) for k, d in enumerate(done)]
        if sent:
            out, *sent = lax.optimization_barrier((out, *sent))
            arrived[tick - 1] = sent[:3]
        if tick == ticks - 2:
            done = sent[3:]
        crossed = moved(out, across, 0)
        if tick == ticks - 1:
            done[-1] = crossed[:, :own * row]

        ins = [crossed, first, odd_above, odd_below]
        old = [(2, 0, 0, 1), (1, 0, 0, own), (3, 0, 0, 1)]
        if tick:
            ins.append(odd_acts)
        if tick == 0:
            ins += [later_above, later_below]
        cases = [(2 * p + 1, [(0, None, 0, own + 2)], old if tick == LAG * p else [(4, None, 0, own + 2)]) for p in busy]
        out, odd_acts, *fixed = call(cases, own + 2, fixed=fixed, ins=ins)
        if tick < blocks:
            arrived.append((moved(out, hop, 0), moved(out[:, (own - 2) * row:], hop, 1), moved(out[:, :2 * row], hop, -1)))
        b = tick - LAG * (planes - 1)
        if 0 <= b < blocks:
            done.append(out)
        for p in busy:
            if tick - LAG * p == blocks - 1:
                even_cache[p] = even_acts[:, 2 * row:(2 + own) * row]
                odd_cache[p] = odd_acts[:, row:(1 + own) * row]

    def natural(value):
        return value.reshape(channels, own, block, cols).transpose(2, 1, 3, 0)

    result, segment = lax.optimization_barrier((done[-1], segment))
    for b in range(blocks - 1):
        result = jnp.where(segment == b, done[b], result)
    cache = odd_cache[-1]
    for p in range(planes):
        cache = jnp.where(segment == 2 * p, even_cache[p], cache)
        cache = jnp.where(segment == 2 * p + 1, odd_cache[p], cache)
    return natural(result), natural(cache)[None]


def solution(mesh):
    segments, slabs = mesh.shape["segment"], mesh.shape["slab"]
    return jax.shard_map(
        functools.partial(local, segments, slabs),
        mesh=mesh,
        in_specs=(
            P(None, "slab", None, None),
            P("segment", None, "slab", None, None),
            P("segment", None, None, None, None, None),
            P("segment", None),
            P("segment", None),
        ),
        out_specs=(P("segment", "slab", None, None), P("segment", None, "slab", None, None)),
        check_vma=False,
    )
```

```python
import functools
import jax
import jax.numpy as jnp
from jax import lax
from jax.experimental import pallas as pl
from jax.experimental.pallas import tpu as pltpu
from jax.sharding import PartitionSpec as P

LAG = 2
CHUNK = 192
VMEM_BYTES = 24 * 2**20
F32 = jnp.float32
BF16 = jnp.bfloat16
ANY = pl.BlockSpec(memory_space=pl.ANY)
VMEM = pl.BlockSpec(memory_space=pltpu.VMEM)
SMEM = pl.BlockSpec(memory_space=pltpu.SMEM)


def turn_kernel(cuts, w_ref, bias_ref, gain_ref, later_ref, first_ref, out_ref, bias_out, gain_out, _, *refs):
    ws, rows, sems, cut_sems = refs[-4:]
    channels = w_ref.shape[-1]
    copies = [pltpu.make_async_copy(w_ref.at[k // 3, k % 3], ws.at[k], sems.at[k]) for k in range(9)]
    vectors = [pltpu.make_async_copy(ref, rows.at[pl.ds(k, 1)], sems.at[9 + k])
               for k, ref in enumerate((bias_ref, gain_ref))]
    parts = [pltpu.make_async_copy(first_ref.at[pl.ds(0, n), :, pl.ds(at, width)], refs[k], cut_sems.at[k])
             for k, (n, at, width) in enumerate(cuts)]
    for copy in vectors + copies + parts:
        copy.start()
    for k, copy in enumerate(copies):
        copy.wait()
        for c in range(3):
            out_ref[k % 3, :, pl.ds((k // 3 * 3 + c) * channels, channels)] = jnp.transpose(ws[k, c], (1, 0))
    for copy in vectors + parts:
        copy.wait()
    turned = jnp.transpose(rows[...], (1, 0))
    bias_out[...] = turned[:, 0:1]
    gain_out[...] = turned[:, 1:2]


def turned_weights(weight, bias, gain, later, first, cuts):
    channels = weight.shape[-1]
    return pl.pallas_call(
        functools.partial(turn_kernel, cuts),
        out_shape=(
            jax.ShapeDtypeStruct((3, channels, 9 * channels), BF16),
            jax.ShapeDtypeStruct((channels, 1), F32),
            jax.ShapeDtypeStruct((channels, 1), F32),
            jax.ShapeDtypeStruct(later.shape, later.dtype),
            *(jax.ShapeDtypeStruct((n, channels, width), BF16) for n, _, width in cuts),
        ),
        in_specs=[pl.BlockSpec(memory_space=pltpu.HBM)] * 3 + [ANY] * 2,
        out_specs=(VMEM, VMEM, VMEM, ANY) + (ANY,) * len(cuts),
        input_output_aliases={3: 3},
        scratch_shapes=[
            pltpu.VMEM((9, 3, channels, channels), BF16),
            pltpu.VMEM((8, channels), F32),
            pltpu.SemaphoreType.DMA((11,)),
            pltpu.SemaphoreType.DMA((len(cuts),)),
        ],
        compiler_params=pltpu.CompilerParams(vmem_limit_bytes=VMEM_BYTES),
        cost_estimate=pl.CostEstimate(flops=0, bytes_accessed=4 * weight.size, transcendentals=0),
    )(*(pltpu.with_memory_space_constraint(v, pltpu.HBM) for v in (weight, bias, gain)), later, first)


def layer_kernel(cases, rows_in, own, cols, block, height, n_in, back, place_ref, w_ref, bias_ref, gain_ref, *refs):
    ins = refs[:n_in]
    out_ref, acts_ref = refs[n_in:n_in + 2]
    xs, buf, total, sems = refs[n_in + 5:]
    channels = xs.shape[0]
    row = block * cols
    rows_out = rows_in - 2
    lanes_in, lanes_out = rows_in * row, rows_out * row
    segment, slab = place_ref[0], place_ref[1]

    def slot(a, c):
        return (3 * a + c) * channels

    def source(part):
        at, index = part[0], part[1]
        return ins[at] if index is None else ins[at].at[index]

    active = functools.reduce(jnp.logical_or, [segment == g for g, _, _ in cases])
    if back is not None:
        @pl.when(segment == back[0])
        def _():
            lanes = pl.ds(0, min(ins[back[1]].shape[1], lanes_out))
            copy = pltpu.make_async_copy(ins[back[1]].at[:, lanes], out_ref.at[:, lanes], sems.at[0])
            copy.start()
            copy.wait()

    for g, x_parts, before in cases:
        @pl.when(segment == g)
        def _():
            copies = []
            for parts, target in ((x_parts, xs), (before, buf.at[pl.ds(slot(0, 1), channels)])):
                at = 0
                for part in parts:
                    src = source(part)
                    width = part[3] * row
                    copies.append(pltpu.make_async_copy(
                        src.at[:, pl.ds(part[2] * row, width)], target.at[:, pl.ds(at, width)],
                        sems.at[len(copies)]))
                    at += width
            for c in copies:
                c.start()
            for c in copies:
                c.wait()

    @pl.when(active)
    def _():
        def squares(i, acc):
            v = xs[pl.ds(pl.multiple_of(i * CHUNK, CHUNK), CHUNK), :].astype(F32)
            v = v * v
            for k in range(0, CHUNK, 8):
                acc = acc + v[k:k + 8]
            return acc

        acc = lax.fori_loop(0, channels // CHUNK, squares, jnp.zeros((8, lanes_in), F32))
        scale = lax.rsqrt(jnp.sum(acc, axis=0, keepdims=True) * (1.0 / channels) + 1e-06)
        lane = lax.broadcasted_iota(jnp.int32, (CHUNK, row), 1)
        col = lax.rem(lane, cols)
        first, last = col == 0, col == cols - 1
        head = lane < row - cols
        zero = jnp.zeros((), BF16)

        def spread(i, _):
            at = pl.multiple_of(i * CHUNK, CHUNK)
            gain = gain_ref[pl.ds(at, CHUNK), :]
            here = [pl.ds(r * row, row) for r in range(rows_in)]
            values = [xs[pl.ds(at, CHUNK), h].astype(F32) for h in here]
            olds = [buf[pl.ds(slot(0, 1) + at, CHUNK), h] for h in here]
            results = []
            for r in range(rows_in):
                g = values[r] * scale[:, r * row:(r + 1) * row] * gain
                new = (0.5 * g * (1.0 + jnp.tanh(0.5 * g))).astype(BF16)
                mixed = pltpu.roll(jnp.where(head, new, olds[r]), cols, 1)
                for a, v in enumerate((olds[r], mixed, new)):
                    results.append((a, 0, r, jnp.where(first, zero, pltpu.roll(v, 1, 1))))
                    results.append((a, 2, r, jnp.where(last, zero, pltpu.roll(v, row - 1, 1))))
                    if a:
                        results.append((a, 1, r, v))
            for a, c, r, v in results:
                buf[pl.ds(slot(a, c) + at, CHUNK), here[r]] = v
            return 0

        lax.fori_loop(0, channels // CHUNK, spread, 0)
        acts_done = pltpu.make_async_copy(buf.at[pl.ds(slot(2, 1), channels)], acts_ref, sems.at[0])
        acts_done.start()
        step = 2 * row
        top = slab * own - (rows_out - own) // 2

        def taps(n, _):
            at = pl.multiple_of(n * step, step)
            part = xs[:, pl.ds(at + row, step)].astype(F32) + bias_ref[...]
            for b in range(3):
                part = part + jnp.dot(w_ref[b], buf[:, pl.ds(at + b * row, step)], preferred_element_type=F32)
            line = top + 2 * n + lax.broadcasted_iota(jnp.int32, (1, step), 1) // row
            total[:, pl.ds(at, step)] = jnp.where(
                jnp.logical_and(line >= 0, line < height), part, 0.0).astype(BF16)
            pltpu.make_async_copy(total.at[:, pl.ds(at, step)], out_ref.at[:, pl.ds(at, step)], sems.at[1]).start()
            return 0

        lax.fori_loop(0, lanes_out // step, taps, 0)
        out_done = pltpu.make_async_copy(total, out_ref, sems.at[1])
        acts_done.wait()
        out_done.wait()


def layer_call(cases, rows_in, own, cols, block, height, place, fixed, ins, back=None):
    weight, bias, gain = fixed
    channels = weight.shape[1]
    row = block * cols
    return pl.pallas_call(
        functools.partial(layer_kernel, cases, rows_in, own, cols, block, height, len(ins), back),
        out_shape=(
            jax.ShapeDtypeStruct((channels, (rows_in - 2) * row), BF16),
            jax.ShapeDtypeStruct((channels, rows_in * row), BF16),
            jax.ShapeDtypeStruct(weight.shape, weight.dtype),
            jax.ShapeDtypeStruct(bias.shape, bias.dtype),
            jax.ShapeDtypeStruct(gain.shape, gain.dtype),
        ),
        in_specs=[SMEM, VMEM, VMEM, VMEM] + [ANY] * len(ins),
        out_specs=(ANY, ANY, VMEM, VMEM, VMEM),
        input_output_aliases={1: 2, 2: 3, 3: 4},
        scratch_shapes=[
            pltpu.VMEM((channels, rows_in * row), BF16),
            pltpu.VMEM((9 * channels, rows_in * row), BF16),
            pltpu.VMEM((channels, (rows_in - 2) * row), BF16),
            pltpu.SemaphoreType.DMA((8,)),
        ],
        compiler_params=pltpu.CompilerParams(vmem_limit_bytes=VMEM_BYTES),
        cost_estimate=pl.CostEstimate(
            flops=2 * (rows_in - 2) * row * 27 * channels * channels, bytes_accessed=0, transcendentals=0),
    )(place, weight, bias, gain, *ins)


def local(segments, slabs, video_in, cache_in, conv_weight, conv_bias, norm_gain):
    frames, own, cols, channels = video_in.shape
    height = own * slabs
    segment = lax.axis_index("segment")
    slab = lax.axis_index("slab")
    axes = ("segment", "slab")
    block = frames // segments
    row = block * cols
    blocks = frames // block
    place = jnp.stack([segment, slab]).astype(jnp.int32)
    evens = range(0, segments, 2)
    odds = range(1, segments, 2)

    def moved(value, pairs, step):
        return lax.ppermute(value, axes, [
            (a * slabs + s, b * slabs + s + step) for a, b in pairs for s in range(slabs) if 0 <= s + step < slabs])

    def lanes(value):
        value = value.reshape(-1, block, own, cols, channels)
        return value.transpose(0, 4, 2, 1, 3).reshape(-1, channels, own * row)

    first = lanes(jnp.concatenate([cache_in[0], video_in[:block]], axis=0))
    first_below = moved(first[..., :2 * row], [(g, g) for g in evens], -1)
    first_above = moved(first[..., (own - 2) * row:], [(g, g) for g in evens], 1)
    place, weight = lax.optimization_barrier((place, conv_weight[0]))
    cuts = ((1, (own - 1) * row, row), (1, 0, row))
    weight, bias, gain, later, odd_last, odd_first = turned_weights(
        weight, conv_bias, norm_gain, lanes(video_in[block:]), first, cuts)
    odd_above = moved(odd_last, [(g, g) for g in odds], 1)
    odd_below = moved(odd_first, [(g, g) for g in odds], -1)
    later_below = moved(later[..., :2 * row], [(0, 0)], -1)
    later_above = moved(later[..., (own - 2) * row:], [(0, 0)], 1)
    fixed = (weight, bias, gain)

    call = functools.partial(layer_call, own=own, cols=cols, block=block, height=height, place=place)
    across = [(g, g ^ 1) for g in range(segments)]
    hop = [(g, g + 1) for g in odds if g + 1 < segments]
    planes = segments // 2
    arrived, done = [], []
    even_acts = odd_acts = None
    even_cache, odd_cache = [None] * planes, [None] * planes
    ticks = blocks + LAG * (planes - 1)
    for tick in range(ticks):
        busy = [p for p in range(planes) if 0 <= tick - LAG * p < blocks]
        ins = [first, first_above, first_below]
        old = [(1, 0, 0, 2), (0, 0, 0, own), (2, 0, 0, 2)]
        if tick:
            ins.append(even_acts)
            kept = [(3, None, 0, own + 4)]
        cases = []
        for p in busy:
            b = tick - LAG * p
            if p == 0 and b == 0:
                parts = [(1, 1, 0, 2), (0, 1, 0, own), (2, 1, 0, 2)]
            else:
                n = len(ins)
                if p == 0:
                    ins += [later, later_above, later_below]
                    parts = [(n + 1, b - 1, 0, 2), (n, b - 1, 0, own), (n + 2, b - 1, 0, 2)]
                else:
                    ins += list(arrived[b])
                    parts = [(n + 1, None, 0, 2), (n, None, 0, own), (n + 2, None, 0, 2)]
            cases.append((2 * p, parts, old if b == 0 else kept))
        if tick == 0:
            ins += [odd_above, odd_below]
        back = None
        if done:
            back = (segments - 1, len(ins))
            ins.append(done[-1])
        out, even_acts, *fixed = call(cases, own + 4, fixed=fixed, ins=ins, back=back)
        sent = list(arrived[tick - 1]) if 0 < tick <= blocks else []
        if sent:
            out, *sent = lax.optimization_barrier((out, *sent))
            arrived[tick - 1] = sent[:3]
        crossed = moved(out, across, 0)
        if tick == ticks - 1:
            done[-1] = crossed[:, :own * row]

        ins = [crossed, first, odd_above, odd_below]
        old = [(2, 0, 0, 1), (1, 0, 0, own), (3, 0, 0, 1)]
        if tick:
            ins.append(odd_acts)
        if tick == 0:
            ins += [later_above, later_below]
        cases = [(2 * p + 1, [(0, None, 0, own + 2)], old if tick == LAG * p else [(4, None, 0, own + 2)]) for p in busy]
        back = (segments - 2, 0) if done and tick < ticks - 1 else None
        out, odd_acts, *fixed = call(cases, own + 2, fixed=fixed, ins=ins, back=back)
        if back is not None:
            done[-1] = out
        if tick < blocks:
            arrived.append((moved(out, hop, 0), moved(out[:, (own - 2) * row:], hop, 1), moved(out[:, :2 * row], hop, -1)))
        b = tick - LAG * (planes - 1)
        if 0 <= b < blocks:
            done.append(out)
        for p in busy:
            if tick - LAG * p == blocks - 1:
                even_cache[p] = even_acts[:, 2 * row:(2 + own) * row]
                odd_cache[p] = odd_acts[:, row:(1 + own) * row]

    done[:-2] = [moved(d, [(segments - 2, b)], 0) for b, d in enumerate(done[:-2])]

    def natural(value):
        return value.reshape(channels, own, block, cols).transpose(2, 1, 3, 0)

    result, segment = lax.optimization_barrier((done[-1], segment))
    for b in range(blocks - 1):
        result = jnp.where(segment == b, done[b], result)
    cache = odd_cache[-1]
    for p in range(planes):
        cache = jnp.where(segment == 2 * p, even_cache[p], cache)
        cache = jnp.where(segment == 2 * p + 1, odd_cache[p], cache)
    return natural(result), natural(cache)[None]


def solution(mesh):
    segments, slabs = mesh.shape["segment"], mesh.shape["slab"]
    return jax.shard_map(
        functools.partial(local, segments, slabs),
        mesh=mesh,
        in_specs=(
            P(None, "slab", None, None),
            P("segment", None, "slab", None, None),
            P("segment", None, None, None, None, None),
            P("segment", None),
            P("segment", None),
        ),
        out_specs=(P("segment", "slab", None, None), P("segment", None, "slab", None, None)),
        check_vma=False,
    )
```

```python
import functools
import jax
import jax.numpy as jnp
from jax import lax
from jax.experimental import pallas as pl
from jax.experimental.pallas import tpu as pltpu
from jax.sharding import PartitionSpec as P

LAG = 2
CHUNK = 128
VMEM_BYTES = 24 * 2**20
F32 = jnp.float32
BF16 = jnp.bfloat16
ANY = pl.BlockSpec(memory_space=pl.ANY)
VMEM = pl.BlockSpec(memory_space=pltpu.VMEM)
SMEM = pl.BlockSpec(memory_space=pltpu.SMEM)


def turn_kernel(cuts, w_ref, bias_ref, gain_ref, later_ref, first_ref, out_ref, bias_out, gain_out, _, *refs):
    ws, rows, sems, cut_sems = refs[-4:]
    channels = w_ref.shape[-1]
    copies = [pltpu.make_async_copy(w_ref.at[k // 3, k % 3], ws.at[k], sems.at[k]) for k in range(9)]
    vectors = [pltpu.make_async_copy(ref, rows.at[pl.ds(k, 1)], sems.at[9 + k])
               for k, ref in enumerate((bias_ref, gain_ref))]
    parts = [pltpu.make_async_copy(first_ref.at[pl.ds(0, n), :, pl.ds(at, width)], refs[k], cut_sems.at[k])
             for k, (n, at, width) in enumerate(cuts)]
    for copy in vectors + copies + parts:
        copy.start()
    for k, copy in enumerate(copies):
        copy.wait()
        for c in range(3):
            out_ref[k % 3, :, pl.ds((k // 3 * 3 + c) * channels, channels)] = jnp.transpose(ws[k, c], (1, 0))
    for copy in vectors + parts:
        copy.wait()
    turned = jnp.transpose(rows[...], (1, 0))
    bias_out[...] = turned[:, 0:1]
    gain_out[...] = turned[:, 1:2]


def turned_weights(weight, bias, gain, later, first, cuts):
    channels = weight.shape[-1]
    return pl.pallas_call(
        functools.partial(turn_kernel, cuts),
        out_shape=(
            jax.ShapeDtypeStruct((3, channels, 9 * channels), BF16),
            jax.ShapeDtypeStruct((channels, 1), F32),
            jax.ShapeDtypeStruct((channels, 1), F32),
            jax.ShapeDtypeStruct(later.shape, later.dtype),
            *(jax.ShapeDtypeStruct((n, channels, width), BF16) for n, _, width in cuts),
        ),
        in_specs=[pl.BlockSpec(memory_space=pltpu.HBM)] * 3 + [ANY] * 2,
        out_specs=(VMEM, VMEM, VMEM, ANY) + (ANY,) * len(cuts),
        input_output_aliases={3: 3},
        scratch_shapes=[
            pltpu.VMEM((9, 3, channels, channels), BF16),
            pltpu.VMEM((8, channels), F32),
            pltpu.SemaphoreType.DMA((11,)),
            pltpu.SemaphoreType.DMA((len(cuts),)),
        ],
        compiler_params=pltpu.CompilerParams(vmem_limit_bytes=VMEM_BYTES),
        cost_estimate=pl.CostEstimate(flops=0, bytes_accessed=4 * weight.size, transcendentals=0),
    )(*(pltpu.with_memory_space_constraint(v, pltpu.HBM) for v in (weight, bias, gain)), later, first)


def layer_kernel(cases, rows_in, own, cols, block, height, n_in, back, place_ref, w_ref, bias_ref, gain_ref, *refs):
    ins = refs[:n_in]
    out_ref, acts_ref = refs[n_in:n_in + 2]
    xs, buf, total, sems = refs[n_in + 5:]
    channels = xs.shape[0]
    row = block * cols
    rows_out = rows_in - 2
    lanes_in, lanes_out = rows_in * row, rows_out * row
    segment, slab = place_ref[0], place_ref[1]

    def slot(a, c):
        return (3 * a + c) * channels

    def source(part):
        at, index = part[0], part[1]
        return ins[at] if index is None else ins[at].at[index]

    active = functools.reduce(jnp.logical_or, [segment == g for g, _, _ in cases])
    if back is not None:
        @pl.when(segment == back[0])
        def _():
            lanes = pl.ds(0, min(ins[back[1]].shape[1], lanes_out))
            copy = pltpu.make_async_copy(ins[back[1]].at[:, lanes], out_ref.at[:, lanes], sems.at[0])
            copy.start()
            copy.wait()

    for g, x_parts, before in cases:
        @pl.when(segment == g)
        def _():
            copies = []
            for parts, target in ((x_parts, xs), (before, buf.at[pl.ds(slot(0, 1), channels)])):
                at = 0
                for part in parts:
                    src = source(part)
                    width = part[3] * row
                    copies.append(pltpu.make_async_copy(
                        src.at[:, pl.ds(part[2] * row, width)], target.at[:, pl.ds(at, width)],
                        sems.at[len(copies)]))
                    at += width
            for c in copies:
                c.start()
            for c in copies:
                c.wait()

    @pl.when(active)
    def _():
        def squares(i, acc):
            v = xs[pl.ds(pl.multiple_of(i * CHUNK, CHUNK), CHUNK), :].astype(F32)
            v = v * v
            for k in range(0, CHUNK, 8):
                acc = acc + v[k:k + 8]
            return acc

        acc = lax.fori_loop(0, channels // CHUNK, squares, jnp.zeros((8, lanes_in), F32))
        scale = lax.rsqrt(jnp.sum(acc, axis=0, keepdims=True) * (1.0 / channels) + 1e-06)
        lane = lax.broadcasted_iota(jnp.int32, (CHUNK, row), 1)
        col = lax.rem(lane, cols)
        first, last = col == 0, col == cols - 1
        head = lane < row - cols
        zero = jnp.zeros((), BF16)

        def spread(i, _):
            at = pl.multiple_of(i * CHUNK, CHUNK)
            gain = gain_ref[pl.ds(at, CHUNK), :]
            here = [pl.ds(r * row, row) for r in range(rows_in)]
            values = [xs[pl.ds(at, CHUNK), h].astype(F32) for h in here]
            olds = [buf[pl.ds(slot(0, 1) + at, CHUNK), h] for h in here]
            results = []
            for r in range(rows_in):
                g = values[r] * scale[:, r * row:(r + 1) * row] * gain
                new = (0.5 * g * (1.0 + jnp.tanh(0.5 * g))).astype(BF16)
                mixed = pltpu.roll(jnp.where(head, new, olds[r]), cols, 1)
                for a, v in enumerate((olds[r], mixed, new)):
                    results.append((a, 0, r, jnp.where(first, zero, pltpu.roll(v, 1, 1))))
                    results.append((a, 2, r, jnp.where(last, zero, pltpu.roll(v, row - 1, 1))))
                    if a:
                        results.append((a, 1, r, v))
            for a, c, r, v in results:
                buf[pl.ds(slot(a, c) + at, CHUNK), here[r]] = v
            return 0

        lax.fori_loop(0, channels // CHUNK, spread, 0)
        acts_done = pltpu.make_async_copy(buf.at[pl.ds(slot(2, 1), channels)], acts_ref, sems.at[0])
        acts_done.start()
        step = 2 * row
        top = slab * own - (rows_out - own) // 2

        def taps(n, _):
            at = pl.multiple_of(n * step, step)
            part = xs[:, pl.ds(at + row, step)].astype(F32) + bias_ref[...]
            for b in range(3):
                part = part + jnp.dot(w_ref[b], buf[:, pl.ds(at + b * row, step)], preferred_element_type=F32)
            line = top + 2 * n + lax.broadcasted_iota(jnp.int32, (1, step), 1) // row
            total[:, pl.ds(at, step)] = jnp.where(
                jnp.logical_and(line >= 0, line < height), part, 0.0).astype(BF16)
            return 0

        lax.fori_loop(0, lanes_out // step, taps, 0)
        out_done = pltpu.make_async_copy(total, out_ref, sems.at[1])
        out_done.start()
        acts_done.wait()
        out_done.wait()


def layer_call(cases, rows_in, own, cols, block, height, place, fixed, ins, back=None):
    weight, bias, gain = fixed
    channels = weight.shape[1]
    row = block * cols
    return pl.pallas_call(
        functools.partial(layer_kernel, cases, rows_in, own, cols, block, height, len(ins), back),
        out_shape=(
            jax.ShapeDtypeStruct((channels, (rows_in - 2) * row), BF16),
            jax.ShapeDtypeStruct((channels, rows_in * row), BF16),
            jax.ShapeDtypeStruct(weight.shape, weight.dtype),
            jax.ShapeDtypeStruct(bias.shape, bias.dtype),
            jax.ShapeDtypeStruct(gain.shape, gain.dtype),
        ),
        in_specs=[SMEM, VMEM, VMEM, VMEM] + [ANY] * len(ins),
        out_specs=(ANY, ANY, VMEM, VMEM, VMEM),
        input_output_aliases={1: 2, 2: 3, 3: 4},
        scratch_shapes=[
            pltpu.VMEM((channels, rows_in * row), BF16),
            pltpu.VMEM((9 * channels, rows_in * row), BF16),
            pltpu.VMEM((channels, (rows_in - 2) * row), BF16),
            pltpu.SemaphoreType.DMA((8,)),
        ],
        compiler_params=pltpu.CompilerParams(vmem_limit_bytes=VMEM_BYTES),
        cost_estimate=pl.CostEstimate(
            flops=2 * (rows_in - 2) * row * 27 * channels * channels, bytes_accessed=0, transcendentals=0),
    )(place, weight, bias, gain, *ins)


def local(segments, slabs, video_in, cache_in, conv_weight, conv_bias, norm_gain):
    frames, own, cols, channels = video_in.shape
    height = own * slabs
    segment = lax.axis_index("segment")
    slab = lax.axis_index("slab")
    axes = ("segment", "slab")
    block = frames // segments
    row = block * cols
    blocks = frames // block
    place = jnp.stack([segment, slab]).astype(jnp.int32)
    evens = range(0, segments, 2)
    odds = range(1, segments, 2)

    def moved(value, pairs, step):
        return lax.ppermute(value, axes, [
            (a * slabs + s, b * slabs + s + step) for a, b in pairs for s in range(slabs) if 0 <= s + step < slabs])

    def lanes(value):
        value = value.reshape(-1, block, own, cols, channels)
        return value.transpose(0, 4, 2, 1, 3).reshape(-1, channels, own * row)

    first = lanes(jnp.concatenate([cache_in[0], video_in[:block]], axis=0))
    first_below = moved(first[..., :2 * row], [(g, g) for g in evens], -1)
    first_above = moved(first[..., (own - 2) * row:], [(g, g) for g in evens], 1)
    place, weight = lax.optimization_barrier((place, conv_weight[0]))
    cuts = ((1, (own - 1) * row, row), (1, 0, row))
    weight, bias, gain, later, odd_last, odd_first = turned_weights(
        weight, conv_bias, norm_gain, lanes(video_in[block:]), first, cuts)
    odd_above = moved(odd_last, [(g, g) for g in odds], 1)
    odd_below = moved(odd_first, [(g, g) for g in odds], -1)
    later_below = moved(later[..., :2 * row], [(0, 0)], -1)
    later_above = moved(later[..., (own - 2) * row:], [(0, 0)], 1)
    fixed = (weight, bias, gain)

    call = functools.partial(layer_call, own=own, cols=cols, block=block, height=height, place=place)
    across = [(g, g ^ 1) for g in range(segments)]
    hop = [(g, g + 1) for g in odds if g + 1 < segments]
    planes = segments // 2
    arrived, done = [], []
    even_acts = odd_acts = None
    even_cache, odd_cache = [None] * planes, [None] * planes
    ticks = blocks + LAG * (planes - 1)
    for tick in range(ticks):
        busy = [p for p in range(planes) if 0 <= tick - LAG * p < blocks]
        ins = [first, first_above, first_below]
        old = [(1, 0, 0, 2), (0, 0, 0, own), (2, 0, 0, 2)]
        if tick:
            ins.append(even_acts)
            kept = [(3, None, 0, own + 4)]
        cases = []
        for p in busy:
            b = tick - LAG * p
            if p == 0 and b == 0:
                parts = [(1, 1, 0, 2), (0, 1, 0, own), (2, 1, 0, 2)]
            else:
                n = len(ins)
                if p == 0:
                    ins += [later, later_above, later_below]
                    parts = [(n + 1, b - 1, 0, 2), (n, b - 1, 0, own), (n + 2, b - 1, 0, 2)]
                else:
                    ins += list(arrived[b])
                    parts = [(n + 1, None, 0, 2), (n, None, 0, own), (n + 2, None, 0, 2)]
            cases.append((2 * p, parts, old if b == 0 else kept))
        if tick == 0:
            ins += [odd_above, odd_below]
        back = None
        if done:
            back = (segments - 1, len(ins))
            ins.append(done[-1])
        out, even_acts, *fixed = call(cases, own + 4, fixed=fixed, ins=ins, back=back)
        sent = list(arrived[tick - 1]) if 0 < tick <= blocks else []
        if sent:
            out, *sent = lax.optimization_barrier((out, *sent))
            arrived[tick - 1] = sent[:3]
        crossed = moved(out, across, 0)
        if tick == ticks - 1:
            done[-1] = crossed[:, :own * row]

        ins = [crossed, first, odd_above, odd_below]
        old = [(2, 0, 0, 1), (1, 0, 0, own), (3, 0, 0, 1)]
        if tick:
            ins.append(odd_acts)
        if tick == 0:
            ins += [later_above, later_below]
        cases = [(2 * p + 1, [(0, None, 0, own + 2)], old if tick == LAG * p else [(4, None, 0, own + 2)]) for p in busy]
        back = (segments - 2, 0) if done and tick < ticks - 1 else None
        out, odd_acts, *fixed = call(cases, own + 2, fixed=fixed, ins=ins, back=back)
        if back is not None:
            done[-1] = out
        if tick < blocks:
            arrived.append((moved(out, hop, 0), moved(out[:, (own - 2) * row:], hop, 1), moved(out[:, :2 * row], hop, -1)))
        b = tick - LAG * (planes - 1)
        if 0 <= b < blocks:
            done.append(out)
        for p in busy:
            if tick - LAG * p == blocks - 1:
                even_cache[p] = even_acts[:, 2 * row:(2 + own) * row]
                odd_cache[p] = odd_acts[:, row:(1 + own) * row]

    done[:-2] = [moved(d, [(segments - 2, b)], 0) for b, d in enumerate(done[:-2])]

    def natural(value):
        return value.reshape(channels, own, block, cols).transpose(2, 1, 3, 0)

    result, segment = lax.optimization_barrier((done[-1], segment))
    for b in range(blocks - 1):
        result = jnp.where(segment == b, done[b], result)
    cache = odd_cache[-1]
    for p in range(planes):
        cache = jnp.where(segment == 2 * p, even_cache[p], cache)
        cache = jnp.where(segment == 2 * p + 1, odd_cache[p], cache)
    return natural(result), natural(cache)[None]


def solution(mesh):
    segments, slabs = mesh.shape["segment"], mesh.shape["slab"]
    return jax.shard_map(
        functools.partial(local, segments, slabs),
        mesh=mesh,
        in_specs=(
            P(None, "slab", None, None),
            P("segment", None, "slab", None, None),
            P("segment", None, None, None, None, None),
            P("segment", None),
            P("segment", None),
        ),
        out_specs=(P("segment", "slab", None, None), P("segment", None, "slab", None, None)),
        check_vma=False,
    )
```
